32 devices in a mesh: seq: 2 (over y), fsdp: 16 (over z, x, core).
Axes of the slice: x: 2, y: 2, z: 4, core: 2. Of those that a mesh axis runs over, the one named last changes fastest.
Arguments:
- tokens: bfloat16 [16, 1536, 896], P('fsdp', 'seq'), may hold values from -6 to 6
- seg_ids: int32 [16, 1536], P('fsdp', 'seq'), may hold values from 0 to 2, as said below
- first_gain: bfloat16 [896], P('fsdp'), may hold values from 0.5 to 1.5
- w_qkv: bfloat16 [896, 1152], P('fsdp'), may hold values from -0.1875 to 0.1875
- b_qkv: bfloat16 [1152], P('fsdp'), may hold values from -3 to 3
- w_out: bfloat16 [896, 896], P('fsdp'), may hold values from -1.5 to 1.5
- second_gain: bfloat16 [896], P('fsdp'), may hold values from 0.5 to 1.5
- w_gate: bfloat16 [896, 4864], P('fsdp'), may hold values from -0.1875 to 0.1875
- w_up: bfloat16 [896, 4864], P('fsdp'), may hold values from -0.1875 to 0.1875
- w_down: bfloat16 [4864, 896], P('fsdp'), may hold values from -0.078125 to 0.078125
- cotangent: bfloat16 [16, 1536, 896], P('fsdp', 'seq'), may hold values from -6 to 6
Outputs:
- output: bfloat16 [16, 1536, 896], P('fsdp', 'seq')
- grad_tokens: bfloat16 [16, 1536, 896], P('fsdp', 'seq')
- grad_first_gain: float32 [896], P('fsdp')
- grad_w_qkv: float32 [896, 1152], P('fsdp')
- grad_b_qk: float32 [1024], P('fsdp')
- grad_b_v: float32 [128], P('fsdp')
- grad_w_out: float32 [896, 896], P('fsdp')
- grad_second_gain: float32 [896], P('fsdp')
- grad_w_gate: float32 [896, 4864], P('fsdp')
- grad_w_up: float32 [896, 4864], P('fsdp')
- grad_w_down: float32 [4864, 896], P('fsdp')
The draws below stay inside these ranges and needn't reach their ends.
Inputs may be any that keep to these rules, and one draw needn't show every extreme that they name: `seg_ids`: along each row the ids never fall; id 0 is a leading document, id 1 a document of at least three quarters of the row's 1536 tokens that covers both halves of the row, id 2 a trailing document; every id appears in every row.
All inputs are finite; a program needn't handle non-finite values.
Results may differ from the reference program's by a relative error of at most 0.017.
Values may be sent and summed in bfloat16 or wider, within the bound.
No kernel may reach another device: no remote copies, remote signals or barrier semaphores. Data moves between devices by JAX's collectives and lax.ppermute only.
A program may use at most 256 MiB of HBM per device.

```python
import jax
import jax.numpy as jnp
from jax import lax

D = 896
HEADS = 14
KV_HEADS = 2
HEAD = 64
FF = 4864
KVD = 128
QKV = 1152
ROW = 1536
ROWS = 16


def draw_seg_ids(key, part):
    key = jax.random.fold_in(key, 11)
    first_key, second_key = jax.random.split(key, 2)
    first_cut = jax.random.randint(first_key, (ROWS, 1), 1, max(2, ROW // 8))
    second_cut = jax.random.randint(second_key, (ROWS, 1), ROW - ROW // 8, ROW)
    places = jnp.arange(ROW, dtype=jnp.int32)[None, :]
    return (places >= first_cut).astype(jnp.int32) + (places >= second_cut).astype(jnp.int32)


def with_spikes(drawn, rng, source, target, parts, factor):
    owner, partner = [(jnp.arange(drawn.shape[position]) // (drawn.shape[position] // parts)).reshape([-1 if axis == position else 1 for axis in range(drawn.ndim)]) for position in (source, target)]
    chosen = jax.random.permutation(rng, parts)[partner]
    strong = (owner == chosen) | (owner == (partner + parts // 2) % parts)
    return jnp.where(strong, factor * drawn, drawn)


def block_scale(rng, extent, cuts, least, top_value):
    def one(dim, blocks):
        steps = jax.random.uniform(jax.random.fold_in(jax.random.fold_in(rng, 6), dim), (blocks,), jnp.float32, least / len(cuts), top_value / len(cuts))
        return jnp.repeat(jnp.exp(steps), extent[dim] // blocks).reshape((-1,) + (1,) * (len(extent) - dim - 1))

    gain = one(*cuts[0])
    for cut in cuts[1:]:
        gain = gain * one(*cut)
    return gain


def scatter_about(own_key, extent, scale, most, shards=(), kind=jnp.bfloat16):
    values = scale * jax.random.normal(own_key, extent, jnp.float32)
    if shards:
        values = values * block_scale(own_key, extent, shards, -0.22, 0.18)
    return jnp.clip(values, -most, most).astype(kind)


def heavy_noise(rng, dims, width, limit, pieces, heavy, kind=jnp.bfloat16):
    drawn = width * jax.random.normal(rng, dims, jnp.float32)
    if pieces:
        drawn = drawn * block_scale(rng, dims, pieces, -0.22, 0.18)
    return jnp.clip(with_spikes(drawn, jax.random.fold_in(rng, 3), *heavy), -limit, limit).astype(kind)


def setup_inputs(seed: int = 0) -> dict:
    streams_of = jax.random.split(jax.random.key(seed), 12)
    return {
        "tokens": heavy_noise(streams_of[0], (ROWS, ROW, D), 1.0, 6.0, ((0, 16), (1, 2)), (0, 2, 16, 2.0)),
        "seg_ids": draw_seg_ids(jax.random.fold_in(streams_of[11], 71), 0),
        "first_gain": jnp.clip(1.0 + 0.1 * jax.random.normal(streams_of[2], (D,), jnp.float32), 0.5, 1.5).astype(jnp.bfloat16),
        "w_qkv": scatter_about(streams_of[3], (D, QKV), D ** -0.5, 0.1875, ((0, 16),)),
        "b_qkv": scatter_about(streams_of[4], (QKV,), 0.5, 3.0, ((0, 16),)),
        "w_out": scatter_about(streams_of[5], (D, D), (max(1, D // 64)) ** -0.5, 1.5, ((0, 16),)),
        "second_gain": jnp.clip(1.0 + 0.1 * jax.random.normal(streams_of[6], (D,), jnp.float32), 0.5, 1.5).astype(jnp.bfloat16),
        "w_gate": scatter_about(streams_of[7], (D, FF), D ** -0.5, 0.1875, ((0, 16),)),
        "w_up": scatter_about(streams_of[8], (D, FF), D ** -0.5, 0.1875, ((0, 16),)),
        "w_down": scatter_about(streams_of[9], (FF, D), FF ** -0.5, 0.078125, ((0, 16),)),
        "cotangent": scatter_about(streams_of[10], (ROWS, ROW, D), 1.0, 6.0, ((0, 16), (1, 2))),
    }


@jax.custom_vjp
def low(v):
    return lax.optimization_barrier(v.astype(jnp.bfloat16)).astype(jnp.float32)

@jax.custom_vjp
def low_back(v):
    return v

def low_keep(v):
    return (low(v), None)

def low_pass(kept, grad):
    return (grad,)

def back_keep(v):
    return (v, None)

def back_low(kept, grad):
    return (low(grad),)
low.defvjp(low_keep, low_pass)
low_back.defvjp(back_keep, back_low)
EPSILON = 1e-06
THETA = 1000000.0
NEGATIVE = -1e+30
HIGHEST = lax.Precision.HIGHEST

def positions_of(row_segs):
    length_all = row_segs.shape[0]
    places = jnp.arange(length_all, dtype=jnp.int32)
    previous = jnp.concatenate([jnp.full((1,), -1, jnp.int32), row_segs[:-1]])
    starts = lax.cummax(jnp.where(row_segs != previous, places, 0).astype(jnp.int32), axis=0)
    return places - starts

def rope_tables(positions, head_size):
    half_size = head_size // 2
    inverse = THETA ** (-(jnp.arange(half_size, dtype=jnp.float32) * 2.0 / head_size))
    angles = positions.astype(jnp.float32)[:, None] * inverse[None, :]
    return (jnp.cos(angles), jnp.sin(angles))

def rotate(values_in, cosines, sines):
    half_size = values_in.shape[-1] // 2
    first_half = values_in[..., :half_size]
    second_half = values_in[..., half_size:]
    cos_wide = cosines[:, None, :]
    sin_wide = sines[:, None, :]
    return jnp.concatenate([first_half * cos_wide - second_half * sin_wide, second_half * cos_wide + first_half * sin_wide], axis=-1)

def rms_scale(values_in):
    return lax.rsqrt(lax.optimization_barrier(jnp.mean(values_in * values_in, axis=-1, keepdims=True)) + EPSILON)

def row_forward(x_row, seg_row, params):
    gain_one, qkv_weight, qkv_bias, out_weight, gain_two, gate_weight, up_weight, down_weight = params
    length_all = x_row.shape[0]
    normed = low(x_row * rms_scale(x_row) * gain_one)
    project = jnp.dot(normed, qkv_weight, precision=HIGHEST) + qkv_bias
    query_pre = low_back(project[:, :D])
    key_pre = low_back(project[:, D:D + KVD])
    value_pre = low_back(project[:, D + KVD:])
    cosines, sines = rope_tables(positions_of(seg_row), HEAD)
    queries = low(rotate(query_pre.reshape(length_all, HEADS, HEAD), cosines, sines))
    keys_all = low(rotate(key_pre.reshape(length_all, KV_HEADS, HEAD), cosines, sines))
    values_all = low(value_pre.reshape(length_all, KV_HEADS, HEAD))
    grouped = queries.reshape(length_all, KV_HEADS, HEADS // KV_HEADS, HEAD)
    scores = low_back(jnp.einsum('qkgd,skd->kgqs', grouped, keys_all, precision=HIGHEST) * HEAD ** (-0.5))
    places = jnp.arange(length_all, dtype=jnp.int32)
    allowed = (seg_row[:, None] == seg_row[None, :]) & (places[None, :] <= places[:, None])
    probs = low(jax.nn.softmax(jnp.where(allowed, scores, NEGATIVE), axis=-1))
    attended = jnp.einsum('kgqs,skd->qkgd', probs, values_all, precision=HIGHEST).reshape(length_all, D)
    attended = low(low_back(attended))
    middle = x_row + low_back(jnp.dot(attended, out_weight, precision=HIGHEST))
    normed_two = low(middle * rms_scale(middle) * gain_two)
    gate_val = low_back(jnp.dot(normed_two, gate_weight, precision=HIGHEST))
    up_val = low_back(jnp.dot(normed_two, up_weight, precision=HIGHEST))
    hidden = low(jax.nn.silu(gate_val) * up_val)
    return middle + low_back(jnp.dot(hidden, down_weight, precision=HIGHEST))

def reference(tokens, seg_ids, first_gain, w_qkv, b_qkv, w_out, second_gain, w_gate, w_up, w_down, cotangent):
    params = (first_gain.astype(jnp.float32), w_qkv.astype(jnp.float32), b_qkv.astype(jnp.float32), w_out.astype(jnp.float32), second_gain.astype(jnp.float32), w_gate.astype(jnp.float32), w_up.astype(jnp.float32), w_down.astype(jnp.float32))
    tokens_f = tokens.astype(jnp.float32)
    cotangent_f = cotangent.astype(jnp.float32)

    def forward(x_all, weights_all):
        row_step = jax.checkpoint(lambda x_row, seg_row: row_forward(x_row, seg_row, weights_all))
        return lax.map(lambda row_pair: row_step(row_pair[0], row_pair[1]), (x_all, seg_ids))
    result, pullback = jax.vjp(forward, tokens_f, params)
    grad_in, grads = pullback(cotangent_f)
    bias_grad = grads[2]
    return (result.astype(jnp.bfloat16), grad_in.astype(jnp.bfloat16), grads[0], grads[1], bias_grad[:D + KVD], bias_grad[D + KVD:], grads[3], grads[4], grads[5], grads[6], grads[7])
```

```python
import functools

import jax
import jax.numpy as jnp
from jax import lax
from jax.experimental import pallas as pl
from jax.experimental.pallas import tpu as pltpu
from jax.sharding import PartitionSpec as P

HEAD = 64
LANES = 128
TILE = 256
EPSILON = 1e-06
THETA = 1000000.0
FAR = -1e30
MIB = 2**20

bf16 = jnp.bfloat16
f32 = jnp.float32


def dot_nn(left, right):
    return lax.dot_general(left, right, (((1,), (0,)), ((), ())), preferred_element_type=f32)


def dot_nt(left, right):
    return lax.dot_general(left, right, (((1,), (1,)), ((), ())), preferred_element_type=f32)


def dot_tn(left, right):
    return lax.dot_general(left, right, (((0,), (0,)), ((), ())), preferred_element_type=f32)


def swap_halves(values_in):
    lane = lax.broadcasted_iota(jnp.int32, values_in.shape, 1)
    ahead = pltpu.roll(values_in, LANES - HEAD // 2, 1)
    behind = pltpu.roll(values_in, HEAD // 2, 1)
    return jnp.where(lane % HEAD < HEAD // 2, ahead, behind)


def turn(values_in, cosines, sines):
    return values_in * cosines + swap_halves(values_in) * sines


def turn_back(grads_in, cosines, sines):
    return grads_in * cosines - swap_halves(grads_in) * sines


def project_kernel(x_ref, gain_ref, w_ref, bias_ref, cos_ref, sin_ref, normed_ref, q_ref, kv_ref):
    x = x_ref[...].astype(f32)
    scale = lax.rsqrt(jnp.mean(x * x, axis=1, keepdims=True) + EPSILON)
    normed = (x * scale * gain_ref[...]).astype(bf16)
    normed_ref[...] = normed
    project = dot_nn(normed, w_ref[...]) + bias_ref[...]
    cosines, sines = cos_ref[...], sin_ref[...]
    width = q_ref.shape[1]
    for start in range(0, width, LANES):
        part = slice(start, start + LANES)
        q_ref[:, part] = turn(project[:, part], cosines, sines).astype(bf16) * (HEAD**-0.5)
    kv_ref[:, :LANES] = turn(project[:, width : width + LANES], cosines, sines).astype(bf16)
    kv_ref[:, LANES:] = project[:, width + LANES :].astype(bf16)


def project_call(x, gain, weight, bias, cosines, sines):
    tokens, width = x.shape
    outs = weight.shape[1]
    rows = tokens // 3
    row = lambda cols: pl.BlockSpec((rows, cols), lambda i: (i, 0))
    whole = lambda *shape: pl.BlockSpec(shape, lambda i: (0, 0))
    return pl.pallas_call(
        project_kernel,
        grid=(3,),
        in_specs=[
            row(width),
            whole(1, width),
            whole(width, outs),
            whole(1, outs),
            row(LANES),
            row(LANES),
        ],
        out_specs=[row(width), row(width), row(2 * LANES)],
        out_shape=[
            jax.ShapeDtypeStruct((tokens, width), bf16),
            jax.ShapeDtypeStruct((tokens, width), bf16),
            jax.ShapeDtypeStruct((tokens, 2 * LANES), bf16),
        ],
        compiler_params=pltpu.CompilerParams(vmem_limit_bytes=32 * MIB),
        cost_estimate=pl.CostEstimate(
            flops=2 * tokens * width * outs, bytes_accessed=8 * MIB, transcendentals=0
        ),
        name="project",
    )(x, gain, weight, bias, cosines, sines)


def spread(ref, columns, out_ref, turned_ref=None):
    both = ref[:, columns].astype(f32)
    shifted = pltpu.roll(both, HEAD, 1)
    low = lax.broadcasted_iota(jnp.int32, both.shape, 1) < HEAD
    for head in range(2):
        for parity in range(2):
            source = both if head == parity else shifted
            alone = jnp.where(low if parity == 0 else ~low, source, 0.0)
            out_ref[head, parity] = alone.astype(bf16)
            if turned_ref is not None:
                turned_ref[head, parity] = alone.T.astype(bf16)


def attention_forward_kernel(
    half_ref, q_ref, qx_ref, kv_ref, kx_ref, rkv_ref, rkx_ref, o_ref, lse_ref, k_s, v_s, rk_s, rv_s, lse_s, *, group
):
    step = pl.program_id(0)
    tokens = q_ref.shape[0]
    block = tokens // 2
    lane = lax.broadcasted_iota(jnp.int32, (block, LANES), 1)
    keys, values = slice(0, LANES), slice(LANES, 2 * LANES)

    @pl.when(step == 0)
    def _():
        spread(kv_ref, keys, k_s)
        spread(kv_ref, values, v_s)
        lse_s[...] = jnp.zeros_like(lse_s)

        @pl.when(half_ref[0] != 0)
        def _():
            spread(rkv_ref, keys, rk_s)
            spread(rkv_ref, values, rv_s)

    def run(remote):
        for b in range(2):
            rows = slice(b * block, (b + 1) * block)
            q = jnp.concatenate([q_ref[rows], qx_ref[rows]], axis=1)
            total = None
            stats = lse_s[rows]
            for parity in range(2):
                kv = (2 * step + parity) // group
                k_at = lambda rows: jnp.concatenate([k_s[kv, parity, rows], kx_ref[rows]], axis=1)
                row_at = lax.broadcasted_iota(jnp.int32, (block, block), 0)
                col_at = lax.broadcasted_iota(jnp.int32, (block, block), 1)
                pieces = [(jnp.where(col_at <= row_at, dot_nt(q, k_at(rows)), FAR), v_s[kv, parity, rows])]
                if b:
                    first = slice(0, block)
                    pieces.append((dot_nt(q, k_at(first)), v_s[kv, parity, first]))
                if remote:
                    far_keys = jnp.concatenate([rk_s[kv, parity], rkx_ref[...]], axis=1)
                    pieces.append((dot_nt(q, far_keys), rv_s[kv, parity]))
                top = functools.reduce(
                    jnp.maximum, [jnp.max(s, axis=1, keepdims=True) for s, _ in pieces]
                )
                weights = [(jnp.exp(s - top), v) for s, v in pieces]
                norm = sum(jnp.sum(p, axis=1, keepdims=True) for p, _ in weights)
                out = sum(dot_nn(p.astype(bf16), v) for p, v in weights) * (1.0 / norm)
                total = out if total is None else total + out
                stats = jnp.where(lane == 2 * step + parity, top + jnp.log(norm), stats)
            o_ref[rows] = total.astype(bf16)
            lse_s[rows] = stats

    @pl.when(half_ref[0] == 0)
    def _():
        run(False)

    @pl.when(half_ref[0] != 0)
    def _():
        run(True)

    @pl.when(step == pl.num_programs(0) - 1)
    def _():
        lse_ref[...] = lse_s[...].T


def attention_forward(half, q, qx, kv, kx, rkv, rkx, group):
    tokens, width = q.shape
    pairs = width // LANES
    column = pl.BlockSpec((tokens, LANES), lambda p, *_: (0, p))
    whole = lambda *shape: pl.BlockSpec(shape, lambda p, *_: (0, 0))
    spare = lambda: pltpu.VMEM((2, 2, tokens, LANES), bf16)
    return pl.pallas_call(
        functools.partial(attention_forward_kernel, group=group),
        grid_spec=pltpu.PrefetchScalarGridSpec(
            num_scalar_prefetch=1,
            grid=(pairs,),
            in_specs=[
                column,
                whole(tokens, LANES),
                whole(tokens, 2 * LANES),
                whole(tokens, LANES),
                whole(tokens, 2 * LANES),
                whole(tokens, LANES),
            ],
            out_specs=[column, whole(LANES, tokens)],
            scratch_shapes=[spare(), spare(), spare(), spare(), pltpu.VMEM((tokens, LANES), f32)],
        ),
        out_shape=[
            jax.ShapeDtypeStruct((tokens, width), bf16),
            jax.ShapeDtypeStruct((LANES, tokens), f32),
        ],
        compiler_params=pltpu.CompilerParams(vmem_limit_bytes=48 * MIB),
        cost_estimate=pl.CostEstimate(
            flops=24 * 10**9, bytes_accessed=8 * MIB, transcendentals=16 * 10**6
        ),
        name="attention_forward",
    )(half, q, qx, kv, kx, rkv, rkx)


def attention_backward_kernel(
    half_ref, q_ref, qx_ref, g_ref, o_ref, lse_ref, cos_ref, sin_ref, kv_ref, kx_ref, rkv_ref, rkx_ref,
    dq_ref, dkv_ref, rdkv_ref, k_s, t_s, v_s, rk_s, rt_s, rv_s, ka, va, rka, rva, *, group
):
    step = pl.program_id(0)
    tokens = q_ref.shape[0]
    block = tokens // 2
    keys, values = slice(0, LANES), slice(LANES, 2 * LANES)

    @pl.when(step == 0)
    def _():
        spread(kv_ref, keys, k_s, t_s)
        spread(kv_ref, values, v_s)
        for ref in (ka, va, rka, rva):
            ref[...] = jnp.zeros_like(ref)

        @pl.when(half_ref[0] != 0)
        def _():
            spread(rkv_ref, keys, rk_s, rt_s)
            spread(rkv_ref, values, rv_s)

    def run(remote):
        near = (k_s, kx_ref, t_s, v_s, ka, va)
        far = (rk_s, rkx_ref, rt_s, rv_s, rka, rva)
        for b in range(2):
            rows = slice(b * block, (b + 1) * block)
            q = q_ref[rows]
            q_wide = jnp.concatenate([q, qx_ref[rows]], axis=1)
            g = g_ref[rows]
            product = (g.astype(f32) * o_ref[rows].astype(f32)).T
            total = None
            for parity in range(2):
                head = 2 * step + parity
                kv = head // group
                lse = lse_ref[pl.ds(head, 1), rows]
                delta = jnp.sum(product[parity * HEAD : (parity + 1) * HEAD], axis=0, keepdims=True)
                work = [(near, c, c == b) for c in range(b + 1)]
                if remote:
                    work += [(far, c, False) for c in range(2)]
                for (k_r, x_r, t_r, v_r, k_acc, v_acc), c, masked in work:
                    part = slice(c * block, (c + 1) * block)
                    s = dot_nt(jnp.concatenate([k_r[kv, parity, part], x_r[part]], axis=1), q_wide)
                    if masked:
                        row_at = lax.broadcasted_iota(jnp.int32, (block, block), 0)
                        col_at = lax.broadcasted_iota(jnp.int32, (block, block), 1)
                        s = jnp.where(row_at <= col_at, s, FAR)
                    p = jnp.exp(s - lse)
                    dp = dot_nt(v_r[kv, parity, part], g)
                    ds = (p * (dp - delta)).astype(bf16)
                    v_acc[kv, parity, part] += dot_nn(p.astype(bf16), g)
                    k_acc[kv, parity, part] += dot_nn(ds, q)
                    dq = dot_nn(t_r[kv, parity, :, part], ds)
                    total = dq if total is None else total + dq
            dq_ref[rows] = turn_back(total.T * (HEAD**-0.5), cos_ref[rows], sin_ref[rows]).astype(bf16)

    @pl.when(half_ref[0] == 0)
    def _():
        run(False)

    @pl.when(half_ref[0] != 0)
    def _():
        run(True)

    @pl.when(step == pl.num_programs(0) - 1)
    def _():
        low = lax.broadcasted_iota(jnp.int32, (tokens, LANES), 1) < HEAD
        for acc, out, columns in (
            (ka, dkv_ref, keys),
            (va, dkv_ref, values),
            (rka, rdkv_ref, keys),
            (rva, rdkv_ref, values),
        ):
            first = acc[0, 0] + pltpu.roll(acc[0, 1], HEAD, 1)
            second = acc[1, 1] + pltpu.roll(acc[1, 0], HEAD, 1)
            out[:, columns] = jnp.where(low, first, second).astype(out.dtype)


def attention_backward(half, q, qx, g, o, lse, cosines, sines, kv, kx, rkv, rkx, group):
    tokens, width = q.shape
    pairs = width // LANES
    column = pl.BlockSpec((tokens, LANES), lambda p, *_: (0, p))
    whole = lambda *shape: pl.BlockSpec(shape, lambda p, *_: (0, 0))
    spare = lambda: pltpu.VMEM((2, 2, tokens, LANES), bf16)
    turned = lambda: pltpu.VMEM((2, 2, LANES, tokens), bf16)
    sums = lambda: pltpu.VMEM((2, 2, tokens, LANES), f32)
    return pl.pallas_call(
        functools.partial(attention_backward_kernel, group=group),
        grid_spec=pltpu.PrefetchScalarGridSpec(
            num_scalar_prefetch=1,
            grid=(pairs,),
            in_specs=[
                column,
                whole(tokens, LANES),
                column,
                column,
                whole(LANES, tokens),
                whole(tokens, LANES),
                whole(tokens, LANES),
                whole(tokens, 2 * LANES),
                whole(tokens, LANES),
                whole(tokens, 2 * LANES),
                whole(tokens, LANES),
            ],
            out_specs=[column, whole(tokens, 2 * LANES), whole(tokens, 2 * LANES)],
            scratch_shapes=[spare(), turned(), spare(), spare(), turned(), spare()]
            + [sums(), sums(), sums(), sums()],
        ),
        out_shape=[
            jax.ShapeDtypeStruct((tokens, width), bf16),
            jax.ShapeDtypeStruct((tokens, 2 * LANES), f32),
            jax.ShapeDtypeStruct((tokens, 2 * LANES), bf16),
        ],
        compiler_params=pltpu.CompilerParams(vmem_limit_bytes=56 * MIB),
        cost_estimate=pl.CostEstimate(
            flops=46 * 10**9, bytes_accessed=12 * MIB, transcendentals=16 * 10**6
        ),
        name="attention_backward",
    )(half, q, qx, g, o, lse, cosines, sines, kv, kx, rkv, rkx)


def mlp_kernel(
    core_ref, near_ref, far_ref, gnear_ref, gfar_ref, w_ref, *rest, first, tiles, carry
):
    if carry:
        old_out_ref, old_grad_ref, out_ref, grad_ref, packed_ref, n_s, t_s, g_s, out_s, grad_s = rest
    else:
        out_ref, grad_ref, packed_ref, n_s, t_s, g_s, out_s, grad_s = rest
    step = pl.program_id(0)
    tile = 2 * (first + step) + core_ref[0]
    tokens, width = near_ref.shape
    shards = w_ref.shape[0]
    depth = width // shards
    own = TILE // shards

    @pl.when(step == 0)
    def _():
        n_s[:tokens] = near_ref[...]
        n_s[tokens:] = far_ref[...]
        g_s[:tokens] = gnear_ref[...]
        g_s[tokens:] = gfar_ref[...]
        t_s[:, :tokens] = near_ref[...].T
        t_s[:, tokens:] = far_ref[...].T
        if carry:
            out_s[...] = old_out_ref[...]
            grad_s[...] = old_grad_ref[...]
        else:
            out_s[...] = jnp.zeros_like(out_s)
            grad_s[...] = jnp.zeros_like(grad_s)

    @pl.when(tile >= tiles)
    def _():
        packed_ref[...] = jnp.zeros_like(packed_ref)

    @pl.when(tile < tiles)
    def _():
        def square(start):
            parts = []
            for c in range(TILE // LANES):
                rows = w_ref[:, start + c * depth : start + (c + 1) * depth, :]
                parts.append(rows.astype(f32).reshape(width, LANES).astype(bf16))
            return jnp.concatenate(parts, axis=1)

        gate_w = square(0)
        up_w = square(2 * depth)
        down_parts = []
        for c in range(width // LANES):
            rows = w_ref[:, 4 * depth + c * own : 4 * depth + (c + 1) * own, :]
            down_parts.append(rows.reshape(TILE, LANES))
        down_w = jnp.concatenate(down_parts, axis=1)
        n = n_s[...]
        g = g_s[...]
        gate = dot_nn(n, gate_w)
        up = dot_nn(n, up_w)
        grad_hidden = dot_nt(g, down_w)
        sig = 1.0 / (1.0 + jnp.exp(-gate))
        silu = gate * sig
        hidden = (silu * up).astype(bf16)
        grad_gate = (grad_hidden * up * (sig + silu * (1.0 - sig))).astype(bf16)
        grad_up = (grad_hidden * silu).astype(bf16)
        out_s[...] += dot_nn(hidden, down_w)
        grad_s[...] += dot_nt(grad_gate, gate_w) + dot_nt(grad_up, up_w)
        chips = shards // 2
        for at, value in ((0, dot_nn(t_s[...], grad_gate)), (1, dot_nn(t_s[...], grad_up))):
            for c in range(TILE // LANES):
                part = value[:, c * LANES : (c + 1) * LANES].astype(bf16)
                start = (2 * at + c) * 2 * depth
                packed_ref[:, start : start + 2 * depth, :] = part.reshape(chips, 2 * depth, LANES)
        down = dot_tn(hidden, g)
        for c in range(width // LANES):
            part = down[:, c * LANES : (c + 1) * LANES].astype(bf16)
            start = 8 * depth + c * 2 * own
            packed_ref[:, start : start + 2 * own, :] = part.reshape(chips, 2 * own, LANES)

    @pl.when(step == pl.num_programs(0) - 1)
    def _():
        out_ref[...] = out_s[...]
        grad_ref[...] = grad_s[...]


def mlp_call(core, near, far, gnear, gfar, packed, first, count, tiles, carried):
    tokens, width = near.shape
    shards = packed.shape[0]
    rows = 6 * width // shards
    whole = lambda *shape: pl.BlockSpec(shape, lambda j, *_: (0,) * len(shape))
    wide = jax.ShapeDtypeStruct((2 * tokens, width), f32)
    carry = carried is not None
    return pl.pallas_call(
        functools.partial(mlp_kernel, first=first, tiles=tiles, carry=carry),
        grid_spec=pltpu.PrefetchScalarGridSpec(
            num_scalar_prefetch=1,
            grid=(count,),
            in_specs=[whole(tokens, width)] * 4
            + [
                pl.BlockSpec(
                    (shards, rows, LANES),
                    lambda j, core: (0, jnp.minimum(2 * (first + j) + core[0], tiles - 1), 0),
                )
            ]
            + ([whole(2 * tokens, width)] * 2 if carry else []),
            out_specs=[whole(2 * tokens, width)] * 2
            + [pl.BlockSpec((shards // 2, 2 * rows, LANES), lambda j, *_: (0, j, 0))],
            scratch_shapes=[
                pltpu.VMEM((2 * tokens, width), bf16),
                pltpu.VMEM((width, 2 * tokens), bf16),
                pltpu.VMEM((2 * tokens, width), bf16),
                pltpu.VMEM((2 * tokens, width), f32),
                pltpu.VMEM((2 * tokens, width), f32),
            ],
        ),
        out_shape=[
            wide,
            wide,
            jax.ShapeDtypeStruct((shards // 2, 2 * rows * count, LANES), bf16),
        ],
        compiler_params=pltpu.CompilerParams(vmem_limit_bytes=60 * MIB),
        cost_estimate=pl.CostEstimate(
            flops=18 * 2 * tokens * width * TILE * count,
            bytes_accessed=40 * MIB,
            transcendentals=2 * tokens * TILE * count,
        ),
        name="feed_forward",
    )(core, near, far, gnear, gfar, packed, *(carried or ()))


def pack_weights(w_gate, w_up, w_down, shards):
    depth, hidden = w_gate.shape
    tiles = hidden // TILE
    own = TILE // shards

    def columns(weight):
        parts = weight.reshape(depth, shards, tiles, own).transpose(0, 2, 1, 3)
        parts = parts.reshape(depth, tiles, TILE // LANES, LANES).transpose(1, 2, 0, 3)
        return parts.reshape(tiles, -1, LANES)

    width = w_down.shape[1]
    down = w_down.reshape(tiles, own, width // LANES, LANES).transpose(0, 2, 1, 3)
    return jnp.concatenate([columns(w_gate), columns(w_up), down.reshape(tiles, -1, LANES)], axis=1)


def unpack_grads(packed, shards, depth):
    tiles = packed.shape[0]
    own = TILE // shards

    def columns(part):
        part = part.reshape(tiles, TILE // LANES, depth, LANES).transpose(2, 0, 1, 3)
        part = part.reshape(depth, tiles, shards, own).transpose(0, 2, 1, 3)
        return part.reshape(depth, tiles * TILE)

    gate, up = columns(packed[:, : 2 * depth]), columns(packed[:, 2 * depth : 4 * depth])
    down = packed[:, 4 * depth :].reshape(tiles, -1, own, LANES).transpose(0, 2, 1, 3)
    return gate, up, down.reshape(tiles * own, -1)


def regroup_weights(gathered, groups, tiles, depth, own):
    shards = gathered.shape[0]
    if shards == groups:
        return gathered
    many = shards // groups
    gathered = gathered.reshape(groups, many, tiles, -1, LANES)
    outs = []
    for start, size in ((0, depth), (2 * depth, depth), (4 * depth, own)):
        stop = start + 2 * depth
        part = gathered[:, :, :, start:stop].reshape(groups, many, tiles, -1, size, LANES)
        outs.append(part.transpose(0, 2, 3, 1, 4, 5).reshape(groups, tiles, -1, LANES))
    return jnp.concatenate(outs, axis=2).reshape(groups, -1, LANES)


class Wires:
    def __init__(self, shards):
        self.shards = shards
        place = lax.axis_index("fsdp")
        self.core = place % 2
        self.inner = (place // 2) % 2
        self.line = place // 4
        self.seq = lax.axis_index("seq")

    def flip(self, values_in, bit):
        return lax.ppermute(values_in, "fsdp", [(i, i ^ bit) for i in range(self.shards)])

    def other_half(self, values_in):
        return lax.ppermute(values_in, "seq", [(0, 1), (1, 0)])


def ordered(bit, own, other):
    return jnp.where(bit == 0, own, other), jnp.where(bit == 0, other, own)


def gather_small(wires, shard):
    if wires.shards != 16:
        return lax.all_gather(shard, "fsdp", axis=0, tiled=False)
    have = shard[None]
    have = jnp.concatenate(ordered(wires.line % 2, have, wires.flip(have, 4)), axis=0)
    have = jnp.concatenate(ordered(wires.line // 2, have, wires.flip(have, 8)), axis=0)
    have = jnp.stack(ordered(wires.inner, have, wires.flip(have, 2)), axis=1)
    have = jnp.stack(ordered(wires.core, have, wires.flip(have, 1)), axis=2)
    return have.reshape((16,) + shard.shape)


def pick(values_in, place, axis):
    return lax.dynamic_index_in_dim(values_in, place, axis, keepdims=False)


def plus(left, right):
    return (left.astype(f32) + right.astype(f32)).astype(bf16)


def reduce_chips(wires, values_in):
    rows = values_in.shape[2]
    half, quarter = rows // 2, rows // 4
    first, second = values_in[:, :, :half], values_in[:, :, half:]
    inner, seq = wires.inner, wires.seq
    second = second.reshape(4, 2, 2, quarter, LANES)
    got_first = wires.flip(pick(first, 1 - inner, 1), 2)
    got_second = wires.other_half(pick(second, 1 - seq, 2))
    first = plus(pick(first, inner, 1), got_first).reshape(4, 2, quarter, LANES)
    second = plus(pick(second, seq, 2), got_second)
    got_first = wires.other_half(pick(first, 1 - seq, 1))
    got_second = wires.flip(pick(second, 1 - inner, 1), 2)
    first = plus(pick(first, seq, 1), got_first)
    second = plus(pick(second, inner, 1), got_second)
    both = jnp.concatenate([first, second], axis=1).reshape(2, 2, half, LANES)
    high, low = wires.line // 2, wires.line % 2
    both = plus(pick(both, high, 0), wires.flip(pick(both, 1 - high, 0), 8))
    both = plus(pick(both, low, 0), wires.flip(pick(both, 1 - low, 0), 4))
    other = wires.other_half(both)
    one, two = ordered(seq, both, other)
    return jnp.concatenate([one[:quarter], two[:quarter], one[quarter:], two[quarter:]], axis=0)


def positions_of(row_segs):
    length_all = row_segs.shape[0]
    places = jnp.arange(length_all, dtype=jnp.int32)
    previous = jnp.concatenate([jnp.full((1,), -1, jnp.int32), row_segs[:-1]])
    starts = lax.cummax(jnp.where(row_segs != previous, places, 0), axis=0)
    return places - starts


def norm_back(grad_normed, normal_part, inv_scale, gain_float):
    scaled = grad_normed * gain_float
    return inv_scale * (
        scaled - normal_part * jnp.mean(scaled * normal_part, axis=-1, keepdims=True)
    )


def rms_scale(values_in):
    return lax.rsqrt(jnp.mean(values_in * values_in, axis=-1, keepdims=True) + EPSILON)


def per_device(
    shards, tokens, seg_ids, first_gain, w_qkv, b_qkv, w_out, second_gain, w_gate, w_up, w_down, cotangent
):
    wires = Wires(shards)
    tokens = tokens[0]
    count, width = tokens.shape
    depth, qkv_width = w_qkv.shape
    kv_width = (qkv_width - width) // 2
    group = (width // HEAD) // (kv_width // HEAD)
    hidden_all = w_gate.shape[1]
    tiles = hidden_all // TILE
    own = TILE // shards
    own_bias = b_qkv.shape[0]
    half = wires.seq.astype(jnp.int32).reshape(1)
    core = wires.core.astype(jnp.int32).reshape(1)
    grad_mlp = cotangent[0]

    pad_rows = -(-(depth + 1) // 8) * 8 - depth
    vector = jnp.concatenate([first_gain, b_qkv, second_gain])
    vector = jnp.pad(vector, (0, qkv_width - vector.shape[0]))
    small = jnp.concatenate([w_qkv, jnp.pad(vector[None], ((0, pad_rows - 1), (0, 0)))], axis=0)
    out_packed = w_out.reshape(depth, width // LANES, LANES).transpose(1, 0, 2).reshape(-1, LANES)
    packed = pack_weights(w_gate, w_up, w_down, shards).reshape(-1, LANES)
    packed_rows = packed.shape[0]
    packed = jnp.concatenate([packed, out_packed], axis=0)
    small_all = gather_small(wires, small)
    packed_all = lax.all_gather(packed, "fsdp", axis=0, tiled=False)
    qkv_full = small_all[:, :depth].reshape(width, qkv_width)
    vectors = small_all[:, depth]
    gain_one = vectors[:, :depth].reshape(1, width).astype(f32)
    bias = vectors[:, depth : depth + own_bias].reshape(1, qkv_width).astype(f32)
    gain_two = vectors[:, depth + own_bias : 2 * depth + own_bias].reshape(1, width).astype(f32)

    other_segs = wires.other_half(seg_ids)
    row_segs = jnp.concatenate(ordered(wires.seq, seg_ids, other_segs), axis=1)[0]
    local_pos = lax.dynamic_slice_in_dim(positions_of(row_segs), wires.seq * count, count)
    inverse = THETA ** (-(jnp.arange(HEAD // 2, dtype=f32) * 2.0 / HEAD))
    angles = local_pos.astype(f32)[:, None] * inverse[None, :]
    cosines, sines = jnp.cos(angles), jnp.sin(angles)
    cosines = jnp.concatenate([cosines] * 4, axis=1)
    sines = jnp.concatenate([-sines, sines] * 2, axis=1)
    doc = jnp.arange(LANES, dtype=jnp.int32)[None, :]
    kx = (seg_ids[0][:, None] == doc).astype(bf16)
    rkx = (other_segs[0][:, None] == doc).astype(bf16)
    qx = jnp.where((seg_ids[0][:, None] == doc) | (doc >= 3), 0.0, FAR).astype(bf16)

    normed, queries, kv = project_call(tokens, gain_one, qkv_full, bias, cosines, sines)
    far_kv = lax.ppermute(kv, "seq", [(0, 1)])
    attended, lse = attention_forward(half, queries, qx, kv, kx, far_kv, rkx, group)
    out_full = packed_all[:, packed_rows:].reshape(shards, width // LANES, depth, LANES)
    out_full = out_full.transpose(0, 2, 1, 3).reshape(width, width)
    residual_in = tokens.astype(f32)
    middle = residual_in + dot_nn(attended, out_full)
    inv_two = rms_scale(middle)
    normal_two = middle * inv_two
    normed_two = (normal_two * gain_two).astype(bf16)

    groups = 16
    packed_mlp = regroup_weights(packed_all[:, :packed_rows], groups, tiles, depth, own) if shards != groups else packed_all
    far_normed = wires.flip(normed_two, 1)
    far_grad = wires.flip(grad_mlp, 1)
    steps = -(-tiles // 2)
    early = steps // 2
    shared = (core, normed_two, far_normed, grad_mlp, far_grad, packed_mlp)
    out_acc, grad_acc, packed_one = mlp_call(*shared, 0, early, tiles, None)
    out_acc, grad_acc, packed_two = mlp_call(*shared, early, steps - early, tiles, (out_acc, grad_acc))
    back = wires.flip(jnp.concatenate([out_acc[count:], grad_acc[count:]], axis=0).astype(bf16), 1)
    result = (middle + out_acc[:count] + back[:count].astype(f32)).astype(bf16)
    grad_normed_two = grad_acc[:count] + back[count:].astype(f32)
    gain_two_grad = jnp.sum(grad_normed_two * normal_two, axis=0)
    grad_out = grad_mlp.astype(f32)
    grad_middle = grad_out + norm_back(grad_normed_two, normal_two, inv_two, gain_two)

    full_depth = width // groups
    own_group = TILE // groups

    def owners(grads):
        pieces = grads.shape[1] // (12 * full_depth)
        if shards == groups:
            total = reduce_chips(wires, grads.reshape(4, 2, -1, LANES))
            total = total.reshape(pieces, 12 * full_depth, LANES)
            parts = []
            for start, size in ((0, full_depth), (4 * full_depth, full_depth), (8 * full_depth, own_group)):
                part = total[:, start : start + 4 * full_depth].reshape(pieces, -1, 2, size, LANES)
                parts.append(part.transpose(0, 2, 1, 3, 4).reshape(pieces, 2, -1, LANES))
            total = jnp.concatenate(parts, axis=2)
            mine, theirs = pick(total, wires.core, 1), pick(total, 1 - wires.core, 1)
            theirs = wires.flip(theirs, 1)
        else:
            many = shards // groups
            grads = grads.reshape(groups // 2, pieces, 12 * full_depth, LANES)
            parts = []
            for start, size in ((0, depth), (4 * full_depth, depth), (8 * full_depth, own)):
                part = grads[:, :, start : start + 4 * full_depth]
                part = part.reshape(groups // 2, pieces, -1, 2 * many, size, LANES)
                parts.append(part.transpose(0, 3, 1, 2, 4, 5).reshape(shards, pieces, -1, LANES))
            grads = jnp.concatenate(parts, axis=2)
            spread_out = jnp.zeros((2,) + grads.shape, f32)
            spread_out = lax.dynamic_update_index_in_dim(spread_out, grads.astype(f32), wires.core, 0)
            total = lax.psum_scatter(spread_out, "fsdp", scatter_dimension=1, tiled=True)[:, 0]
            total = lax.psum(total.astype(bf16), "seq")
            return total.transpose(1, 0, 2, 3).reshape(2 * pieces, -1, LANES)
        first, second = ordered(wires.core, mine, theirs)
        return jnp.stack([first, second], axis=1).reshape(2 * pieces, -1, LANES)

    mlp_grads = jnp.concatenate([owners(packed_one), owners(packed_two)], axis=0)[:tiles]
    gate_grad, up_grad, down_grad = unpack_grads(mlp_grads, shards, depth)

    grad_branch = grad_middle.astype(bf16)
    out_grad = dot_tn(attended, grad_branch)
    grad_attended = dot_nt(grad_branch, out_full).astype(bf16)
    query_grad, kv_grad, far_kv_grad = attention_backward(
        half, queries, qx, grad_attended, attended, lse, cosines, sines, kv, kx, far_kv, rkx, group
    )
    got_kv = lax.ppermute(far_kv_grad, "seq", [(1, 0)])
    kv_grad = kv_grad + got_kv.astype(f32)
    key_grad = kv_grad[:, :kv_width].reshape(count, -1, 2, HEAD // 2)
    cos_half = cosines[:, None, : HEAD // 2]
    sin_half = sines[:, None, HEAD // 2 : HEAD]
    first_half, second_half = key_grad[:, :, 0], key_grad[:, :, 1]
    key_grad = jnp.stack(
        [first_half * cos_half + second_half * sin_half, second_half * cos_half - first_half * sin_half],
        axis=2,
    ).reshape(count, kv_width)
    kv_grad = jnp.concatenate([key_grad, kv_grad[:, kv_width:]], axis=1).astype(bf16)
    grad_project = jnp.concatenate([query_grad, kv_grad], axis=1)
    bias_grad = jnp.sum(grad_project.astype(f32), axis=0)
    qkv_grad = dot_tn(normed, grad_project)
    grad_normed = dot_nt(grad_project, qkv_full)
    inv_one = rms_scale(residual_in)
    normal_one = residual_in * inv_one
    gain_one_grad = jnp.sum(grad_normed * normal_one, axis=0)
    grad_input = grad_middle + norm_back(grad_normed, normal_one, inv_one, gain_one)

    qk_own = (width + kv_width) // shards
    vector = jnp.concatenate(
        [
            gain_one_grad.reshape(shards, depth),
            gain_two_grad.reshape(shards, depth),
            bias_grad[: width + kv_width].reshape(shards, qk_own),
            bias_grad[width + kv_width :].reshape(shards, -1),
        ],
        axis=1,
    )
    vector = jnp.pad(vector, ((0, 0), (0, qkv_width - vector.shape[1])))[:, None]
    vector = jnp.pad(vector, ((0, 0), (0, pad_rows - 1), (0, 0)))
    small_grad = jnp.concatenate([qkv_grad.reshape(shards, depth, qkv_width), vector], axis=1)
    out_grad = out_grad.reshape(shards, depth, width)

    def lanes(grads):
        rows, cols = grads.shape[1:]
        return grads.reshape(shards, rows, cols // LANES, LANES).transpose(0, 2, 1, 3).reshape(shards, -1, LANES)

    def unlanes(grads, cols):
        return grads.reshape(cols // LANES, -1, LANES).transpose(1, 0, 2).reshape(-1, cols)

    def small_owner(grads):
        if shards != 16:
            total = lax.psum_scatter(grads, "fsdp", scatter_dimension=0, tiled=True)[0]
            return lax.psum(total.astype(bf16), "seq")
        cols = grads.shape[2]
        grads = lanes(grads.astype(bf16)).reshape(8, 2, -1, LANES)
        grads = plus(pick(grads, wires.core, 1), wires.flip(pick(grads, 1 - wires.core, 1), 1))
        return unlanes(reduce_chips(wires, grads.reshape(4, 2, -1, LANES)), cols)

    small_total = small_owner(small_grad).astype(f32)
    out_total = small_owner(out_grad).astype(f32)
    vector = small_total[depth]
    ends = [0, depth, 2 * depth, 2 * depth + qk_own, 2 * depth + own_bias]
    gain_one_grad, gain_two_grad, bias_qk, bias_v = (vector[a:b] for a, b in zip(ends, ends[1:]))
    return (
        result[None],
        grad_input.astype(bf16)[None],
        gain_one_grad,
        small_total[:depth],
        bias_qk,
        bias_v,
        out_total,
        gain_two_grad,
        gate_grad.astype(f32),
        up_grad.astype(f32),
        down_grad.astype(f32),
    )


def solution(mesh):
    rows, split, lone = P("fsdp", "seq", None), P("fsdp", None), P("fsdp")
    in_specs = (rows, P("fsdp", "seq"), lone, split, lone, split, lone, split, split, split, rows)
    out_specs = (rows, rows, lone, split, lone, lone, split, lone, split, split, split)
    return jax.shard_map(
        functools.partial(per_device, mesh.shape["fsdp"]),
        mesh=mesh,
        in_specs=in_specs,
        out_specs=out_specs,
        check_vma=False,
    )
```

```python
import functools

import jax
import jax.numpy as jnp
from jax import lax
from jax.experimental import pallas as pl
from jax.experimental.pallas import tpu as pltpu
from jax.sharding import PartitionSpec as P

HEAD = 64
LANES = 128
TILE = 256
EPSILON = 1e-06
THETA = 1000000.0
FAR = -1e30
MIB = 2**20
EARLY = 10
SHARED = 2

LIGHT = pl.CostEstimate(flops=1, bytes_accessed=1, transcendentals=0)
HEAVY = pl.CostEstimate(flops=6 * 10**10, bytes_accessed=16 * MIB, transcendentals=0)

bf16 = jnp.bfloat16
f32 = jnp.float32


def dot_nn(left, right):
    return lax.dot_general(left, right, (((1,), (0,)), ((), ())), preferred_element_type=f32)


def dot_nt(left, right):
    return lax.dot_general(left, right, (((1,), (1,)), ((), ())), preferred_element_type=f32)


def dot_tn(left, right):
    return lax.dot_general(left, right, (((0,), (0,)), ((), ())), preferred_element_type=f32)


def swap_halves(values_in):
    lane = lax.broadcasted_iota(jnp.int32, values_in.shape, 1)
    ahead = pltpu.roll(values_in, LANES - HEAD // 2, 1)
    behind = pltpu.roll(values_in, HEAD // 2, 1)
    return jnp.where(lane % HEAD < HEAD // 2, ahead, behind)


def turn(values_in, cosines, sines):
    return values_in * cosines + swap_halves(values_in) * sines


def turn_back(grads_in, cosines, sines):
    return grads_in * cosines - swap_halves(grads_in) * sines


def project_kernel(x_ref, gain_ref, w_ref, bias_ref, cos_ref, sin_ref, normed_ref, q_ref, kv_ref):
    x = x_ref[...].astype(f32)
    scale = lax.rsqrt(jnp.mean(x * x, axis=1, keepdims=True) + EPSILON)
    normed = (x * scale * gain_ref[...]).astype(bf16)
    normed_ref[...] = normed
    project = dot_nn(normed, w_ref[...]) + bias_ref[...]
    cosines, sines = cos_ref[...], sin_ref[...]
    width = q_ref.shape[1]
    for start in range(0, width, LANES):
        part = slice(start, start + LANES)
        q_ref[:, part] = turn(project[:, part], cosines, sines).astype(bf16) * (HEAD**-0.5)
    kv_ref[:, :LANES] = turn(project[:, width : width + LANES], cosines, sines).astype(bf16)
    kv_ref[:, LANES:] = project[:, width + LANES :].astype(bf16)


def project_call(x, gain, weight, bias, cosines, sines):
    tokens, width = x.shape
    outs = weight.shape[1]
    rows = tokens // 3
    row = lambda cols: pl.BlockSpec((rows, cols), lambda i: (i, 0))
    whole = lambda *shape: pl.BlockSpec(shape, lambda i: (0, 0))
    return pl.pallas_call(
        project_kernel,
        grid=(3,),
        in_specs=[
            row(width),
            whole(1, width),
            whole(width, outs),
            whole(1, outs),
            row(LANES),
            row(LANES),
        ],
        out_specs=[row(width), row(width), row(2 * LANES)],
        out_shape=[
            jax.ShapeDtypeStruct((tokens, width), bf16),
            jax.ShapeDtypeStruct((tokens, width), bf16),
            jax.ShapeDtypeStruct((tokens, 2 * LANES), bf16),
        ],
        compiler_params=pltpu.CompilerParams(vmem_limit_bytes=62 * MIB),
        cost_estimate=LIGHT,
        name="project",
    )(x, gain, weight, bias, cosines, sines)


def spread(ref, columns, out_ref, turned_ref=None):
    both = ref[:, columns].astype(f32)
    shifted = pltpu.roll(both, HEAD, 1)
    low = lax.broadcasted_iota(jnp.int32, both.shape, 1) < HEAD
    for head in range(2):
        for parity in range(2):
            source = both if head == parity else shifted
            alone = jnp.where(low if parity == 0 else ~low, source, 0.0)
            out_ref[head, parity] = alone.astype(bf16)
            if turned_ref is not None:
                turned_ref[head, parity] = alone.T.astype(bf16)


def causal(scores, flipped):
    row_at = lax.broadcasted_iota(jnp.int32, scores.shape, 0)
    col_at = lax.broadcasted_iota(jnp.int32, scores.shape, 1)
    return jnp.where(row_at <= col_at if flipped else col_at <= row_at, scores, FAR)


def near_forward_kernel(q_ref, qx_ref, kv_ref, kx_ref, o_ref, lse_ref, k_s, v_s, *, group):
    step = pl.program_id(0)
    block = q_ref.shape[0] // 2
    lane = lax.broadcasted_iota(jnp.int32, (block, LANES), 1)

    @pl.when(step == 0)
    def _():
        spread(kv_ref, slice(0, LANES), k_s)
        spread(kv_ref, slice(LANES, 2 * LANES), v_s)
        lse_ref[...] = jnp.zeros_like(lse_ref)

    for b in range(2):
        rows = slice(b * block, (b + 1) * block)
        q = jnp.concatenate([q_ref[rows], qx_ref[rows]], axis=1)
        total = None
        stats = lse_ref[rows]
        for parity in range(2):
            kv = (2 * step + parity) // group
            k_at = lambda rows: jnp.concatenate([k_s[kv, parity, rows], kx_ref[rows]], axis=1)
            pieces = [(causal(dot_nt(q, k_at(rows)), False), v_s[kv, parity, rows])]
            if b:
                first = slice(0, block)
                pieces.append((dot_nt(q, k_at(first)), v_s[kv, parity, first]))
            top = functools.reduce(jnp.maximum, [jnp.max(s, axis=1, keepdims=True) for s, _ in pieces])
            weights = [(jnp.exp(s - top), v) for s, v in pieces]
            norm = sum(jnp.sum(p, axis=1, keepdims=True) for p, _ in weights)
            out = sum(dot_nn(p.astype(bf16), v) for p, v in weights) * (1.0 / norm)
            total = out if total is None else total + out
            stats = jnp.where(lane == 2 * step + parity, top + jnp.log(norm), stats)
        o_ref[rows] = total
        lse_ref[rows] = stats


def far_forward_kernel(half_ref, q_ref, qx_ref, kv_ref, kx_ref, near_ref, stats_ref, o_ref, lse_ref, k_s, v_s, lse_s, *, group):
    step = pl.program_id(0)
    tokens = q_ref.shape[0]
    block = tokens // 2

    @pl.when(step == 0)
    def _():
        spread(kv_ref, slice(0, LANES), k_s)
        spread(kv_ref, slice(LANES, 2 * LANES), v_s)
        lse_s[...] = stats_ref[...]

    def run(blocks, keys):
        for b in blocks:
            rows = slice(b * block, (b + 1) * block)
            q = jnp.concatenate([q_ref[rows], qx_ref[rows]], axis=1)
            lane = lax.broadcasted_iota(jnp.int32, (block, LANES), 1)
            stats = lse_s[rows]
            total = None
            scale = None
            for parity in range(2):
                head = 2 * step + parity
                kv = head // group
                k = jnp.concatenate([k_s[kv, parity, keys], kx_ref[keys]], axis=1)
                s = dot_nt(q, k)
                top = jnp.max(s, axis=1, keepdims=True)
                p = jnp.exp(s - top)
                norm = jnp.sum(p, axis=1, keepdims=True)
                far = top + jnp.log(norm)
                near = jnp.sum(jnp.where(lane == head, stats, 0.0), axis=1, keepdims=True)
                both = jnp.maximum(near, far)
                both = both + jnp.log(jnp.exp(near - both) + jnp.exp(far - both))
                out = dot_nn(p.astype(bf16), v_s[kv, parity, keys]) * jnp.exp(top - both)
                total = out if total is None else total + out
                weight = jnp.exp(near - both)
                scale = weight if scale is None else jnp.where(lane < HEAD, scale, weight)
                stats = jnp.where(lane == head, both, stats)
            o_ref[rows] = (near_ref[rows] * scale + total).astype(bf16)
            lse_s[rows] = stats

    @pl.when(half_ref[0] == 0)
    def _():
        first = slice(0, block)
        o_ref[first] = near_ref[first].astype(bf16)
        run((1,), slice(0, tokens))

    @pl.when(half_ref[0] != 0)
    def _():
        run((0, 1), slice(0, block))

    @pl.when(step == pl.num_programs(0) - 1)
    def _():
        lse_ref[...] = lse_s[...].T


def near_forward(q, qx, kv, kx, group):
    tokens, width = q.shape
    column = pl.BlockSpec((tokens, LANES), lambda p: (0, p))
    whole = lambda *shape: pl.BlockSpec(shape, lambda p: (0, 0))
    spare = lambda: pltpu.VMEM((2, 2, tokens, LANES), bf16)
    return pl.pallas_call(
        functools.partial(near_forward_kernel, group=group),
        grid=(width // LANES,),
        in_specs=[column, whole(tokens, LANES), whole(tokens, 2 * LANES), whole(tokens, LANES)],
        out_specs=[column, whole(tokens, LANES)],
        scratch_shapes=[spare(), spare()],
        out_shape=[
            jax.ShapeDtypeStruct((tokens, width), f32),
            jax.ShapeDtypeStruct((tokens, LANES), f32),
        ],
        compiler_params=pltpu.CompilerParams(vmem_limit_bytes=62 * MIB),
        cost_estimate=HEAVY,
        name="attention_near",
    )(q, qx, kv, kx)


def far_forward(half, q, qx, kv, kx, near, stats, group):
    tokens, width = q.shape
    column = pl.BlockSpec((tokens, LANES), lambda p, *_: (0, p))
    whole = lambda *shape: pl.BlockSpec(shape, lambda p, *_: (0, 0))
    spare = lambda: pltpu.VMEM((2, 2, tokens, LANES), bf16)
    return pl.pallas_call(
        functools.partial(far_forward_kernel, group=group),
        grid_spec=pltpu.PrefetchScalarGridSpec(
            num_scalar_prefetch=1,
            grid=(width // LANES,),
            in_specs=[
                column,
                whole(tokens, LANES),
                whole(tokens, 2 * LANES),
                whole(tokens, LANES),
                column,
                whole(tokens, LANES),
            ],
            out_specs=[column, whole(LANES, tokens)],
            scratch_shapes=[spare(), spare(), pltpu.VMEM((tokens, LANES), f32)],
        ),
        out_shape=[
            jax.ShapeDtypeStruct((tokens, width), bf16),
            jax.ShapeDtypeStruct((LANES, tokens), f32),
        ],
        compiler_params=pltpu.CompilerParams(vmem_limit_bytes=62 * MIB),
        cost_estimate=LIGHT,
        name="attention_far",
    )(half, q, qx, kv, kx, near, stats)


def back_block(q, q_wide, g, lse, delta, k, kx, turned, v, masked):
    s = dot_nt(jnp.concatenate([k, kx], axis=1), q_wide)
    if masked:
        s = causal(s, True)
    p = jnp.exp(s - lse)
    ds = (p * (dot_nt(v, g) - delta)).astype(bf16)
    return dot_nn(p.astype(bf16), g), dot_nn(ds, q), dot_nn(turned, ds)


def gather_heads(acc, out_ref, columns):
    low = lax.broadcasted_iota(jnp.int32, acc.shape[2:], 1) < HEAD
    first = acc[0, 0] + pltpu.roll(acc[0, 1], HEAD, 1)
    second = acc[1, 1] + pltpu.roll(acc[1, 0], HEAD, 1)
    out_ref[:, columns] = jnp.where(low, first, second).astype(out_ref.dtype)


def far_backward_kernel(half_ref, q_ref, qx_ref, g_ref, o_ref, lse_ref, kv_ref, kx_ref, dq_ref, dkv_ref, k_s, t_s, v_s, ka, va, *, group):
    step = pl.program_id(0)
    tokens = q_ref.shape[0]
    block = tokens // 2
    keys, values = slice(0, LANES), slice(LANES, 2 * LANES)

    @pl.when(step == 0)
    def _():
        spread(kv_ref, keys, k_s, t_s)
        spread(kv_ref, values, v_s)
        ka[...] = jnp.zeros_like(ka)
        va[...] = jnp.zeros_like(va)

    def run(blocks, key_blocks):
        for b in blocks:
            rows = slice(b * block, (b + 1) * block)
            q = q_ref[rows]
            q_wide = jnp.concatenate([q, qx_ref[rows]], axis=1)
            g = g_ref[rows]
            product = (g.astype(f32) * o_ref[rows].astype(f32)).T
            total = None
            for parity in range(2):
                head = 2 * step + parity
                kv = head // group
                lse = lse_ref[pl.ds(head, 1), rows]
                delta = jnp.sum(product[parity * HEAD : (parity + 1) * HEAD], axis=0, keepdims=True)
                for c in key_blocks:
                    part = slice(c * block, (c + 1) * block)
                    dv, dk, dq = back_block(
                        q, q_wide, g, lse, delta, k_s[kv, parity, part], kx_ref[part],
                        t_s[kv, parity, :, part], v_s[kv, parity, part], False,
                    )
                    va[kv, parity, part] += dv
                    ka[kv, parity, part] += dk
                    total = dq if total is None else total + dq
            dq_ref[:, rows] = total

    @pl.when(half_ref[0] == 0)
    def _():
        dq_ref[:, :block] = jnp.zeros((LANES, block), f32)
        run((1,), (0, 1))

    @pl.when(half_ref[0] != 0)
    def _():
        run((0, 1), (0,))

    @pl.when(step == pl.num_programs(0) - 1)
    def _():
        gather_heads(ka, dkv_ref, keys)
        gather_heads(va, dkv_ref, values)


def near_backward_kernel(q_ref, qx_ref, g_ref, o_ref, lse_ref, cos_ref, sin_ref, kv_ref, kx_ref, far_ref, dq_ref, dkv_ref, k_s, t_s, v_s, ka, va, *, group):
    step = pl.program_id(0)
    tokens = q_ref.shape[0]
    block = tokens // 2
    keys, values = slice(0, LANES), slice(LANES, 2 * LANES)

    @pl.when(step == 0)
    def _():
        spread(kv_ref, keys, k_s, t_s)
        spread(kv_ref, values, v_s)
        ka[...] = jnp.zeros_like(ka)
        va[...] = jnp.zeros_like(va)

    for b in range(2):
        rows = slice(b * block, (b + 1) * block)
        q = q_ref[rows]
        q_wide = jnp.concatenate([q, qx_ref[rows]], axis=1)
        g = g_ref[rows]
        product = (g.astype(f32) * o_ref[rows].astype(f32)).T
        total = far_ref[:, rows]
        for parity in range(2):
            head = 2 * step + parity
            kv = head // group
            lse = lse_ref[pl.ds(head, 1), rows]
            delta = jnp.sum(product[parity * HEAD : (parity + 1) * HEAD], axis=0, keepdims=True)
            for c in range(b + 1):
                part = slice(c * block, (c + 1) * block)
                dv, dk, dq = back_block(
                    q, q_wide, g, lse, delta, k_s[kv, parity, part], kx_ref[part],
                    t_s[kv, parity, :, part], v_s[kv, parity, part], c == b,
                )
                va[kv, parity, part] += dv
                ka[kv, parity, part] += dk
                total = total + dq
        dq_ref[rows] = turn_back(total.T * (HEAD**-0.5), cos_ref[rows], sin_ref[rows]).astype(bf16)

    @pl.when(step == pl.num_programs(0) - 1)
    def _():
        gather_heads(ka, dkv_ref, keys)
        gather_heads(va, dkv_ref, values)


def backward_scratch(tokens):
    return [
        pltpu.VMEM((2, 2, tokens, LANES), bf16),
        pltpu.VMEM((2, 2, LANES, tokens), bf16),
        pltpu.VMEM((2, 2, tokens, LANES), bf16),
        pltpu.VMEM((2, 2, tokens, LANES), f32),
        pltpu.VMEM((2, 2, tokens, LANES), f32),
    ]


def far_backward(half, q, qx, g, o, lse, kv, kx, group):
    tokens, width = q.shape
    column = pl.BlockSpec((tokens, LANES), lambda p, *_: (0, p))
    across = pl.BlockSpec((LANES, tokens), lambda p, *_: (p, 0))
    whole = lambda *shape: pl.BlockSpec(shape, lambda p, *_: (0, 0))
    return pl.pallas_call(
        functools.partial(far_backward_kernel, group=group),
        grid_spec=pltpu.PrefetchScalarGridSpec(
            num_scalar_prefetch=1,
            grid=(width // LANES,),
            in_specs=[
                column,
                whole(tokens, LANES),
                column,
                column,
                whole(LANES, tokens),
                whole(tokens, 2 * LANES),
                whole(tokens, LANES),
            ],
            out_specs=[across, whole(tokens, 2 * LANES)],
            scratch_shapes=backward_scratch(tokens),
        ),
        out_shape=[
            jax.ShapeDtypeStruct((width, tokens), f32),
            jax.ShapeDtypeStruct((tokens, 2 * LANES), bf16),
        ],
        compiler_params=pltpu.CompilerParams(vmem_limit_bytes=62 * MIB),
        cost_estimate=HEAVY,
        name="attention_far_back",
    )(half, q, qx, g, o, lse, kv, kx)


def near_backward(q, qx, g, o, lse, cosines, sines, kv, kx, far, group):
    tokens, width = q.shape
    column = pl.BlockSpec((tokens, LANES), lambda p: (0, p))
    across = pl.BlockSpec((LANES, tokens), lambda p: (p, 0))
    whole = lambda *shape: pl.BlockSpec(shape, lambda p: (0, 0))
    return pl.pallas_call(
        functools.partial(near_backward_kernel, group=group),
        grid=(width // LANES,),
        in_specs=[
            column,
            whole(tokens, LANES),
            column,
            column,
            whole(LANES, tokens),
            whole(tokens, LANES),
            whole(tokens, LANES),
            whole(tokens, 2 * LANES),
            whole(tokens, LANES),
            across,
        ],
        out_specs=[column, whole(tokens, 2 * LANES)],
        scratch_shapes=backward_scratch(tokens),
        out_shape=[
            jax.ShapeDtypeStruct((tokens, width), bf16),
            jax.ShapeDtypeStruct((tokens, 2 * LANES), f32),
        ],
        compiler_params=pltpu.CompilerParams(vmem_limit_bytes=62 * MIB),
        cost_estimate=LIGHT,
        name="attention_near_back",
    )(q, qx, g, o, lse, cosines, sines, kv, kx, far)


def project_back_kernel(at_ref, x_ref, gain_ref, normed_ref, dq_ref, dkv_ref, got_ref, cos_ref, sin_ref, w_ref, gm_ref, att_ref, gin_ref, mine_ref, theirs_ref, bias_ref, gain_grad_ref):
    kv = dkv_ref[...] + got_ref[...].astype(f32)
    keys = turn_back(kv[:, :LANES], cos_ref[...], sin_ref[...])
    project = jnp.concatenate([dq_ref[...], keys.astype(bf16), kv[:, LANES:].astype(bf16)], axis=1)
    bias_ref[...] = jnp.sum(project.astype(f32), axis=0, keepdims=True)
    grad = dot_nt(project, w_ref[...])
    x = x_ref[...].astype(f32)
    scale = lax.rsqrt(jnp.mean(x * x, axis=1, keepdims=True) + EPSILON)
    normal = x * scale
    gain_grad_ref[...] = jnp.sum(grad * normal, axis=0, keepdims=True)
    grad = grad * gain_ref[...]
    middle = gm_ref[...]
    mean = jnp.mean(grad * normal, axis=1, keepdims=True)
    gin_ref[...] = (middle + scale * (grad - normal * mean)).astype(bf16)
    core, inner, line, seq = (at_ref[i] for i in range(4))
    width = x.shape[1]
    chips = 8
    piece = width // chips // 2
    normed_t, att_t = normed_ref[...].T, att_ref[...].T
    columns = [(normed_t, project[:, s : s + LANES]) for s in range(0, project.shape[1], LANES)]
    branch = middle.astype(bf16)
    columns += [(att_t, branch[:, s : s + LANES]) for s in range(0, width, LANES)]
    for pair in range(len(columns) // 2):
        (left, one), (other, two) = columns[2 * pair : 2 * pair + 2]
        if left is other:
            value = dot_nn(left, jnp.concatenate([one, two], axis=1))
            one, two = value[:, :LANES], value[:, LANES:]
        else:
            one, two = dot_nn(left, one), dot_nn(other, two)
        quarter = pair // 2
        half = (quarter % 2) ^ seq
        start = quarter // 2 * 4 * piece + pair % 2 * 2 * piece
        for chip in range(chips):
            rows = slice(chip * 2 * piece, (chip + 1) * 2 * piece)
            here, there = one[rows], two[rows]
            low = jnp.concatenate([here[:piece], there[:piece]], axis=0)
            high = jnp.concatenate([here[piece:], there[piece:]], axis=0)
            away = (chip // 2) ^ line
            place = 2 * (away % 2) + away // 2
            for ref, first in ((mine_ref, core == 0), (theirs_ref, core != 0)):
                value = jnp.where(first, low, high).astype(bf16)
                ref[(chip % 2) ^ inner, half, place, start : start + 2 * piece, :] = value
    for ref in (mine_ref, theirs_ref):
        ref[:, :, :, 8 * piece :, :] = jnp.zeros(ref.shape[:3] + (8, LANES), bf16)


def project_back(at, x, gain, normed, dq, dkv, got, cosines, sines, weight, grad_middle, attended):
    tokens, width = x.shape
    outs = weight.shape[1]
    rows = (outs + width) // LANES * (width // 16) // 2 + 8
    packed = jax.ShapeDtypeStruct((2, 2, 4, rows, LANES), bf16)
    out_shape = [
        jax.ShapeDtypeStruct((tokens, width), bf16),
        packed,
        packed,
        jax.ShapeDtypeStruct((1, outs), f32),
        jax.ShapeDtypeStruct((1, width), f32),
    ]
    args = (x, gain, normed, dq, dkv, got, cosines, sines, weight, grad_middle, attended)
    whole = lambda array: pl.BlockSpec(array.shape, lambda i, *_: (0,) * len(array.shape))
    return pl.pallas_call(
        project_back_kernel,
        grid_spec=pltpu.PrefetchScalarGridSpec(
            num_scalar_prefetch=1,
            grid=(1,),
            in_specs=[whole(array) for array in args],
            out_specs=[whole(array) for array in out_shape],
        ),
        out_shape=out_shape,
        compiler_params=pltpu.CompilerParams(vmem_limit_bytes=62 * MIB),
        cost_estimate=LIGHT,
        name="project_back",
    )(at, *args)


LINE = (0, 2, 1, 3)


def mlp_kernel(at_ref, near_ref, far_ref, gnear_ref, gfar_ref, *rest, counts, tiles, first, split):
    w_refs, rest = rest[: len(counts)], rest[len(counts) :]
    out_ref, grad_ref, other_ref, keep_x, send_x, keep_y, send_y = rest[:7]
    n_s, t_s, g_s, p_s, out_s, grad_s, gate_s, up_s, down_s = rest[7:]
    step = pl.program_id(0)
    tile = 2 * (first + step) + at_ref[0]
    tokens, width = near_ref.shape
    shards = w_refs[0].shape[0]
    depth = width // shards
    own = TILE // shards
    chips = shards // 2

    @pl.when(step == 0)
    def _():
        n_s[:tokens] = near_ref[...]
        n_s[tokens:] = far_ref[...]
        g_s[:tokens] = gnear_ref[...]
        g_s[tokens:] = gfar_ref[...]
        t_s[:, :tokens] = near_ref[...].T
        t_s[:, tokens:] = far_ref[...].T
        out_s[...] = jnp.zeros_like(out_s)
        grad_s[...] = jnp.zeros_like(grad_s)

    def load(w_ref):
        for at, square in ((0, gate_s), (2 * depth, up_s)):
            for c in range(TILE // LANES):
                rows = w_ref[:, at + c * depth : at + (c + 1) * depth, :]
                rows = rows.astype(f32).reshape(width, LANES).astype(bf16)
                square[:, c * LANES : (c + 1) * LANES] = rows
        for c in range(width // LANES):
            rows = w_ref[:, 4 * depth + c * own : 4 * depth + (c + 1) * own, :]
            down_s[:, c * LANES : (c + 1) * LANES] = rows.reshape(TILE, LANES)

    begin = 0
    for w_ref, many in zip(w_refs, counts):
        pl.when((step >= begin) & (step < begin + many))(functools.partial(load, w_ref))
        begin += many

    @pl.when(tile >= tiles)
    def _():
        p_s[...] = jnp.zeros_like(p_s)

    @pl.when(tile < tiles)
    def _():
        gate_w, up_w, down_w = gate_s[...], up_s[...], down_s[...]
        n = n_s[...]
        g = g_s[...]
        gate = dot_nn(n, gate_w)
        up = dot_nn(n, up_w)
        grad_hidden = dot_nt(g, down_w)
        sig = 1.0 / (1.0 + jnp.exp(-gate))
        silu = gate * sig
        hidden = (silu * up).astype(bf16)
        grad_gate = (grad_hidden * up * (sig + silu * (1.0 - sig))).astype(bf16)
        grad_up = (grad_hidden * silu).astype(bf16)
        out_s[...] += dot_nn(hidden, down_w)
        grad_s[...] += dot_nt(grad_gate, gate_w) + dot_nt(grad_up, up_w)
        for at, value in ((0, dot_nn(t_s[...], grad_gate)), (1, dot_nn(t_s[...], grad_up))):
            for c in range(TILE // LANES):
                part = value[:, c * LANES : (c + 1) * LANES].astype(bf16)
                start = (2 * at + c) * 2 * depth
                p_s[:, start : start + 2 * depth, :] = part.reshape(chips, 2 * depth, LANES)
        down = dot_tn(hidden, g)
        for c in range(width // LANES):
            part = down[:, c * LANES : (c + 1) * LANES].astype(bf16)
            start = 8 * depth + c * 2 * own
            p_s[:, start : start + 2 * own, :] = part.reshape(chips, 2 * own, LANES)

    half_rows = 6 * depth
    inner, line, seq = at_ref[1], at_ref[2], at_ref[3]

    def piece(line_off, inner_off, half_off):
        chip = 2 * (line ^ line_off) + (inner ^ inner_off)
        start = pl.multiple_of((seq ^ half_off) * half_rows, half_rows)
        return p_s[chip, pl.ds(start, half_rows), :]

    @pl.when(step < split)
    def _():
        for a, off in enumerate(LINE):
            for h in range(2):
                keep_x[h, a] = piece(off, 0, h)
                send_x[h, a] = piece(off, 1, h)

    @pl.when(step >= split)
    def _():
        for a, off in enumerate(LINE):
            for b in range(2):
                keep_y[b, a] = piece(off, b, 0)
                send_y[b, a] = piece(off, b, 1)

    @pl.when(step == pl.num_programs(0) - 1)
    def _():
        out_ref[...] = out_s[:tokens]
        grad_ref[...] = grad_s[:tokens]
        other_ref[:tokens] = out_s[tokens:].astype(bf16)
        other_ref[tokens:] = grad_s[tokens:].astype(bf16)


def mlp_call(at, near, far, gnear, gfar, weights, counts, tiles, first, split):
    tokens, width = near.shape
    shards = weights[0][0].shape[0]
    rows = 6 * width // shards
    count = sum(counts)
    whole = lambda *shape: pl.BlockSpec(shape, lambda j, *_: (0,) * len(shape))
    early = pl.BlockSpec((2, 4, rows, LANES), lambda j, *_: (0, 0, jnp.minimum(j, split - 1), 0))
    late = pl.BlockSpec((2, 4, rows, LANES), lambda j, *_: (0, 0, jnp.maximum(j - split, 0), 0))
    shape_x = jax.ShapeDtypeStruct((2, 4, rows * split, LANES), bf16)
    shape_y = jax.ShapeDtypeStruct((2, 4, rows * (count - split), LANES), bf16)
    wide = jax.ShapeDtypeStruct((tokens, width), f32)

    def block_of(index):
        return pl.BlockSpec((shards, rows, LANES), lambda j, at: (0, index(j, at), 0))

    return pl.pallas_call(
        functools.partial(mlp_kernel, counts=counts, tiles=tiles, first=first, split=split),
        grid_spec=pltpu.PrefetchScalarGridSpec(
            num_scalar_prefetch=1,
            grid=(count,),
            in_specs=[whole(tokens, width)] * 4 + [block_of(index) for _, index in weights],
            out_specs=[whole(tokens, width)] * 2
            + [whole(2 * tokens, width), early, early, late, late],
            scratch_shapes=[
                pltpu.VMEM((2 * tokens, width), bf16),
                pltpu.VMEM((width, 2 * tokens), bf16),
                pltpu.VMEM((2 * tokens, width), bf16),
                pltpu.VMEM((shards // 2, 2 * rows, LANES), bf16),
                pltpu.VMEM((2 * tokens, width), f32),
                pltpu.VMEM((2 * tokens, width), f32),
                pltpu.VMEM((width, TILE), bf16),
                pltpu.VMEM((width, TILE), bf16),
                pltpu.VMEM((TILE, width), bf16),
            ],
        ),
        out_shape=[
            wide,
            wide,
            jax.ShapeDtypeStruct((2 * tokens, width), bf16),
            shape_x,
            shape_x,
            shape_y,
            shape_y,
        ],
        compiler_params=pltpu.CompilerParams(vmem_limit_bytes=62 * MIB),
        cost_estimate=HEAVY,
        name="feed_forward",
    )(at, near, far, gnear, gfar, *(w for w, _ in weights))


def pack_kernel(half_ref, gate_ref, up_ref, down_ref, out_ref, one_ref, two_ref, *, shards, early, shared):
    depth, hidden = gate_ref.shape
    width = down_ref.shape[1]
    tiles = hidden // TILE
    own = TILE // shards
    rows = 6 * depth
    per = LANES // own
    lane = lax.broadcasted_iota(jnp.int32, (depth, LANES), 1) // own

    def write(target, at, blocks, tile):
        target[at : at + 4 * depth, :] = blocks
        for c in range(width // LANES):
            start = at + 4 * depth + c * own
            target[start : start + own, :] = down_ref[tile * own : (tile + 1) * own, c * LANES : (c + 1) * LANES]

    for tile in range(tiles):
        blocks = []
        for ref in (gate_ref, up_ref):
            for c in range(TILE // LANES):
                total = None
                by_shift = {}
                for i in range(per):
                    at = ((c * per + i) * tiles + tile) * own
                    by_shift.setdefault((i - at // own) % per, []).append((i, at // LANES))
                for shift, sources in by_shift.items():
                    value = None
                    for i, block in sources:
                        part = ref[:, block * LANES : (block + 1) * LANES].astype(f32)
                        here = lane == (i - shift) % per
                        value = part if value is None else jnp.where(here, part, value)
                    if shift:
                        value = pltpu.roll(value, shift * own, 1)
                    if total is None:
                        total = value
                    else:
                        for i, _ in sources:
                            total = jnp.where(lane == i, value, total)
                blocks.append(total)
        blocks = jnp.concatenate(blocks, axis=0).astype(bf16)
        if tile < early:
            write(one_ref, tile * rows, blocks, tile)
        elif tile < early + 2 * shared:
            which, at = divmod(tile - early, shared)
            pl.when(half_ref[0] == which)(
                functools.partial(write, one_ref, (early + at) * rows, blocks, tile)
            )
        else:
            write(two_ref, (tile - early - 2 * shared) * rows, blocks, tile)
    pieces = [out_ref[:, c * LANES : (c + 1) * LANES].astype(f32) for c in range(width // LANES)]
    one_ref[(early + shared) * rows :, :] = jnp.concatenate(pieces, axis=0).astype(bf16)


def pack_call(half, w_gate, w_up, w_down, w_out, shards, early, shared):
    depth, hidden = w_gate.shape
    width = w_down.shape[1]
    rows = 6 * depth
    tiles = hidden // TILE
    sizes = (early + shared) * rows + width // LANES * depth, (tiles - early - 2 * shared) * rows
    whole = lambda shape: pl.BlockSpec(shape, lambda i, *_: (0, 0))
    return pl.pallas_call(
        functools.partial(pack_kernel, shards=shards, early=early, shared=shared),
        grid_spec=pltpu.PrefetchScalarGridSpec(
            num_scalar_prefetch=1,
            grid=(1,),
            in_specs=[whole(w.shape) for w in (w_gate, w_up, w_down, w_out)],
            out_specs=[whole((n, LANES)) for n in sizes],
        ),
        out_shape=[jax.ShapeDtypeStruct((n, LANES), bf16) for n in sizes],
        compiler_params=pltpu.CompilerParams(vmem_limit_bytes=62 * MIB),
        cost_estimate=LIGHT,
        name="pack",
    )(half, w_gate, w_up, w_down, w_out)


def unpack_kernel(one_ref, two_ref, gate_ref, up_ref, down_ref, *, shards):
    depth, hidden = gate_ref.shape
    width = down_ref.shape[1]
    tiles = hidden // TILE
    own = TILE // shards
    per = LANES // own
    early = one_ref.shape[0]
    lane = lax.broadcasted_iota(jnp.int32, (depth, LANES), 1) // own
    tile_at = lambda tile: one_ref.at[tile] if tile < early else two_ref.at[tile - early]
    wide = [tile_at(tile)[: 4 * depth, :].astype(f32) for tile in range(tiles)]
    for number, ref in enumerate((gate_ref, up_ref)):
        for block in range(hidden // LANES):
            total = None
            for i in range(per):
                shard, tile = divmod(block * per + i, tiles)
                c, at = divmod(shard, per)
                start = (2 * number + c) * depth
                value = wide[tile][start : start + depth]
                if (i - at) % per:
                    value = pltpu.roll(value, (i - at) % per * own, 1)
                total = value if total is None else jnp.where(lane == i, value, total)
            ref[:, block * LANES : (block + 1) * LANES] = total
    for tile in range(tiles):
        for c in range(width // LANES):
            start = 4 * depth + c * own
            value = tile_at(tile)[start : start + own, :].astype(f32)
            down_ref[tile * own : (tile + 1) * own, c * LANES : (c + 1) * LANES] = value


def unpack_call(packed, tiles, shards, depth):
    own = TILE // shards
    width = (packed[0].shape[1] - 4 * depth) // own * LANES
    return pl.pallas_call(
        functools.partial(unpack_kernel, shards=shards),
        out_shape=[
            jax.ShapeDtypeStruct((depth, tiles * TILE), f32),
            jax.ShapeDtypeStruct((depth, tiles * TILE), f32),
            jax.ShapeDtypeStruct((tiles * own, width), f32),
        ],
        compiler_params=pltpu.CompilerParams(vmem_limit_bytes=62 * MIB),
        cost_estimate=LIGHT,
        name="unpack",
    )(*packed)


def pack_weights(w_gate, w_up, w_down, shards):
    depth, hidden = w_gate.shape
    tiles = hidden // TILE
    own = TILE // shards

    def columns(weight):
        parts = weight.reshape(depth, shards, tiles, own).transpose(0, 2, 1, 3)
        parts = parts.reshape(depth, tiles, TILE // LANES, LANES).transpose(1, 2, 0, 3)
        return parts.reshape(tiles, -1, LANES)

    width = w_down.shape[1]
    down = w_down.reshape(tiles, own, width // LANES, LANES).transpose(0, 2, 1, 3)
    return jnp.concatenate([columns(w_gate), columns(w_up), down.reshape(tiles, -1, LANES)], axis=1)


def unpack_grads(packed, shards, depth):
    tiles = packed.shape[0]
    own = TILE // shards

    def columns(part):
        part = part.reshape(tiles, TILE // LANES, depth, LANES).transpose(2, 0, 1, 3)
        part = part.reshape(depth, tiles, shards, own).transpose(0, 2, 1, 3)
        return part.reshape(depth, tiles * TILE)

    gate, up = columns(packed[:, : 2 * depth]), columns(packed[:, 2 * depth : 4 * depth])
    down = packed[:, 4 * depth :].reshape(tiles, -1, own, LANES).transpose(0, 2, 1, 3)
    return gate, up, down.reshape(tiles * own, -1)


def regroup_weights(gathered, groups, tiles, depth, own):
    shards = gathered.shape[0]
    if shards == groups:
        return gathered
    many = shards // groups
    gathered = gathered.reshape(groups, many, tiles, -1, LANES)
    outs = []
    for start, size in ((0, depth), (2 * depth, depth), (4 * depth, own)):
        stop = start + 2 * depth
        part = gathered[:, :, :, start:stop].reshape(groups, many, tiles, -1, size, LANES)
        outs.append(part.transpose(0, 2, 3, 1, 4, 5).reshape(groups, tiles, -1, LANES))
    return jnp.concatenate(outs, axis=2).reshape(groups, -1, LANES)


class Wires:
    def __init__(self, shards):
        self.shards = shards
        place = lax.axis_index("fsdp")
        self.core = place % 2
        self.inner = (place // 2) % 2
        self.line = place // 4
        self.seq = lax.axis_index("seq")

    def flip(self, values_in, bit):
        return lax.ppermute(values_in, "fsdp", [(i, i ^ bit) for i in range(self.shards)])

    def other_half(self, values_in):
        return lax.ppermute(values_in, "seq", [(0, 1), (1, 0)])


def ordered(bit, own, other):
    return jnp.where(bit == 0, own, other), jnp.where(bit == 0, other, own)


def gather_small(wires, shard, beside):
    if wires.shards != 16:
        return lax.all_gather(shard, "fsdp", axis=0, tiled=False)
    rows = shard.shape[0] // 2
    have = lax.dynamic_slice_in_dim(shard, wires.seq * rows, rows)[None]
    have = jnp.stack(ordered(wires.line // 2, have, wires.flip(have, 8)), axis=0)
    have = jnp.concatenate(ordered(wires.line % 2, have, wires.flip(have, 4)), axis=1)
    have = have.reshape(4, rows, -1)
    beside = beside(have)
    have = jnp.stack(ordered(wires.inner, have, after(wires.flip(have, 2), beside)), axis=1)
    have = jnp.concatenate(ordered(wires.seq, have, wires.other_half(have)), axis=2)
    have = jnp.stack(ordered(wires.core, have, wires.flip(have, 1)), axis=2)
    return have.reshape((16,) + shard.shape)


def pick(values_in, place, axis):
    return lax.dynamic_index_in_dim(values_in, place, axis, keepdims=False)


def plus(*terms):
    return sum(term.astype(f32) for term in terms).astype(bf16)


def after(values_in, others):
    return lax.optimization_barrier((values_in, others))[0]


class ChipSum:
    def __init__(self, wires, keep_x, send_x, keep_y, send_y):
        self.wires = wires
        self.kept = keep_x, keep_y
        self.sent = send_x, send_y

    def first(self, others):
        send_x, send_y = after(self.sent, others)
        self.got = [(self.wires.flip(send_x, 2), self.wires.other_half(send_y))]

    def second(self, others):
        self.got = after(self.got[0], others)
        self.sent = tuple(plus(k[1], g[1]) for k, g in zip(self.kept, self.got))
        self.next = self.wires.other_half(self.sent[0]), self.wires.flip(self.sent[1], 2)

    def third(self, others):
        terms = list(zip(self.kept, self.got, after(self.next, others)))
        part = lambda at: jnp.concatenate([plus(k[0][at], g[0][at], n[at]) for k, g, n in terms], axis=1)
        self.sent = part(slice(2, 4))
        self.kept = part(slice(0, 2))
        self.got = self.wires.flip(self.sent, 4)

    def fourth(self, others):
        self.got = after(self.got, others)
        self.sent = plus(self.kept[1], self.got[1])
        self.next = self.wires.flip(self.sent, 8)

    def fifth(self, others):
        self.kept = self.sent = plus(self.kept[0], self.got[0], after(self.next, others))

    def sixth(self, others):
        self.got = self.wires.other_half(after(self.sent, others))

    def total(self, others):
        return ordered(self.wires.seq, self.kept, after(self.got, others))


class SmallSum:
    def __init__(self, wires, mine, theirs, cut):
        self.wires, self.mine, self.cut = wires, mine, cut
        self.theirs = wires.flip(theirs, 1)

    def first(self, others):
        wires, cut = self.wires, self.cut
        self.theirs = after(self.theirs, others)
        both = lambda *at: plus(self.mine[at], self.theirs[at])
        whole, top, end = slice(None), slice(0, cut), slice(cut, None)
        self.sent = both(1, whole, whole, top), both(whole, 1, whole, end)
        self.kept = both(0, whole, whole, top), both(whole, 0, whole, end)
        self.got = wires.flip(self.sent[0], 2), wires.other_half(self.sent[1])

    def second(self, others):
        got = after(self.got, others)
        self.sent = tuple(plus(k[1], g[1]) for k, g in zip(self.kept, got))
        self.kept = tuple(plus(k[0], g[0]) for k, g in zip(self.kept, got))
        self.got = self.wires.other_half(self.sent[0]), self.wires.flip(self.sent[1], 2)

    def third(self, others):
        terms = list(zip(self.kept, after(self.got, others)))
        part = lambda at: jnp.concatenate([plus(k[at], g[at]) for k, g in terms], axis=1)
        self.sent, self.kept = part(slice(2, 4)), part(slice(0, 2))
        self.got = self.wires.flip(self.sent, 4)

    def fourth(self, others):
        got = after(self.got, others)
        self.sent, self.kept = plus(self.kept[1], got[1]), plus(self.kept[0], got[0])
        self.got = self.wires.flip(self.sent, 8)

    def fifth(self, others):
        self.sent = plus(self.kept, after(self.got, others))
        self.got = self.wires.other_half(self.sent)

    def total(self, others):
        return jnp.stack(ordered(self.wires.seq, self.sent, after(self.got, others)), axis=0)


def norm_back(grad_normed, normal_part, inv_scale, gain_float):
    scaled = grad_normed * gain_float
    return inv_scale * (
        scaled - normal_part * jnp.mean(scaled * normal_part, axis=-1, keepdims=True)
    )


def rms_scale(values_in):
    return lax.rsqrt(jnp.mean(values_in * values_in, axis=-1, keepdims=True) + EPSILON)


def quarters_in(wires, values_in):
    half = values_in.shape[0] // 2
    got = wires.other_half(values_in[half:])
    return jnp.concatenate(ordered(wires.seq, values_in[:half], got), axis=0)


def quarters_out(wires, values_in, others=()):
    half = values_in.shape[0] // 2
    first, second = values_in[:half], values_in[half:]
    kept, sent = ordered(wires.seq, first, second)
    return jnp.concatenate([kept, after(wires.other_half(sent), others)], axis=0)


def per_device(
    shards, tokens, seg_ids, first_gain, w_qkv, b_qkv, w_out, second_gain, w_gate, w_up, w_down, cotangent
):
    wires = Wires(shards)
    tokens = tokens[0]
    count, width = tokens.shape
    depth, qkv_width = w_qkv.shape
    kv_width = (qkv_width - width) // 2
    group = (width // HEAD) // (kv_width // HEAD)
    tiles = w_gate.shape[1] // TILE
    own = TILE // shards
    own_bias = b_qkv.shape[0]
    groups = 16
    chips = groups // 2
    full_depth = width // groups
    full_own = TILE // groups
    small_mesh = shards == groups
    half = wires.seq.astype(jnp.int32).reshape(1)
    if small_mesh:
        at = jnp.stack([wires.core, wires.inner, wires.line, wires.seq]).astype(jnp.int32)
    else:
        at = jnp.stack([wires.core] + [jnp.zeros_like(wires.core)] * 3).astype(jnp.int32)
    steps = -(-tiles // 2)
    early, shared = (EARLY, SHARED) if small_mesh else (2 * (steps // 2), 0)

    pad_rows = -(-(depth + 1) // 8) * 8 - depth
    vector = jnp.concatenate([first_gain, b_qkv, second_gain])
    vector = jnp.pad(vector, (0, qkv_width - vector.shape[0]))
    small = jnp.concatenate([w_qkv, jnp.pad(vector[None], ((0, pad_rows - 1), (0, 0)))], axis=0)
    other_segs = wires.other_half(seg_ids)
    tokens = quarters_in(wires, tokens)
    small, (w_gate, w_up, w_down, w_out) = lax.optimization_barrier((small, (w_gate, w_up, w_down, w_out)))
    out_packed = w_out.reshape(depth, width // LANES, LANES).transpose(1, 0, 2).reshape(-1, LANES)
    if small_mesh:
        packed_one, packed_two = pack_call(
            half, w_gate, w_up, w_down, w_out, shards, early, shared
        )
    else:
        packed = pack_weights(w_gate, w_up, w_down, shards)
        packed_one = jnp.concatenate([packed[:early].reshape(-1, LANES), out_packed], axis=0)
        packed_two = packed[early:].reshape(-1, LANES)
    all_one = lax.all_gather(packed_one, "fsdp", axis=0, tiled=False)
    packed_two = after(packed_two, packed_one)
    all_two = lax.all_gather(packed_two, "fsdp", axis=0, tiled=False)
    block = count // 2

    def tables(seg_ids, other_segs):
        less = lambda k: jnp.sum((seg_ids < k).astype(jnp.int32)) + jnp.sum((other_segs < k).astype(jnp.int32))
        ones, twos = less(1), less(2)
        own_segs = jnp.concatenate(ordered(wires.seq, seg_ids[0, :block], other_segs[0, block:]))
        far_segs = jnp.concatenate(ordered(wires.seq, seg_ids[0, block:], other_segs[0, :block]))
        index = jnp.arange(count, dtype=jnp.int32)
        index = index + jnp.where(wires.seq == 0, jnp.where(index < block, 0, 2 * block), block)
        local_pos = index - jnp.where(own_segs == 0, 0, jnp.where(own_segs == 1, ones, twos))
        inverse = THETA ** (-(jnp.arange(HEAD // 2, dtype=f32) * 2.0 / HEAD))
        angles = local_pos.astype(f32)[:, None] * inverse[None, :]
        cosines, sines = jnp.cos(angles), jnp.sin(angles)
        cosines = jnp.concatenate([cosines] * 4, axis=1)
        sines = jnp.concatenate([-sines, sines] * 2, axis=1)
        doc = jnp.arange(LANES, dtype=jnp.int32)[None, :]
        kx = (own_segs[:, None] == doc).astype(bf16)
        rkx = (far_segs[:, None] == doc).astype(bf16)
        qx = jnp.where((own_segs[:, None] == doc) | (doc >= 3), 0.0, FAR).astype(bf16)
        return cosines, sines, kx, rkx, qx

    made = []

    def beside(started):
        made.extend(tables(*after((seg_ids, other_segs), started)))
        made.append(after(tokens, started))
        return tuple(made)

    small_all = gather_small(wires, small, beside)
    if not made:
        beside(())
    cosines, sines, kx, rkx, qx, tokens = made
    qkv_full = small_all[:, :depth].reshape(width, qkv_width)
    vectors = small_all[:, depth]
    gain_one = vectors[:, :depth].reshape(1, width).astype(f32)
    bias = vectors[:, depth : depth + own_bias].reshape(1, qkv_width).astype(f32)
    gain_two = vectors[:, depth + own_bias : 2 * depth + own_bias].reshape(1, width).astype(f32)

    normed, queries, kv = project_call(tokens, gain_one, qkv_full, bias, cosines, sines)
    far_kv = wires.other_half(kv)
    cotangent = after(cotangent[0], small_all)
    got = wires.other_half(cotangent[block:])
    near, stats = near_forward(queries, qx, kv, kx, group)
    far_kv, got = after((far_kv, got), stats)
    grad_mlp = jnp.concatenate(ordered(wires.seq, cotangent[:block], got), axis=0)
    far_grad = wires.flip(grad_mlp, 1)
    attended, lse = far_forward(half, queries, qx, far_kv, rkx, near, after(stats, grad_mlp), group)
    far_grad = after(far_grad, lse)
    first_rows = all_one.shape[1] - out_packed.shape[0]
    out_full = all_one[:, first_rows:].reshape(shards, width // LANES, depth, LANES)
    out_full = out_full.transpose(0, 2, 1, 3).reshape(width, width)
    residual_in = tokens.astype(f32)
    middle = residual_in + dot_nn(attended, out_full)
    inv_two = rms_scale(middle)
    normal_two = middle * inv_two
    normed_two = (normal_two * gain_two).astype(bf16)
    far_normed = wires.flip(normed_two, 1)

    if not small_mesh:
        all_one = regroup_weights(all_one[:, :first_rows], groups, early, depth, own)
        all_two = regroup_weights(all_two, groups, tiles - early, depth, own)
    rows = 6 * full_depth
    tokens_in = at, normed_two, far_normed, grad_mlp, far_grad
    own_tile = lambda start, last: lambda j, at: jnp.clip(2 * (j - start) + at[0], 0, last)
    one_steps = early // 2
    two_weights, two_counts = [(all_two, own_tile(shared, tiles - early - 2 * shared - 1))], [steps - one_steps - shared]
    if shared:
        mine = lax.dynamic_slice_in_dim(all_one, (early + wires.core) * rows, rows, axis=1)
        theirs = wires.other_half(mine)
    out_one, grad_one, other_one, *grads_one = mlp_call(
        *tokens_in, [(all_one, own_tile(0, early - 1))], [one_steps], tiles, 0, one_steps // 2
    )
    if shared:
        both = jnp.concatenate(ordered(wires.seq, mine, after(theirs, grad_one)), axis=1)
        two_weights.insert(0, (both, lambda j, at: jnp.minimum(j, shared - 1)))
        two_counts.insert(0, shared)
    if small_mesh:
        sum_one = ChipSum(wires, *grads_one)
        sum_one.first(())
    back_one = wires.flip(other_one, 1)
    out_two, grad_two, other_two, *grads_two = mlp_call(
        *tokens_in, two_weights, two_counts, tiles, one_steps, (steps - one_steps + 1) // 2
    )
    if small_mesh:
        sum_two = ChipSum(wires, *grads_two)
        sum_one.second(grad_two)
        other_two = after(other_two, sum_one.sent)
    back_two = wires.flip(other_two, 1)
    back_one = after(back_one, grad_two)

    def halves(own_one, own_two, at):
        rows = slice(at * count, (at + 1) * count)
        return own_one + own_two + (back_one[rows].astype(f32) + back_two[rows].astype(f32))

    grad_normed_two = halves(grad_one, grad_two, 1)
    gain_two_grad = jnp.sum(grad_normed_two * normal_two, axis=0)
    grad_middle = grad_mlp.astype(f32) + norm_back(grad_normed_two, normal_two, inv_two, gain_two)

    grad_attended = dot_nt(grad_middle.astype(bf16), out_full).astype(bf16)
    if small_mesh:
        sum_two.first(grad_attended)
    far_query, far_kv_grad = far_backward(half, queries, qx, grad_attended, attended, lse, far_kv, rkx, group)
    got_kv = wires.other_half(far_kv_grad)
    if small_mesh:
        sum_one.third(far_query)
        far_query = after(far_query, sum_one.sent)
    result = (middle + halves(out_one, out_two, 0)).astype(bf16)
    query_grad, kv_grad = near_backward(
        queries, qx, grad_attended, attended, lse, cosines, sines, kv, kx, far_query, group
    )
    got_kv = after(got_kv, query_grad)
    if small_mesh:
        sum_two.second(query_grad)
        got_kv = after(got_kv, sum_two.sent)
        sum_one.fourth(sum_two.sent)
        query_grad = after(query_grad, (sum_one.sent, sum_two.sent))
    grad_input, mine, theirs, bias_grad, gain_one_grad = project_back(
        at, tokens, gain_one, normed, query_grad, kv_grad, got_kv, cosines, sines, qkv_full, grad_middle, attended
    )

    qk_own = (width + kv_width) // shards
    vector = jnp.concatenate(
        [
            gain_one_grad.reshape(shards, depth),
            gain_two_grad.reshape(shards, depth),
            bias_grad[0, : width + kv_width].reshape(shards, qk_own),
            bias_grad[0, width + kv_width :].reshape(shards, -1),
        ],
        axis=1,
    )
    vector = jnp.pad(vector, ((0, 0), (0, LANES - vector.shape[1] % LANES)))
    blocks = (qkv_width + width) // LANES
    cut = blocks // 4 * full_depth
    if small_mesh:
        vector = vector.reshape(4, 2, 2, -1, LANES)
        vector = vector[jnp.arange(4)[jnp.array(LINE)] ^ wires.line]
        vector = vector[:, jnp.arange(2) ^ wires.inner]
        vector = jnp.pad(vector, ((0, 0),) * 3 + ((0, 8 - vector.shape[3]), (0, 0)))
        vector = vector.transpose(2, 1, 0, 3, 4).astype(bf16)
        mine, theirs = (
            lax.dynamic_update_slice(array, pick(vector, c, 0)[:, None], (0, wires.seq, 0, 2 * cut, 0))
            for array, c in ((mine, wires.core), (theirs, 1 - wires.core))
        )
        sum_one.fifth(grad_input)
        sum_two.third(grad_input)
        mine, theirs = after((mine, theirs), (sum_one.sent, sum_two.sent))
        small = SmallSum(wires, mine, theirs, cut)
        small.first(())
        result = after(result, small.sent)
        small.second(())
        sum_two.fourth(small.sent)
        sum_one.sixth(small.sent)
        grad_input = after(grad_input, small.sent)
        small.third(sum_two.sent)
        small.fourth(())
        sum_two.fifth(small.sent)
        sum_two.sixth(())
        small.fifth(sum_two.sent)
        ends_one = sum_one.total(sum_two.sent)
        result = quarters_out(wires, result, small.sent)
        grad_input = quarters_out(wires, grad_input, small.sent)
        total = small.total(())
        vector = total[0, 2 * cut :]
        total = jnp.stack([total[:, :cut], total[:, cut : 2 * cut]], axis=0)
        total = total.reshape(blocks, depth, LANES)
    else:
        result, grad_input = quarters_out(wires, result), quarters_out(wires, grad_input)
        total = jnp.stack(ordered(wires.core, mine, theirs), axis=0)[:, :, :, jnp.array(LINE), : 2 * cut]
        total = total.reshape(2, 2, 2, 4, 2, blocks // 4, shards // groups, depth, LANES)
        total = total.transpose(3, 1, 0, 6, 4, 2, 5, 7, 8).reshape(shards, -1, LANES)
        vector = jnp.pad(vector.reshape(shards, -1, LANES), ((0, 0), (0, 6), (0, 0)))
        total = jnp.concatenate([total.astype(f32), vector], axis=1)
        total = lax.psum_scatter(total, "fsdp", scatter_dimension=0, tiled=True)[0]
        total = lax.psum(total.astype(bf16), "seq")
        vector = total[blocks * depth :]
        total = total[: blocks * depth].reshape(blocks, depth, LANES)
    vector = vector.reshape(-1).astype(f32)
    total = total.transpose(1, 0, 2).reshape(depth, -1).astype(f32)
    ends = [0, depth, 2 * depth, 2 * depth + qk_own, 2 * depth + own_bias]
    gain_one_grad, gain_two_grad, bias_qk, bias_v = (vector[a:b] for a, b in zip(ends, ends[1:]))

    half_rows = 6 * full_depth

    def natural(one, two):
        pieces = one.shape[0] // half_rows
        both = jnp.stack([one.reshape(pieces, half_rows, LANES), two.reshape(pieces, half_rows, LANES)], axis=1)
        both = both.reshape(pieces, 2 * half_rows, LANES)
        parts = []
        for start, size in ((0, full_depth), (4 * full_depth, full_depth), (8 * full_depth, full_own)):
            part = both[:, start : start + 4 * full_depth].reshape(pieces, -1, 2, size, LANES)
            parts.append(part.transpose(0, 2, 1, 3, 4).reshape(pieces, 2, -1, LANES))
        return jnp.concatenate(parts, axis=2)

    if small_mesh:
        finished = []
        for ends in (ends_one, sum_two.total(small.sent)):
            whole = natural(*ends)
            theirs = wires.flip(pick(whole, 1 - wires.core, 1), 1)
            first, second = ordered(wires.core, pick(whole, wires.core, 1), theirs)
            finished.append(jnp.stack([first, second], axis=1).reshape(-1, *first.shape[1:]))
        gate_grad, up_grad, down_grad = unpack_call(finished, tiles, shards, depth)
    else:
        many = shards // groups
        terms = []
        for keep_x, send_x, keep_y, send_y in (grads_one, grads_two):
            first = jnp.stack([keep_x, send_x], axis=0).reshape(2, 2, 4, -1, half_rows, LANES)
            second = jnp.stack([keep_y, send_y], axis=0).reshape(2, 2, 4, -1, half_rows, LANES)
            places = jnp.array(LINE)
            first = first.transpose(2, 0, 3, 1, 4, 5)[places].reshape(chips, -1, 2, half_rows, LANES)
            second = second.transpose(2, 1, 3, 0, 4, 5)[places].reshape(chips, -1, 2, half_rows, LANES)
            terms += [first, second]
        terms = jnp.concatenate(terms, axis=1).reshape(chips, steps, 2 * half_rows, LANES)
        parts = []
        for start, size in ((0, depth), (4 * full_depth, depth), (8 * full_depth, own)):
            part = terms[:, :, start : start + 4 * full_depth]
            part = part.reshape(chips, steps, -1, 2 * many, size, LANES)
            parts.append(part.transpose(0, 3, 1, 2, 4, 5).reshape(shards, steps, -1, LANES))
        terms = jnp.concatenate(parts, axis=2).astype(f32)
        terms = lax.dynamic_update_index_in_dim(jnp.zeros((2,) + terms.shape, f32), terms, wires.core, 0)
        terms = lax.psum_scatter(terms, "fsdp", scatter_dimension=1, tiled=True)[:, 0]
        terms = lax.psum(terms.astype(bf16), "seq")
        mlp_grads = terms.transpose(1, 0, 2, 3).reshape(2 * steps, -1, LANES)[:tiles]
        gate_grad, up_grad, down_grad = unpack_grads(mlp_grads, shards, depth)
    return (
        result[None],
        grad_input[None],
        gain_one_grad,
        total[:, :qkv_width],
        bias_qk,
        bias_v,
        total[:, qkv_width:],
        gain_two_grad,
        gate_grad.astype(f32),
        up_grad.astype(f32),
        down_grad.astype(f32),
    )


def solution(mesh):
    rows, split, lone = P("fsdp", "seq", None), P("fsdp", None), P("fsdp")
    in_specs = (rows, P("fsdp", "seq"), lone, split, lone, split, lone, split, split, split, rows)
    out_specs = (rows, rows, lone, split, lone, lone, split, lone, split, split, split)
    return jax.shard_map(
        functools.partial(per_device, mesh.shape["fsdp"]),
        mesh=mesh,
        in_specs=in_specs,
        out_specs=out_specs,
        check_vma=False,
    )
```

```python
import functools

import jax
import jax.numpy as jnp
from jax import lax
from jax.experimental import pallas as pl
from jax.experimental.pallas import tpu as pltpu
from jax.sharding import PartitionSpec as P

HEAD = 64
LANES = 128
TILE = 256
EPSILON = 1e-06
THETA = 1000000.0
FAR = -1e30
MIB = 2**20
EARLY = 10
SHARED = 2

LIGHT = pl.CostEstimate(flops=1, bytes_accessed=1, transcendentals=0)
MIDDLE = pl.CostEstimate(flops=8 * 10**9, bytes_accessed=MIB, transcendentals=0)
SHORT = pl.CostEstimate(flops=28 * 10**8, bytes_accessed=MIB, transcendentals=0)
HEAVY = pl.CostEstimate(flops=6 * 10**10, bytes_accessed=16 * MIB, transcendentals=0)

bf16 = jnp.bfloat16
f32 = jnp.float32


def dot_nn(left, right):
    return lax.dot_general(left, right, (((1,), (0,)), ((), ())), preferred_element_type=f32)


def dot_nt(left, right):
    return lax.dot_general(left, right, (((1,), (1,)), ((), ())), preferred_element_type=f32)


def dot_tn(left, right):
    return lax.dot_general(left, right, (((0,), (0,)), ((), ())), preferred_element_type=f32)


def swap_halves(values_in):
    lane = lax.broadcasted_iota(jnp.int32, values_in.shape, 1)
    ahead = pltpu.roll(values_in, LANES - HEAD // 2, 1)
    behind = pltpu.roll(values_in, HEAD // 2, 1)
    return jnp.where(lane % HEAD < HEAD // 2, ahead, behind)


def turn(values_in, cosines, sines):
    return values_in * cosines + swap_halves(values_in) * sines


def turn_back(grads_in, cosines, sines):
    return grads_in * cosines - swap_halves(grads_in) * sines


def project_kernel(x_ref, gain_ref, w_ref, bias_ref, cos_ref, sin_ref, normed_ref, q_ref, kv_ref):
    x = x_ref[...].astype(f32)
    scale = lax.rsqrt(jnp.mean(x * x, axis=1, keepdims=True) + EPSILON)
    normed = (x * scale * gain_ref[...]).astype(bf16)
    normed_ref[...] = normed
    project = dot_nn(normed, w_ref[...]) + bias_ref[...]
    cosines, sines = cos_ref[...], sin_ref[...]
    width = q_ref.shape[1]
    for start in range(0, width, LANES):
        part = slice(start, start + LANES)
        q_ref[:, part] = turn(project[:, part], cosines, sines).astype(bf16) * (HEAD**-0.5)
    kv_ref[:, :LANES] = turn(project[:, width : width + LANES], cosines, sines).astype(bf16)
    kv_ref[:, LANES:] = project[:, width + LANES :].astype(bf16)


def project_call(x, gain, weight, bias, cosines, sines):
    tokens, width = x.shape
    outs = weight.shape[1]
    rows = tokens // 3
    row = lambda cols: pl.BlockSpec((rows, cols), lambda i: (i, 0))
    whole = lambda *shape: pl.BlockSpec(shape, lambda i: (0, 0))
    return pl.pallas_call(
        project_kernel,
        grid=(3,),
        in_specs=[
            row(width),
            whole(1, width),
            whole(width, outs),
            whole(1, outs),
            row(LANES),
            row(LANES),
        ],
        out_specs=[row(width), row(width), row(2 * LANES)],
        out_shape=[
            jax.ShapeDtypeStruct((tokens, width), bf16),
            jax.ShapeDtypeStruct((tokens, width), bf16),
            jax.ShapeDtypeStruct((tokens, 2 * LANES), bf16),
        ],
        compiler_params=pltpu.CompilerParams(vmem_limit_bytes=62 * MIB),
        cost_estimate=LIGHT,
        name="project",
    )(x, gain, weight, bias, cosines, sines)


def dropping(kernel, start, count):
    def inner(*refs, **settings):
        kernel(*refs[:start], *refs[start + count :], **settings)

    return inner


def spread(ref, columns, out_ref, turned_ref=None):
    both = ref[:, columns].astype(f32)
    shifted = pltpu.roll(both, HEAD, 1)
    low = lax.broadcasted_iota(jnp.int32, both.shape, 1) < HEAD
    for head in range(2):
        for parity in range(2):
            source = both if head == parity else shifted
            alone = jnp.where(low if parity == 0 else ~low, source, 0.0)
            out_ref[head, parity] = alone.astype(bf16)
            if turned_ref is not None:
                turned_ref[head, parity] = alone.T.astype(bf16)


def causal(scores, flipped):
    row_at = lax.broadcasted_iota(jnp.int32, scores.shape, 0)
    col_at = lax.broadcasted_iota(jnp.int32, scores.shape, 1)
    return jnp.where(row_at <= col_at if flipped else col_at <= row_at, scores, FAR)


def near_forward_kernel(q_ref, qx_ref, kv_ref, kx_ref, o_ref, lse_ref, k_s, v_s, *, group):
    step = pl.program_id(0)
    block = q_ref.shape[0] // 2
    lane = lax.broadcasted_iota(jnp.int32, (block, LANES), 1)

    @pl.when(step == 0)
    def _():
        spread(kv_ref, slice(0, LANES), k_s)
        spread(kv_ref, slice(LANES, 2 * LANES), v_s)
        lse_ref[...] = jnp.zeros_like(lse_ref)

    for b in range(2):
        rows = slice(b * block, (b + 1) * block)
        q = jnp.concatenate([q_ref[rows], qx_ref[rows]], axis=1)
        total = None
        stats = lse_ref[rows]
        for parity in range(2):
            kv = (2 * step + parity) // group
            k_at = lambda rows: jnp.concatenate([k_s[kv, parity, rows], kx_ref[rows]], axis=1)
            pieces = [(causal(dot_nt(q, k_at(rows)), False), v_s[kv, parity, rows])]
            if b:
                first = slice(0, block)
                pieces.append((dot_nt(q, k_at(first)), v_s[kv, parity, first]))
            top = functools.reduce(jnp.maximum, [jnp.max(s, axis=1, keepdims=True) for s, _ in pieces])
            weights = [(jnp.exp(s - top), v) for s, v in pieces]
            norm = sum(jnp.sum(p, axis=1, keepdims=True) for p, _ in weights)
            out = sum(dot_nn(p.astype(bf16), v) for p, v in weights) * (1.0 / norm)
            total = out if total is None else total + out
            stats = jnp.where(lane == 2 * step + parity, top + jnp.log(norm), stats)
        o_ref[rows] = total
        lse_ref[rows] = stats


def far_forward_kernel(half_ref, q_ref, qx_ref, kv_ref, kx_ref, near_ref, stats_ref, o_ref, lse_ref, k_s, v_s, lse_s, *, group):
    step = pl.program_id(0)
    tokens = q_ref.shape[0]
    block = tokens // 2

    @pl.when(step == 0)
    def _():
        spread(kv_ref, slice(0, LANES), k_s)
        spread(kv_ref, slice(LANES, 2 * LANES), v_s)
        lse_s[...] = stats_ref[...]

    def run(blocks, keys):
        for b in blocks:
            rows = slice(b * block, (b + 1) * block)
            q = jnp.concatenate([q_ref[rows], qx_ref[rows]], axis=1)
            lane = lax.broadcasted_iota(jnp.int32, (block, LANES), 1)
            stats = lse_s[rows]
            total = None
            scale = None
            for parity in range(2):
                head = 2 * step + parity
                kv = head // group
                k = jnp.concatenate([k_s[kv, parity, keys], kx_ref[keys]], axis=1)
                s = dot_nt(q, k)
                top = jnp.max(s, axis=1, keepdims=True)
                p = jnp.exp(s - top)
                norm = jnp.sum(p, axis=1, keepdims=True)
                far = top + jnp.log(norm)
                near = jnp.sum(jnp.where(lane == head, stats, 0.0), axis=1, keepdims=True)
                both = jnp.maximum(near, far)
                both = both + jnp.log(jnp.exp(near - both) + jnp.exp(far - both))
                out = dot_nn(p.astype(bf16), v_s[kv, parity, keys]) * jnp.exp(top - both)
                total = out if total is None else total + out
                weight = jnp.exp(near - both)
                scale = weight if scale is None else jnp.where(lane < HEAD, scale, weight)
                stats = jnp.where(lane == head, both, stats)
            o_ref[rows] = (near_ref[rows] * scale + total).astype(bf16)
            lse_s[rows] = stats

    @pl.when(half_ref[0] == 0)
    def _():
        first = slice(0, block)
        o_ref[first] = near_ref[first].astype(bf16)
        run((1,), slice(0, tokens))

    @pl.when(half_ref[0] != 0)
    def _():
        run((0, 1), slice(0, block))

    @pl.when(step == pl.num_programs(0) - 1)
    def _():
        lse_ref[...] = lse_s[...].T


def near_forward(q, qx, kv, kx, group):
    tokens, width = q.shape
    column = pl.BlockSpec((tokens, LANES), lambda p: (0, p))
    whole = lambda *shape: pl.BlockSpec(shape, lambda p: (0, 0))
    spare = lambda: pltpu.VMEM((2, 2, tokens, LANES), bf16)
    return pl.pallas_call(
        functools.partial(near_forward_kernel, group=group),
        grid=(width // LANES,),
        in_specs=[column, whole(tokens, LANES), whole(tokens, 2 * LANES), whole(tokens, LANES)],
        out_specs=[column, whole(tokens, LANES)],
        scratch_shapes=[spare(), spare()],
        out_shape=[
            jax.ShapeDtypeStruct((tokens, width), f32),
            jax.ShapeDtypeStruct((tokens, LANES), f32),
        ],
        compiler_params=pltpu.CompilerParams(vmem_limit_bytes=62 * MIB),
        cost_estimate=HEAVY,
        name="attention_near",
    )(q, qx, kv, kx)


def far_forward(half, q, qx, kv, kx, near, stats, group):
    tokens, width = q.shape
    column = pl.BlockSpec((tokens, LANES), lambda p, *_: (0, p))
    whole = lambda *shape: pl.BlockSpec(shape, lambda p, *_: (0, 0))
    spare = lambda: pltpu.VMEM((2, 2, tokens, LANES), bf16)
    return pl.pallas_call(
        functools.partial(far_forward_kernel, group=group),
        grid_spec=pltpu.PrefetchScalarGridSpec(
            num_scalar_prefetch=1,
            grid=(width // LANES,),
            in_specs=[
                column,
                whole(tokens, LANES),
                whole(tokens, 2 * LANES),
                whole(tokens, LANES),
                column,
                whole(tokens, LANES),
            ],
            out_specs=[column, whole(LANES, tokens)],
            scratch_shapes=[spare(), spare(), pltpu.VMEM((tokens, LANES), f32)],
        ),
        out_shape=[
            jax.ShapeDtypeStruct((tokens, width), bf16),
            jax.ShapeDtypeStruct((LANES, tokens), f32),
        ],
        compiler_params=pltpu.CompilerParams(vmem_limit_bytes=62 * MIB),
        cost_estimate=LIGHT,
        name="attention_far",
    )(half, q, qx, kv, kx, near, stats)


def back_block(q, q_wide, g, lse, delta, k, kx, turned, v, masked):
    s = dot_nt(jnp.concatenate([k, kx], axis=1), q_wide)
    if masked:
        s = causal(s, True)
    p = jnp.exp(s - lse)
    ds = (p * (dot_nt(v, g) - delta)).astype(bf16)
    return dot_nn(p.astype(bf16), g), dot_nn(ds, q), dot_nn(turned, ds)


def gather_heads(acc, out_ref, columns):
    low = lax.broadcasted_iota(jnp.int32, acc.shape[2:], 1) < HEAD
    first = acc[0, 0] + pltpu.roll(acc[0, 1], HEAD, 1)
    second = acc[1, 1] + pltpu.roll(acc[1, 0], HEAD, 1)
    out_ref[:, columns] = jnp.where(low, first, second).astype(out_ref.dtype)


def far_backward_kernel(half_ref, q_ref, qx_ref, g_ref, o_ref, lse_ref, kv_ref, kx_ref, dq_ref, dkv_ref, k_s, t_s, v_s, ka, va, *, group):
    step = pl.program_id(0)
    tokens = q_ref.shape[0]
    block = tokens // 2
    keys, values = slice(0, LANES), slice(LANES, 2 * LANES)

    @pl.when(step == 0)
    def _():
        spread(kv_ref, keys, k_s, t_s)
        spread(kv_ref, values, v_s)
        ka[...] = jnp.zeros_like(ka)
        va[...] = jnp.zeros_like(va)

    def run(blocks, key_blocks):
        for b in blocks:
            rows = slice(b * block, (b + 1) * block)
            q = q_ref[rows]
            q_wide = jnp.concatenate([q, qx_ref[rows]], axis=1)
            g = g_ref[rows]
            product = (g.astype(f32) * o_ref[rows].astype(f32)).T
            total = None
            for parity in range(2):
                head = 2 * step + parity
                kv = head // group
                lse = lse_ref[pl.ds(head, 1), rows]
                delta = jnp.sum(product[parity * HEAD : (parity + 1) * HEAD], axis=0, keepdims=True)
                for c in key_blocks:
                    part = slice(c * block, (c + 1) * block)
                    dv, dk, dq = back_block(
                        q, q_wide, g, lse, delta, k_s[kv, parity, part], kx_ref[part],
                        t_s[kv, parity, :, part], v_s[kv, parity, part], False,
                    )
                    va[kv, parity, part] += dv
                    ka[kv, parity, part] += dk
                    total = dq if total is None else total + dq
            dq_ref[:, rows] = total

    @pl.when(half_ref[0] == 0)
    def _():
        dq_ref[:, :block] = jnp.zeros((LANES, block), f32)
        run((1,), (0, 1))

    @pl.when(half_ref[0] != 0)
    def _():
        run((0, 1), (0,))

    @pl.when(step == pl.num_programs(0) - 1)
    def _():
        gather_heads(ka, dkv_ref, keys)
        gather_heads(va, dkv_ref, values)


def near_backward_kernel(q_ref, qx_ref, g_ref, o_ref, lse_ref, cos_ref, sin_ref, kv_ref, kx_ref, far_ref, dq_ref, dkv_ref, k_s, t_s, v_s, ka, va, *, group):
    step = pl.program_id(0)
    tokens = q_ref.shape[0]
    block = tokens // 2
    keys, values = slice(0, LANES), slice(LANES, 2 * LANES)

    @pl.when(step == 0)
    def _():
        spread(kv_ref, keys, k_s, t_s)
        spread(kv_ref, values, v_s)
        ka[...] = jnp.zeros_like(ka)
        va[...] = jnp.zeros_like(va)

    for b in range(2):
        rows = slice(b * block, (b + 1) * block)
        q = q_ref[rows]
        q_wide = jnp.concatenate([q, qx_ref[rows]], axis=1)
        g = g_ref[rows]
        product = (g.astype(f32) * o_ref[rows].astype(f32)).T
        total = far_ref[:, rows]
        for parity in range(2):
            head = 2 * step + parity
            kv = head // group
            lse = lse_ref[pl.ds(head, 1), rows]
            delta = jnp.sum(product[parity * HEAD : (parity + 1) * HEAD], axis=0, keepdims=True)
            for c in range(b + 1):
                part = slice(c * block, (c + 1) * block)
                dv, dk, dq = back_block(
                    q, q_wide, g, lse, delta, k_s[kv, parity, part], kx_ref[part],
                    t_s[kv, parity, :, part], v_s[kv, parity, part], c == b,
                )
                va[kv, parity, part] += dv
                ka[kv, parity, part] += dk
                total = total + dq
        dq_ref[rows] = turn_back(total.T * (HEAD**-0.5), cos_ref[rows], sin_ref[rows]).astype(bf16)

    @pl.when(step == pl.num_programs(0) - 1)
    def _():
        gather_heads(ka, dkv_ref, keys)
        gather_heads(va, dkv_ref, values)


ANYWHERE = pl.BlockSpec(memory_space=pl.ANY)


def alike(arrays):
    return [jax.ShapeDtypeStruct(array.shape, array.dtype) for array in arrays]


def backward_scratch(tokens):
    return [
        pltpu.VMEM((2, 2, tokens, LANES), bf16),
        pltpu.VMEM((2, 2, LANES, tokens), bf16),
        pltpu.VMEM((2, 2, tokens, LANES), bf16),
        pltpu.VMEM((2, 2, tokens, LANES), f32),
        pltpu.VMEM((2, 2, tokens, LANES), f32),
    ]


def far_backward(half, q, qx, g, o, lse, kv, kx, group, through):
    tokens, width = q.shape
    column = pl.BlockSpec((tokens, LANES), lambda p, *_: (0, p))
    across = pl.BlockSpec((LANES, tokens), lambda p, *_: (p, 0))
    whole = lambda *shape: pl.BlockSpec(shape, lambda p, *_: (0, 0))
    return pl.pallas_call(
        functools.partial(dropping(dropping(far_backward_kernel, 10, len(through)), 8, len(through)), group=group),
        grid_spec=pltpu.PrefetchScalarGridSpec(
            num_scalar_prefetch=1,
            grid=(width // LANES,),
            in_specs=[
                column,
                whole(tokens, LANES),
                column,
                column,
                whole(LANES, tokens),
                whole(tokens, 2 * LANES),
                whole(tokens, LANES),
            ]
            + [ANYWHERE] * len(through),
            out_specs=[across, whole(tokens, 2 * LANES)] + [ANYWHERE] * len(through),
            scratch_shapes=backward_scratch(tokens),
        ),
        out_shape=[
            jax.ShapeDtypeStruct((width, tokens), f32),
            jax.ShapeDtypeStruct((tokens, 2 * LANES), bf16),
            *alike(through),
        ],
        input_output_aliases={8 + i: 2 + i for i in range(len(through))},
        compiler_params=pltpu.CompilerParams(vmem_limit_bytes=62 * MIB),
        cost_estimate=LIGHT,
        name="attention_far_back",
    )(half, q, qx, g, o, lse, kv, kx, *through)


def near_backward(q, qx, g, o, lse, cosines, sines, kv, kx, far, group, others):
    tokens, width = q.shape
    column = pl.BlockSpec((tokens, LANES), lambda p: (0, p))
    across = pl.BlockSpec((LANES, tokens), lambda p: (p, 0))
    whole = lambda *shape: pl.BlockSpec(shape, lambda p: (0, 0))
    return pl.pallas_call(
        functools.partial(dropping(near_backward_kernel, 10, len(others)), group=group),
        grid=(width // LANES,),
        in_specs=[
            column,
            whole(tokens, LANES),
            column,
            column,
            whole(LANES, tokens),
            whole(tokens, LANES),
            whole(tokens, LANES),
            whole(tokens, 2 * LANES),
            whole(tokens, LANES),
            across,
        ]
        + [ANYWHERE] * len(others),
        out_specs=[column, whole(tokens, 2 * LANES)],
        scratch_shapes=backward_scratch(tokens),
        out_shape=[
            jax.ShapeDtypeStruct((tokens, width), bf16),
            jax.ShapeDtypeStruct((tokens, 2 * LANES), f32),
        ],
        compiler_params=pltpu.CompilerParams(vmem_limit_bytes=62 * MIB),
        cost_estimate=LIGHT,
        name="attention_near_back",
    )(q, qx, g, o, lse, cosines, sines, kv, kx, far, *others)


def weight_grads_kernel(at_ref, normed_ref, dq_ref, dkv_ref, got_ref, cos_ref, sin_ref, branch_ref, att_ref, project_ref, mine_ref, theirs_ref, bias_ref):
    kv = dkv_ref[...] + got_ref[...].astype(f32)
    keys = turn_back(kv[:, :LANES], cos_ref[...], sin_ref[...])
    project = jnp.concatenate([dq_ref[...], keys.astype(bf16), kv[:, LANES:].astype(bf16)], axis=1)
    project_ref[...] = project
    bias = jnp.sum(project.astype(f32), axis=0, keepdims=True)
    bias_ref[...] = bias
    core, inner, line, seq = (at_ref[i] for i in range(4))
    width = normed_ref.shape[1]
    chips = 8
    piece = width // chips // 2
    normed_t, att_t = normed_ref[...].T, att_ref[...].T
    columns = [(normed_t, project[:, s : s + LANES]) for s in range(0, project.shape[1], LANES)]
    columns += [(att_t, branch_ref[:, s : s + LANES]) for s in range(0, width, LANES)]
    for pair in range(len(columns) // 2):
        (left, one), (other, two) = columns[2 * pair : 2 * pair + 2]
        if left is other:
            value = dot_nn(left, jnp.concatenate([one, two], axis=1))
            one, two = value[:, :LANES], value[:, LANES:]
        else:
            one, two = dot_nn(left, one), dot_nn(other, two)
        quarter = pair // 2
        half = (quarter % 2) ^ seq
        start = quarter // 2 * (4 * piece + 16) + pair % 2 * 2 * piece
        for chip in range(chips):
            rows = slice(chip * 2 * piece, (chip + 1) * 2 * piece)
            here, there = one[rows], two[rows]
            low = jnp.concatenate([here[:piece], there[:piece]], axis=0)
            high = jnp.concatenate([here[piece:], there[piece:]], axis=0)
            away = (chip // 2) ^ line
            place = 2 * (away % 2) + away // 2
            for ref, first in ((mine_ref, core == 0), (theirs_ref, core != 0)):
                value = jnp.where(first, low, high).astype(bf16)
                ref[(chip % 2) ^ inner, half, place, start : start + 2 * piece, :] = value
    row = lax.broadcasted_iota(jnp.int32, (16, LANES), 0)
    last = bias[:, project.shape[1] - LANES :]
    for chip in range(chips):
        away = (chip // 2) ^ line
        place = 2 * (away % 2) + away // 2
        first = bias[:, chip * LANES : (chip + 1) * LANES]
        value = jnp.where(row == 0, first, jnp.where(row == 1, last, 0.0)).astype(bf16)
        for ref in (mine_ref, theirs_ref):
            for half in range(2):
                ref[(chip % 2) ^ inner, half, place, 4 * piece : 4 * piece + 16, :] = value
                ref[(chip % 2) ^ inner, half, place, 8 * piece + 16 :, :] = value


def weight_grads(at, normed, dq, dkv, got, cosines, sines, branch, attended, outs, others):
    tokens, width = normed.shape
    rows = (outs + width) // LANES * (width // 16) // 2 + 32
    packed = jax.ShapeDtypeStruct((2, 2, 4, rows, LANES), bf16)
    out_shape = [
        jax.ShapeDtypeStruct((tokens, outs), bf16),
        packed,
        packed,
        jax.ShapeDtypeStruct((1, outs), f32),
    ]
    args = (normed, dq, dkv, got, cosines, sines, branch, attended)
    whole = lambda array: pl.BlockSpec(array.shape, lambda i, *_: (0,) * len(array.shape))
    return pl.pallas_call(
        dropping(weight_grads_kernel, 9, len(others)),
        grid_spec=pltpu.PrefetchScalarGridSpec(
            num_scalar_prefetch=1,
            grid=(1,),
            in_specs=[whole(array) for array in args] + [ANYWHERE] * len(others),
            out_specs=[whole(array) for array in out_shape],
        ),
        out_shape=out_shape,
        compiler_params=pltpu.CompilerParams(vmem_limit_bytes=62 * MIB),
        cost_estimate=LIGHT,
        name="weight_grads",
    )(at, *args, *others)


def store_half(value, kept_ref, sent_ref):
    for step, ref in enumerate((kept_ref, sent_ref)):

        @pl.when(pl.program_id(0) == step)
        def _(ref=ref):
            ref[...] = value


def input_grad_kernel(at_ref, x_ref, gain_ref, project_ref, w_ref, gm_ref, kept_ref, sent_ref):
    grad = dot_nt(project_ref[...], w_ref[...]) * gain_ref[...]
    x = x_ref[...].astype(f32)
    scale = lax.rsqrt(jnp.mean(x * x, axis=1, keepdims=True) + EPSILON)
    normal = x * scale
    mean = jnp.mean(grad * normal, axis=1, keepdims=True)
    store_half((gm_ref[...] + scale * (grad - normal * mean)).astype(bf16), kept_ref, sent_ref)


def input_grad(half, x, gain, project, weight, grad_middle, others):
    tokens, width = x.shape
    outs = weight.shape[1]
    rows = tokens // 2
    row = lambda cols: pl.BlockSpec((rows, cols), lambda i, half: (i ^ half[0], 0))
    whole = lambda *shape: pl.BlockSpec(shape, lambda i, half: (0, 0))
    return pl.pallas_call(
        dropping(input_grad_kernel, 6, len(others)),
        grid_spec=pltpu.PrefetchScalarGridSpec(
            num_scalar_prefetch=1,
            grid=(2,),
            in_specs=[row(width), whole(1, width), row(outs), whole(width, outs), row(width)]
            + [ANYWHERE] * len(others),
            out_specs=[whole(rows, width)] * 2,
        ),
        out_shape=[jax.ShapeDtypeStruct((rows, width), bf16)] * 2,
        compiler_params=pltpu.CompilerParams(vmem_limit_bytes=62 * MIB),
        cost_estimate=LIGHT,
        name="input_grad",
    )(half, x, gain, project, weight, grad_middle, *others)


def out_project_kernel(x_ref, att_ref, gain_ref, w_ref, middle_ref, normed_ref, out_ref, raw_s, w_s, sem, *, start):
    step = pl.program_id(0)

    @pl.when(step == 0)
    def _():
        if start is None:
            w_s[...] = w_ref[...]
        else:
            copy = pltpu.make_async_copy(w_ref.at[:, pl.ds(start, raw_s.shape[1]), :], raw_s, sem)
            copy.start()
            copy.wait()
            width = w_s.shape[0]
            depth = width // raw_s.shape[0]
            for c in range(width // LANES):
                rows = raw_s[:, c * depth : (c + 1) * depth, :].astype(f32)
                w_s[:, c * LANES : (c + 1) * LANES] = rows.reshape(width, LANES).astype(bf16)
        out_ref[...] = w_s[...]

    middle = x_ref[...].astype(f32) + dot_nn(att_ref[...], w_s[...])
    middle_ref[...] = middle
    scale = lax.rsqrt(jnp.mean(middle * middle, axis=1, keepdims=True) + EPSILON)
    normed_ref[...] = (middle * scale * gain_ref[...]).astype(bf16)


def out_project(x, attended, gain, weight, start, rows):
    tokens, width = x.shape
    part = tokens // 3
    row = pl.BlockSpec((part, width), lambda i: (i, 0))
    whole = lambda *shape: pl.BlockSpec(shape, lambda i: (0, 0))
    raw = start is not None
    return pl.pallas_call(
        functools.partial(out_project_kernel, start=start),
        grid=(3,),
        in_specs=[
            row,
            row,
            whole(1, width),
            pl.BlockSpec(memory_space=pl.ANY) if raw else whole(width, width),
        ],
        out_specs=[row, row, whole(width, width)],
        out_shape=[
            jax.ShapeDtypeStruct((tokens, width), f32),
            jax.ShapeDtypeStruct((tokens, width), bf16),
            jax.ShapeDtypeStruct((width, width), bf16),
        ],
        scratch_shapes=[
            pltpu.VMEM((weight.shape[0], rows, LANES) if raw else (8, LANES), bf16),
            pltpu.VMEM((width, width), bf16),
            pltpu.SemaphoreType.DMA,
        ],
        compiler_params=pltpu.CompilerParams(vmem_limit_bytes=62 * MIB),
        cost_estimate=LIGHT,
        name="out_project",
    )(x, attended, gain, weight)


def middle_back_kernel(at_ref, o1_ref, o2_ref, o3_ref, o4_ref, g1_ref, g2_ref, g3_ref, g4_ref, middle_ref, gout_ref, gain_ref, w_ref, kept_ref, sent_ref, gm_ref, branch_ref, gatt_ref):
    middle = middle_ref[...]
    added = sum(ref[...].astype(f32) for ref in (o1_ref, o2_ref, o3_ref, o4_ref))
    store_half((middle + added).astype(bf16), kept_ref, sent_ref)
    grad = sum(ref[...].astype(f32) for ref in (g1_ref, g2_ref, g3_ref, g4_ref))
    grad = grad * gain_ref[...]
    scale = lax.rsqrt(jnp.mean(middle * middle, axis=1, keepdims=True) + EPSILON)
    normal = middle * scale
    mean = jnp.mean(grad * normal, axis=1, keepdims=True)
    grad = gout_ref[...].astype(f32) + scale * (grad - normal * mean)
    gm_ref[...] = grad
    branch = grad.astype(bf16)
    branch_ref[...] = branch
    gatt_ref[...] = dot_nt(branch, w_ref[...]).astype(bf16)


def middle_back(half, terms, middle, grad_out, gain, weight, others, through):
    tokens, width = middle.shape
    rows = tokens // 2
    row = pl.BlockSpec((rows, width), lambda i, half: (i ^ half[0], 0))
    below = pl.BlockSpec((rows, width), lambda i, half: (2 + (i ^ half[0]), 0))
    whole = lambda *shape: pl.BlockSpec(shape, lambda i, half: (0, 0))
    shape = lambda kind: jax.ShapeDtypeStruct((tokens, width), kind)
    return pl.pallas_call(
        dropping(dropping(middle_back_kernel, 18, len(through)), 13, len(others) + len(through)),
        grid_spec=pltpu.PrefetchScalarGridSpec(
            num_scalar_prefetch=1,
            grid=(2,),
            in_specs=[row] * 4
            + [below] * 4
            + [row, row, whole(1, width), whole(width, width)]
            + [ANYWHERE] * (len(others) + len(through)),
            out_specs=[whole(rows, width)] * 2 + [row] * 3 + [ANYWHERE] * len(through),
        ),
        out_shape=[jax.ShapeDtypeStruct((rows, width), bf16)] * 2 + [shape(f32), shape(bf16), shape(bf16)] + alike(through),
        input_output_aliases={13 + len(others) + i: 5 + i for i in range(len(through))},
        compiler_params=pltpu.CompilerParams(vmem_limit_bytes=62 * MIB),
        cost_estimate=LIGHT,
        name="middle_back",
    )(half, *terms, *terms, middle, grad_out, gain, weight, *others, *through)


LINE = (0, 2, 1, 3)


def mlp_kernel(at_ref, near_ref, far_ref, gnear_ref, gfar_ref, *rest, counts, tiles, first, split):
    w_refs, rest = rest[: len(counts)], rest[len(counts) :]
    own_ref, other_ref, keep_x, send_x, keep_y, send_y = rest[:6]
    n_s, t_s, g_s, p_s, out_s, grad_s, gate_s, up_s, down_s = rest[6:]
    step = pl.program_id(0)
    tile = 2 * (first + step) + at_ref[0]
    tokens, width = near_ref.shape
    shards = w_refs[0].shape[0]
    depth = width // shards
    own = TILE // shards
    chips = shards // 2

    @pl.when(step == 0)
    def _():
        n_s[:tokens] = near_ref[...]
        n_s[tokens:] = far_ref[...]
        g_s[:tokens] = gnear_ref[...]
        g_s[tokens:] = gfar_ref[...]
        t_s[:, :tokens] = near_ref[...].T
        t_s[:, tokens:] = far_ref[...].T
        out_s[...] = jnp.zeros_like(out_s)
        grad_s[...] = jnp.zeros_like(grad_s)

    def load(w_ref):
        for at, square in ((0, gate_s), (2 * depth, up_s)):
            for c in range(TILE // LANES):
                rows = w_ref[:, at + c * depth : at + (c + 1) * depth, :]
                rows = rows.astype(f32).reshape(width, LANES).astype(bf16)
                square[:, c * LANES : (c + 1) * LANES] = rows
        for c in range(width // LANES):
            rows = w_ref[:, 4 * depth + c * own : 4 * depth + (c + 1) * own, :]
            down_s[:, c * LANES : (c + 1) * LANES] = rows.reshape(TILE, LANES)

    begin = 0
    for w_ref, many in zip(w_refs, counts):
        pl.when((step >= begin) & (step < begin + many))(functools.partial(load, w_ref))
        begin += many

    @pl.when(tile >= tiles)
    def _():
        p_s[...] = jnp.zeros_like(p_s)

    @pl.when(tile < tiles)
    def _():
        gate_w, up_w, down_w = gate_s[...], up_s[...], down_s[...]
        n = n_s[...]
        g = g_s[...]
        gate = dot_nn(n, gate_w)
        up = dot_nn(n, up_w)
        grad_hidden = dot_nt(g, down_w)
        sig = 1.0 / (1.0 + jnp.exp(-gate))
        silu = gate * sig
        hidden = (silu * up).astype(bf16)
        grad_gate = (grad_hidden * up * (sig + silu * (1.0 - sig))).astype(bf16)
        grad_up = (grad_hidden * silu).astype(bf16)
        out_s[...] += dot_nn(hidden, down_w)
        grad_s[...] += dot_nt(grad_gate, gate_w) + dot_nt(grad_up, up_w)
        for at, value in ((0, dot_nn(t_s[...], grad_gate)), (1, dot_nn(t_s[...], grad_up))):
            for c in range(TILE // LANES):
                part = value[:, c * LANES : (c + 1) * LANES].astype(bf16)
                start = (2 * at + c) * 2 * depth
                p_s[:, start : start + 2 * depth, :] = part.reshape(chips, 2 * depth, LANES)
        down = dot_tn(hidden, g)
        for c in range(width // LANES):
            part = down[:, c * LANES : (c + 1) * LANES].astype(bf16)
            start = 8 * depth + c * 2 * own
            p_s[:, start : start + 2 * own, :] = part.reshape(chips, 2 * own, LANES)

    half_rows = 6 * depth
    inner, line, seq = at_ref[1], at_ref[2], at_ref[3]

    def piece(line_off, inner_off, half_off):
        chip = 2 * (line ^ line_off) + (inner ^ inner_off)
        start = pl.multiple_of((seq ^ half_off) * half_rows, half_rows)
        return p_s[chip, pl.ds(start, half_rows), :]

    @pl.when(step < split)
    def _():
        for a, off in enumerate(LINE):
            for h in range(2):
                keep_x[h, a] = piece(off, 0, h)
                send_x[h, a] = piece(off, 1, h)

    @pl.when(step >= split)
    def _():
        for a, off in enumerate(LINE):
            for b in range(2):
                keep_y[b, a] = piece(off, b, 0)
                send_y[b, a] = piece(off, b, 1)

    @pl.when(step == pl.num_programs(0) - 1)
    def _():
        for ref, rows in ((own_ref, slice(0, tokens)), (other_ref, slice(tokens, 2 * tokens))):
            ref[:tokens] = out_s[rows].astype(bf16)
            ref[tokens:] = grad_s[rows].astype(bf16)


def mlp_call(at, near, far, gnear, gfar, weights, counts, tiles, first, split):
    tokens, width = near.shape
    shards = weights[0][0].shape[0]
    rows = 6 * width // shards
    count = sum(counts)
    whole = lambda *shape: pl.BlockSpec(shape, lambda j, *_: (0,) * len(shape))
    early = pl.BlockSpec((2, 4, rows, LANES), lambda j, *_: (0, 0, jnp.minimum(j, split - 1), 0))
    late = pl.BlockSpec((2, 4, rows, LANES), lambda j, *_: (0, 0, jnp.maximum(j - split, 0), 0))
    shape_x = jax.ShapeDtypeStruct((2, 4, rows * split, LANES), bf16)
    shape_y = jax.ShapeDtypeStruct((2, 4, rows * (count - split), LANES), bf16)
    wide = jax.ShapeDtypeStruct((2 * tokens, width), bf16)

    def block_of(index):
        return pl.BlockSpec((shards, rows, LANES), lambda j, at: (0, index(j, at), 0))

    return pl.pallas_call(
        functools.partial(mlp_kernel, counts=counts, tiles=tiles, first=first, split=split),
        grid_spec=pltpu.PrefetchScalarGridSpec(
            num_scalar_prefetch=1,
            grid=(count,),
            in_specs=[whole(tokens, width)] * 4 + [block_of(index) for _, index in weights],
            out_specs=[whole(2 * tokens, width)] * 2 + [early, early, late, late],
            scratch_shapes=[
                pltpu.VMEM((2 * tokens, width), bf16),
                pltpu.VMEM((width, 2 * tokens), bf16),
                pltpu.VMEM((2 * tokens, width), bf16),
                pltpu.VMEM((shards // 2, 2 * rows, LANES), bf16),
                pltpu.VMEM((2 * tokens, width), f32),
                pltpu.VMEM((2 * tokens, width), f32),
                pltpu.VMEM((width, TILE), bf16),
                pltpu.VMEM((width, TILE), bf16),
                pltpu.VMEM((TILE, width), bf16),
            ],
        ),
        out_shape=[
            wide,
            wide,
            shape_x,
            shape_x,
            shape_y,
            shape_y,
        ],
        compiler_params=pltpu.CompilerParams(vmem_limit_bytes=62 * MIB),
        cost_estimate=HEAVY,
        name="feed_forward",
    )(at, near, far, gnear, gfar, *(w for w, _ in weights))


def pack_kernel(half_ref, gate_ref, up_ref, down_ref, out_ref, one_ref, two_ref, *, shards, early, shared):
    depth, hidden = gate_ref.shape
    width = down_ref.shape[1]
    tiles = hidden // TILE
    own = TILE // shards
    rows = 6 * depth
    per = LANES // own
    lane = lax.broadcasted_iota(jnp.int32, (depth, LANES), 1) // own

    def write(target, at, blocks, tile):
        target[at : at + 4 * depth, :] = blocks
        for c in range(width // LANES):
            start = at + 4 * depth + c * own
            target[start : start + own, :] = down_ref[tile * own : (tile + 1) * own, c * LANES : (c + 1) * LANES]

    for tile in range(tiles):
        blocks = []
        for ref in (gate_ref, up_ref):
            for c in range(TILE // LANES):
                total = None
                by_shift = {}
                for i in range(per):
                    at = ((c * per + i) * tiles + tile) * own
                    by_shift.setdefault((i - at // own) % per, []).append((i, at // LANES))
                for shift, sources in by_shift.items():
                    value = None
                    for i, block in sources:
                        part = ref[:, block * LANES : (block + 1) * LANES].astype(f32)
                        here = lane == (i - shift) % per
                        value = part if value is None else jnp.where(here, part, value)
                    if shift:
                        value = pltpu.roll(value, shift * own, 1)
                    if total is None:
                        total = value
                    else:
                        for i, _ in sources:
                            total = jnp.where(lane == i, value, total)
                blocks.append(total)
        blocks = jnp.concatenate(blocks, axis=0).astype(bf16)
        if tile < early:
            write(one_ref, tile * rows, blocks, tile)
        elif tile < early + 2 * shared:
            which, at = divmod(tile - early, shared)
            pl.when(half_ref[0] == which)(
                functools.partial(write, one_ref, (early + at) * rows, blocks, tile)
            )
        else:
            write(two_ref, (tile - early - 2 * shared) * rows, blocks, tile)
    pieces = [out_ref[:, c * LANES : (c + 1) * LANES].astype(f32) for c in range(width // LANES)]
    at = (early + shared) * rows
    rest = one_ref.shape[0] - at - len(pieces) * depth
    if rest:
        pieces.append(jnp.zeros((rest, LANES), f32))
    one_ref[at:, :] = jnp.concatenate(pieces, axis=0).astype(bf16)


def out_rows(width, depth):
    return -(-(width // LANES * depth) // 16) * 16


def pack_call(half, w_gate, w_up, w_down, w_out, shards, early, shared):
    depth, hidden = w_gate.shape
    width = w_down.shape[1]
    rows = 6 * depth
    tiles = hidden // TILE
    sizes = (early + shared) * rows + out_rows(width, depth), (tiles - early - 2 * shared) * rows
    whole = lambda shape: pl.BlockSpec(shape, lambda i, *_: (0, 0))
    return pl.pallas_call(
        functools.partial(pack_kernel, shards=shards, early=early, shared=shared),
        grid_spec=pltpu.PrefetchScalarGridSpec(
            num_scalar_prefetch=1,
            grid=(1,),
            in_specs=[whole(w.shape) for w in (w_gate, w_up, w_down, w_out)],
            out_specs=[whole((n, LANES)) for n in sizes],
        ),
        out_shape=[jax.ShapeDtypeStruct((n, LANES), bf16) for n in sizes],
        compiler_params=pltpu.CompilerParams(vmem_limit_bytes=62 * MIB),
        cost_estimate=LIGHT,
        name="pack",
    )(half, w_gate, w_up, w_down, w_out)


def unpack_kernel(at_ref, *refs, shards, cuts):
    chunks = [refs[:4], refs[4:8]]
    wg_ref, wu_ref, gate_ref, up_ref, down_ref, gain_ref, *scratch = refs[8:]
    depth, hidden = gate_ref.shape
    width = down_ref.shape[1]
    tiles = hidden // TILE
    own = TILE // shards
    per = LANES // own
    half_rows = 6 * depth
    core, seq = at_ref[0], at_ref[3]
    for (a, b, c, d), ref in zip(chunks, scratch):
        ref[core, seq] = a[...]
        ref[core, 1 - seq] = b[...]
        ref[1 - core, seq] = c[...]
        ref[1 - core, 1 - seq] = d[...]
    counts = [3 * sum(cut) // half_rows for cut in cuts]

    def rows_of(tile, half, start, size):
        at = tile // 2
        chunk = at >= counts[0]
        at -= counts[0] * chunk
        first, second = cuts[chunk]
        place = at * half_rows + start
        begin, cut = 0, first
        if place >= 3 * first:
            place, begin, cut = place - 3 * first, first, second

        def line_of(place):
            block, place = divmod(place, cut)
            return block * (first + second) + begin + place

        if size == depth:
            row = line_of(place)
            both = scratch[chunk][tile % 2, half, row : row + 2 * size, :].astype(f32)
            low, high = both[:size], both[size:]
        else:
            low, high = (
                scratch[chunk][tile % 2, half, row : row + size, :].astype(f32)
                for row in (line_of(place), line_of(place + size))
            )
        return jnp.where(core == 0, low, high)

    lane = lax.broadcasted_iota(jnp.int32, (depth, LANES), 1) // own
    wide = [[rows_of(tile, at // 3, at % 3 * 2 * depth, depth) for at in range(4)] for tile in range(tiles)]
    gain = jnp.zeros((depth, LANES), f32)
    for number, (ref, weight_ref) in enumerate(((gate_ref, wg_ref), (up_ref, wu_ref))):
        for block in range(hidden // LANES):
            total = None
            for i in range(per):
                shard, tile = divmod(block * per + i, tiles)
                c, at = divmod(shard, per)
                value = wide[tile][2 * number + c]
                if (i - at) % per:
                    value = pltpu.roll(value, (i - at) % per * own, 1)
                total = value if total is None else jnp.where(lane == i, value, total)
            columns = slice(block * LANES, (block + 1) * LANES)
            ref[:, columns] = total
            gain = gain + total * weight_ref[:, columns].astype(f32)
    gain_ref[...] = gain
    for tile in range(tiles):
        for c in range(width // LANES):
            value = rows_of(tile, 1, 2 * depth + c * 2 * own, own)
            down_ref[tile * own : (tile + 1) * own, c * LANES : (c + 1) * LANES] = value


def unpack_call(at, chunks, cuts, w_gate, w_up, shards):
    depth, hidden = w_gate.shape
    tiles = hidden // TILE
    own = TILE // shards
    width = depth * shards
    args = [piece for chunk in chunks for piece in chunk] + [w_gate, w_up]
    out_shape = [
        jax.ShapeDtypeStruct((depth, hidden), f32),
        jax.ShapeDtypeStruct((depth, hidden), f32),
        jax.ShapeDtypeStruct((tiles * own, width), f32),
        jax.ShapeDtypeStruct((depth, LANES), f32),
    ]
    whole = lambda array: pl.BlockSpec(array.shape, lambda i, *_: (0, 0))
    return pl.pallas_call(
        functools.partial(unpack_kernel, shards=shards, cuts=cuts),
        grid_spec=pltpu.PrefetchScalarGridSpec(
            num_scalar_prefetch=1,
            grid=(1,),
            in_specs=[whole(array) for array in args],
            out_specs=[whole(array) for array in out_shape],
            scratch_shapes=[pltpu.VMEM((2, 2, *chunk[0].shape), bf16) for chunk in chunks],
        ),
        out_shape=out_shape,
        compiler_params=pltpu.CompilerParams(vmem_limit_bytes=62 * MIB),
        cost_estimate=LIGHT,
        name="unpack",
    )(at, *args)


def pack_weights(w_gate, w_up, w_down, shards):
    depth, hidden = w_gate.shape
    tiles = hidden // TILE
    own = TILE // shards

    def columns(weight):
        parts = weight.reshape(depth, shards, tiles, own).transpose(0, 2, 1, 3)
        parts = parts.reshape(depth, tiles, TILE // LANES, LANES).transpose(1, 2, 0, 3)
        return parts.reshape(tiles, -1, LANES)

    width = w_down.shape[1]
    down = w_down.reshape(tiles, own, width // LANES, LANES).transpose(0, 2, 1, 3)
    return jnp.concatenate([columns(w_gate), columns(w_up), down.reshape(tiles, -1, LANES)], axis=1)


def unpack_grads(packed, shards, depth):
    tiles = packed.shape[0]
    own = TILE // shards

    def columns(part):
        part = part.reshape(tiles, TILE // LANES, depth, LANES).transpose(2, 0, 1, 3)
        part = part.reshape(depth, tiles, shards, own).transpose(0, 2, 1, 3)
        return part.reshape(depth, tiles * TILE)

    gate, up = columns(packed[:, : 2 * depth]), columns(packed[:, 2 * depth : 4 * depth])
    down = packed[:, 4 * depth :].reshape(tiles, -1, own, LANES).transpose(0, 2, 1, 3)
    return gate, up, down.reshape(tiles * own, -1)


def regroup_weights(gathered, groups, tiles, depth, own):
    shards = gathered.shape[0]
    if shards == groups:
        return gathered
    many = shards // groups
    gathered = gathered.reshape(groups, many, tiles, -1, LANES)
    outs = []
    for start, size in ((0, depth), (2 * depth, depth), (4 * depth, own)):
        stop = start + 2 * depth
        part = gathered[:, :, :, start:stop].reshape(groups, many, tiles, -1, size, LANES)
        outs.append(part.transpose(0, 2, 3, 1, 4, 5).reshape(groups, tiles, -1, LANES))
    return jnp.concatenate(outs, axis=2).reshape(groups, -1, LANES)


class Wires:
    def __init__(self, shards):
        self.shards = shards
        place = lax.axis_index("fsdp")
        self.core = place % 2
        self.inner = (place // 2) % 2
        self.line = place // 4
        self.seq = lax.axis_index("seq")

    def flip(self, values_in, bit):
        return lax.ppermute(values_in, "fsdp", [(i, i ^ bit) for i in range(self.shards)])

    def other_half(self, values_in):
        return lax.ppermute(values_in, "seq", [(0, 1), (1, 0)])


def ordered(bit, own, other):
    return jnp.where(bit == 0, own, other), jnp.where(bit == 0, other, own)


def gather_small(wires, shard, beside):
    if wires.shards != 16:
        return lax.all_gather(shard, "fsdp", axis=0, tiled=False)
    rows = shard.shape[0] // 2
    have = lax.dynamic_slice_in_dim(shard, wires.seq * rows, rows)[None]
    have = jnp.stack(ordered(wires.line // 2, have, wires.flip(have, 8)), axis=0)
    have = jnp.concatenate(ordered(wires.line % 2, have, wires.flip(have, 4)), axis=1)
    have = have.reshape(4, rows, -1)
    beside = beside(have)
    have = jnp.stack(ordered(wires.inner, have, after(wires.flip(have, 2), beside)), axis=1)
    have = jnp.concatenate(ordered(wires.seq, have, wires.other_half(have)), axis=2)
    have = jnp.stack(ordered(wires.core, have, wires.flip(have, 1)), axis=2)
    return have.reshape((16,) + shard.shape)


def pick(values_in, place, axis):
    return lax.dynamic_index_in_dim(values_in, place, axis, keepdims=False)


def plus(*terms):
    return sum(term.astype(f32) for term in terms).astype(bf16)


def after(values_in, others):
    return lax.optimization_barrier((values_in, others))[0]


def sums_kernel(*refs, plan):
    ins = iter(refs)
    for out_ref, parts in zip(refs[sum(map(sum, plan)) :], plan):
        start = 0
        for count in parts:
            total = sum(next(ins)[...].astype(f32) for _ in range(count)).astype(bf16)
            stop = start + total.shape[-2]
            out_ref[..., start:stop, :] = total
            start = stop


def sums(groups, grid=1, others=(), cost=LIGHT, through=()):
    args, in_specs, out_specs, out_shape, plan = [], [], [], [], []
    for parts in groups:
        below = 0
        for terms in parts:
            for array, block, place in terms:
                args.append(array)
                if grid == 1:
                    index = lambda i, place=place: place
                else:
                    index = lambda i, place=place: (*place[:-2], i, 0)
                in_specs.append(pl.BlockSpec(block, index))
            below += block[-2]
        lead = tuple(n for n in block[:-2] if n is not None)
        out_specs.append(pl.BlockSpec((*lead, below, LANES), lambda i, n=len(lead): (0,) * n + (i, 0)))
        out_shape.append(jax.ShapeDtypeStruct((*lead, below * grid, LANES), bf16))
        plan.append([len(terms) for terms in parts])
    return pl.pallas_call(
        dropping(functools.partial(sums_kernel, plan=plan), len(args), len(others) + len(through)),
        grid=(grid,),
        in_specs=in_specs + [ANYWHERE] * (len(others) + len(through)),
        out_specs=out_specs + [ANYWHERE] * len(through),
        out_shape=out_shape + alike(through),
        input_output_aliases={len(args) + len(others) + i: len(plan) + i for i in range(len(through))},
        compiler_params=pltpu.CompilerParams(vmem_limit_bytes=62 * MIB),
        cost_estimate=cost,
        name="sums",
    )(*args, *others, *through)


class ChipSum:
    def __init__(self, wires, keep_x, send_x, keep_y, send_y, grid):
        self.wires, self.grid = wires, grid
        self.kept = keep_x, keep_y
        self.got = wires.flip(send_x, 2), wires.other_half(send_y)

    def rows(self, array):
        return array.shape[-2] // self.grid

    def second(self):
        whole = lambda array: (array, (None, 4, self.rows(array), LANES), (1, 0, 0, 0))
        return [[[whole(k), whole(g)]] for k, g in zip(self.kept, self.got)]

    def second_sent(self, *sent):
        self.sent = sent
        self.next = self.wires.other_half(sent[0]), self.wires.flip(sent[1], 2)

    def third(self):
        groups = []
        for at in (1, 0):
            parts = []
            for k, g, n in zip(self.kept, self.got, self.next):
                old = (None, 2, self.rows(k), LANES), (0, at, 0, 0)
                parts.append([(k, *old), (g, *old), (n, old[0][1:], old[1][1:])])
            groups.append(parts)
        return groups

    def third_sent(self, sent, kept):
        self.sent, self.kept = (sent,), kept
        self.got = self.wires.flip(sent, 4)

    def fourth(self):
        block = (None, self.rows(self.kept), LANES)
        return [[[(self.kept, block, (1, 0, 0)), (self.got, block, (1, 0, 0))]]]

    def fourth_sent(self, sent):
        self.sent = (sent,)
        self.next = self.wires.flip(sent, 8)

    def fifth(self):
        block = (None, self.rows(self.kept), LANES)
        terms = [(self.kept, block, (0, 0, 0)), (self.got, block, (0, 0, 0)), (self.next, block[1:], (0, 0))]
        return [[terms]]

    def fifth_sent(self, sent):
        self.sent = (sent,)
        self.got = self.wires.other_half(sent)

    def total(self):
        return ordered(self.wires.seq, self.sent[0], self.got)


def quarters_in(wires, values_in):
    half = values_in.shape[0] // 2
    got = wires.other_half(values_in[half:])
    return jnp.concatenate(ordered(wires.seq, values_in[:half], got), axis=0)


def per_device(
    shards, tokens, seg_ids, first_gain, w_qkv, b_qkv, w_out, second_gain, w_gate, w_up, w_down, cotangent
):
    wires = Wires(shards)
    tokens = tokens[0]
    count, width = tokens.shape
    depth, qkv_width = w_qkv.shape
    kv_width = (qkv_width - width) // 2
    group = (width // HEAD) // (kv_width // HEAD)
    tiles = w_gate.shape[1] // TILE
    own = TILE // shards
    own_bias = b_qkv.shape[0]
    groups = 16
    chips = groups // 2
    full_depth = width // groups
    full_own = TILE // groups
    small_mesh = shards == groups
    half = wires.seq.astype(jnp.int32).reshape(1)
    if small_mesh:
        at = jnp.stack([wires.core, wires.inner, wires.line, wires.seq]).astype(jnp.int32)
    else:
        at = jnp.stack([wires.core] + [jnp.zeros_like(wires.core)] * 3).astype(jnp.int32)
    steps = -(-tiles // 2)
    early, shared = (EARLY, SHARED) if small_mesh else (2 * (steps // 2), 0)

    pad_rows = -(-(depth + 1) // 8) * 8 - depth
    vector = jnp.concatenate([first_gain, b_qkv, second_gain])
    vector = jnp.pad(vector, (0, qkv_width - vector.shape[0]))
    small = jnp.concatenate([w_qkv, jnp.pad(vector[None], ((0, pad_rows - 1), (0, 0)))], axis=0)
    other_segs = wires.other_half(seg_ids)
    tokens = quarters_in(wires, tokens)
    small, (w_gate, w_up, w_down, w_out) = lax.optimization_barrier((small, (w_gate, w_up, w_down, w_out)))
    out_packed = w_out.reshape(depth, width // LANES, LANES).transpose(1, 0, 2).reshape(-1, LANES)
    out_packed = jnp.pad(out_packed, ((0, out_rows(width, depth) - out_packed.shape[0]), (0, 0)))
    if small_mesh:
        packed_one, packed_two = pack_call(
            half, w_gate, w_up, w_down, w_out, shards, early, shared
        )
    else:
        packed = pack_weights(w_gate, w_up, w_down, shards)
        packed_one = jnp.concatenate([packed[:early].reshape(-1, LANES), out_packed], axis=0)
        packed_two = packed[early:].reshape(-1, LANES)
    all_one = lax.all_gather(packed_one, "fsdp", axis=0, tiled=False)
    packed_two = after(packed_two, packed_one)
    all_two = lax.all_gather(packed_two, "fsdp", axis=0, tiled=False)
    block = count // 2

    def tables(seg_ids, other_segs):
        less = lambda k: jnp.sum((seg_ids < k).astype(jnp.int32)) + jnp.sum((other_segs < k).astype(jnp.int32))
        ones, twos = less(1), less(2)
        own_segs = jnp.concatenate(ordered(wires.seq, seg_ids[0, :block], other_segs[0, block:]))
        far_segs = jnp.concatenate(ordered(wires.seq, seg_ids[0, block:], other_segs[0, :block]))
        index = jnp.arange(count, dtype=jnp.int32)
        index = index + jnp.where(wires.seq == 0, jnp.where(index < block, 0, 2 * block), block)
        local_pos = index - jnp.where(own_segs == 0, 0, jnp.where(own_segs == 1, ones, twos))
        inverse = THETA ** (-(jnp.arange(HEAD // 2, dtype=f32) * 2.0 / HEAD))
        angles = local_pos.astype(f32)[:, None] * inverse[None, :]
        cosines, sines = jnp.cos(angles), jnp.sin(angles)
        cosines = jnp.concatenate([cosines] * 4, axis=1)
        sines = jnp.concatenate([-sines, sines] * 2, axis=1)
        doc = jnp.arange(LANES, dtype=jnp.int32)[None, :]
        kx = (own_segs[:, None] == doc).astype(bf16)
        rkx = (far_segs[:, None] == doc).astype(bf16)
        qx = jnp.where((own_segs[:, None] == doc) | (doc >= 3), 0.0, FAR).astype(bf16)
        return cosines, sines, kx, rkx, qx

    made = []

    def beside(started):
        made.extend(tables(*after((seg_ids, other_segs), started)))
        made.append(after(tokens, started))
        return tuple(made)

    small_all = gather_small(wires, small, beside)
    if not made:
        beside(())
    cosines, sines, kx, rkx, qx, tokens = made
    qkv_full = small_all[:, :depth].reshape(width, qkv_width)
    vectors = small_all[:, depth]
    gain_one = vectors[:, :depth].reshape(1, width).astype(f32)
    bias = vectors[:, depth : depth + own_bias].reshape(1, qkv_width).astype(f32)
    gain_two = vectors[:, depth + own_bias : 2 * depth + own_bias].reshape(1, width).astype(f32)

    normed, queries, kv = project_call(tokens, gain_one, qkv_full, bias, cosines, sines)
    far_kv = wires.other_half(kv)
    cotangent = after(cotangent[0], small_all)
    got = wires.other_half(cotangent[block:])
    near, stats = near_forward(queries, qx, kv, kx, group)
    far_kv, got = after((far_kv, got), stats)
    grad_mlp = jnp.concatenate(ordered(wires.seq, cotangent[:block], got), axis=0)
    far_grad = wires.flip(grad_mlp, 1)
    attended, lse = far_forward(half, queries, qx, far_kv, rkx, near, after(stats, grad_mlp), group)
    far_grad = after(far_grad, lse)
    first_rows = all_one.shape[1] - out_packed.shape[0]
    if small_mesh:
        start, out_weight = first_rows, all_one
    else:
        out_weight = all_one[:, first_rows : first_rows + width // LANES * depth]
        out_weight = out_weight.reshape(shards, width // LANES, depth, LANES).transpose(0, 2, 1, 3)
        start, out_weight = None, out_weight.reshape(width, width)
    middle, normed_two, out_full = out_project(
        tokens, attended, gain_two, out_weight, start, out_packed.shape[0]
    )
    far_normed = wires.flip(normed_two, 1)

    if not small_mesh:
        all_one = regroup_weights(all_one[:, :first_rows], groups, early, depth, own)
        all_two = regroup_weights(all_two, groups, tiles - early, depth, own)
    rows = 6 * full_depth
    tokens_in = at, normed_two, far_normed, grad_mlp, far_grad
    own_tile = lambda start, last: lambda j, at: jnp.clip(2 * (j - start) + at[0], 0, last)
    one_steps = early // 2
    two_weights, two_counts = [(all_two, own_tile(shared, tiles - early - 2 * shared - 1))], [steps - one_steps - shared]
    if shared:
        mine = lax.dynamic_slice_in_dim(all_one, (early + wires.core) * rows, rows, axis=1)
        theirs = wires.other_half(mine)
    own_one, other_one, *grads_one = mlp_call(
        *tokens_in, [(all_one, own_tile(0, early - 1))], [one_steps], tiles, 0, one_steps // 2
    )
    if shared:
        both = jnp.concatenate(ordered(wires.seq, mine, after(theirs, own_one)), axis=1)
        two_weights.insert(0, (both, lambda j, at: jnp.minimum(j, shared - 1)))
        two_counts.insert(0, shared)
    if small_mesh:
        sum_one = ChipSum(wires, *grads_one, 3)
    back_one = wires.flip(other_one, 1)
    own_two, other_two, *grads_two = mlp_call(
        *tokens_in, two_weights, two_counts, tiles, one_steps, (steps - one_steps) // 2
    )
    back_two = wires.flip(other_two, 1)
    if small_mesh:
        sum_one.second_sent(*sums(sum_one.second(), 3, (own_two,), HEAVY))

    others = sum_one.sent if small_mesh else ()
    kept_result, sent_result, grad_middle, branch, grad_attended, *grads_two = middle_back(
        half, (own_one, own_two, back_one, back_two), middle, grad_mlp, gain_two, out_full, others, grads_two
    )
    if small_mesh:
        sum_two = ChipSum(wires, *grads_two, 3)
    far_query, far_kv_grad = far_backward(
        half, queries, qx, grad_attended, attended, lse, far_kv, rkx, group, ()
    )
    got_kv = wires.other_half(far_kv_grad)
    others = ()
    if small_mesh:
        sum_one.third_sent(*sums(sum_one.third(), 3, (far_query,), MIDDLE))
        others = sum_one.sent
    query_grad, kv_grad = near_backward(
        queries, qx, grad_attended, attended, lse, cosines, sines, kv, kx, far_query, group, others
    )
    others = ()
    if small_mesh:
        *sent_two, sent_one, sent_result = sums(
            sum_two.second() + sum_one.fourth(), 3, (query_grad, got_kv), through=(sent_result,)
        )
        sum_two.second_sent(*sent_two)
        sum_one.fourth_sent(sent_one)
        others = (*sum_two.sent, *sum_one.sent)
    got_result = wires.other_half(sent_result)
    project, mine, theirs, bias_grad = weight_grads(
        at, normed, query_grad, kv_grad, got_kv, cosines, sines, branch, attended, qkv_width, others
    )

    qk_own = (width + kv_width) // shards
    blocks = (qkv_width + width) // LANES
    cut = blocks // 4 * full_depth
    if small_mesh:
        theirs = wires.flip(theirs, 1)
        kept_grad, sent_grad = input_grad(half, tokens, gain_one, project, qkv_full, grad_middle, ())
        sent_two, kept_two, sent_one = sums(sum_two.third() + sum_one.fifth(), 3, (kept_grad,), HEAVY)
        sum_two.third_sent(sent_two, kept_two)
        sum_one.fifth_sent(sent_one)
        groups_of = []
        for axis in range(2):
            block = [2, 2, 4, cut + 16, LANES]
            block[axis] = None
            for part in (0, 1):
                place = [0, 0, 0, axis, 0]
                place[axis] = part
                groups_of.append([[(array, tuple(block), tuple(place)) for array in (mine, theirs)]])
        small = ChipSum(wires, *sums(groups_of, 1, sum_two.sent), 1)
        small.second_sent(*sums(small.second(), 1, (got_result,), SHORT))
        sent_two, sent_grad = sums(sum_two.fourth(), 3, small.sent, through=(sent_grad,))
        sum_two.fourth_sent(sent_two)
        small.third_sent(*sums(small.third(), 1, sum_two.sent, MIDDLE))
        got_grad = wires.other_half(sent_grad)
        small.fourth_sent(*sums(small.fourth(), 1))
        sent_two, sum_one.got, got_grad = sums(
            sum_two.fifth(), 3, small.sent, HEAVY, (sum_one.got, got_grad)
        )
        sum_two.fifth_sent(sent_two)
        small.fifth_sent(*sums(small.fifth(), 1, sum_two.sent))
        one, two = small.total()
        bias = one[2 * cut + 16 : 2 * cut + 18].astype(f32)
        bias_qk = lax.dynamic_slice_in_dim(bias[0], wires.core * qk_own, qk_own)
        bias_v = lax.dynamic_slice_in_dim(bias[1], lax.axis_index("fsdp") * (kv_width // shards), kv_width // shards)
        total = jnp.stack([one, two], axis=0).reshape(2, 2, cut + 16, LANES)[:, :, :cut]
        total = total.transpose(1, 0, 2, 3).reshape(blocks, depth, LANES)
    else:
        kept_grad, sent_grad = input_grad(half, tokens, gain_one, project, qkv_full, grad_middle, ())
        got_grad = wires.other_half(sent_grad)
        total = jnp.stack(ordered(wires.core, mine, theirs), axis=0)[:, :, :, jnp.array(LINE)]
        total = total.reshape(*total.shape[:4], 2, cut + 16, LANES)[:, :, :, :, :, :cut]
        total = total.reshape(2, 2, 2, 4, 2, blocks // 4, shards // groups, depth, LANES)
        total = total.transpose(3, 1, 0, 6, 4, 2, 5, 7, 8).reshape(shards, -1, LANES)
        total = lax.psum_scatter(total.astype(f32), "fsdp", scatter_dimension=0, tiled=True)[0]
        total = lax.psum(total.astype(bf16), "seq").reshape(blocks, depth, LANES)
        bias = lax.psum(bias_grad[0], ("seq", "fsdp"))
        place = lax.axis_index("fsdp")
        bias_qk = lax.dynamic_slice_in_dim(bias, place * qk_own, qk_own)
        bias_v = lax.dynamic_slice_in_dim(
            bias, width + kv_width + place * (kv_width // shards), kv_width // shards
        )
    result = jnp.concatenate([kept_result, got_result], axis=0)
    grad_input = jnp.concatenate([kept_grad, got_grad], axis=0)
    total = total.transpose(1, 0, 2).reshape(depth, -1).astype(f32)
    gain_one_grad = jnp.sum(total[:, :qkv_width] * w_qkv.astype(f32), axis=1) / first_gain.astype(f32)

    half_rows = 6 * full_depth
    if small_mesh:
        chunks, cuts = [], []
        for chip_sum, (first, _, second, _) in ((sum_one, grads_one), (sum_two, grads_two)):
            pair = chip_sum.sent[0], chip_sum.got
            chunks.append((*pair, *(wires.flip(piece, 1) for piece in pair)))
            cuts.append((first.shape[2] // 3, second.shape[2] // 3))
        gate_grad, up_grad, down_grad, gain_two_grad = unpack_call(at, chunks, cuts, w_gate, w_up, shards)
        gain_two_grad = jnp.sum(gain_two_grad, axis=1) / second_gain.astype(f32)
    else:
        many = shards // groups
        terms = []
        for keep_x, send_x, keep_y, send_y in (grads_one, grads_two):
            first = jnp.stack([keep_x, send_x], axis=0).reshape(2, 2, 4, -1, half_rows, LANES)
            second = jnp.stack([keep_y, send_y], axis=0).reshape(2, 2, 4, -1, half_rows, LANES)
            places = jnp.array(LINE)
            first = first.transpose(2, 0, 3, 1, 4, 5)[places].reshape(chips, -1, 2, half_rows, LANES)
            second = second.transpose(2, 1, 3, 0, 4, 5)[places].reshape(chips, -1, 2, half_rows, LANES)
            terms += [first, second]
        terms = jnp.concatenate(terms, axis=1).reshape(chips, steps, 2 * half_rows, LANES)
        parts = []
        for start, size in ((0, depth), (4 * full_depth, depth), (8 * full_depth, own)):
            part = terms[:, :, start : start + 4 * full_depth]
            part = part.reshape(chips, steps, -1, 2 * many, size, LANES)
            parts.append(part.transpose(0, 3, 1, 2, 4, 5).reshape(shards, steps, -1, LANES))
        terms = jnp.concatenate(parts, axis=2).astype(f32)
        terms = lax.dynamic_update_index_in_dim(jnp.zeros((2,) + terms.shape, f32), terms, wires.core, 0)
        terms = lax.psum_scatter(terms, "fsdp", scatter_dimension=1, tiled=True)[:, 0]
        terms = lax.psum(terms.astype(bf16), "seq")
        mlp_grads = terms.transpose(1, 0, 2, 3).reshape(2 * steps, -1, LANES)[:tiles]
        gate_grad, up_grad, down_grad = unpack_grads(mlp_grads, shards, depth)
        both = gate_grad.astype(f32) * w_gate.astype(f32) + up_grad.astype(f32) * w_up.astype(f32)
        gain_two_grad = jnp.sum(both, axis=1) / second_gain.astype(f32)
    return (
        result[None],
        grad_input[None],
        gain_one_grad,
        total[:, :qkv_width],
        bias_qk,
        bias_v,
        total[:, qkv_width:],
        gain_two_grad,
        gate_grad.astype(f32),
        up_grad.astype(f32),
        down_grad.astype(f32),
    )


def solution(mesh):
    rows, split, lone = P("fsdp", "seq", None), P("fsdp", None), P("fsdp")
    in_specs = (rows, P("fsdp", "seq"), lone, split, lone, split, lone, split, split, split, rows)
    out_specs = (rows, rows, lone, split, lone, lone, split, lone, split, split, split)
    return jax.shard_map(
        functools.partial(per_device, mesh.shape["fsdp"]),
        mesh=mesh,
        in_specs=in_specs,
        out_specs=out_specs,
        check_vma=False,
    )
```

```python
import functools

import jax
import jax.numpy as jnp
from jax import lax
from jax.experimental import pallas as pl
from jax.experimental.pallas import tpu as pltpu
from jax.sharding import PartitionSpec as P

HEAD = 64
LANES = 128
TILE = 256
EPSILON = 1e-06
THETA = 1000000.0
FAR = -1e30
MIB = 2**20
EARLY = 10
SHARED = 2

LIGHT = pl.CostEstimate(flops=1, bytes_accessed=1, transcendentals=0)
MIDDLE = pl.CostEstimate(flops=8 * 10**9, bytes_accessed=MIB, transcendentals=0)
HEAVY = pl.CostEstimate(flops=6 * 10**10, bytes_accessed=16 * MIB, transcendentals=0)

bf16 = jnp.bfloat16
f32 = jnp.float32


def dot_nn(left, right):
    return lax.dot_general(left, right, (((1,), (0,)), ((), ())), preferred_element_type=f32)


def dot_nt(left, right):
    return lax.dot_general(left, right, (((1,), (1,)), ((), ())), preferred_element_type=f32)


def dot_tn(left, right):
    return lax.dot_general(left, right, (((0,), (0,)), ((), ())), preferred_element_type=f32)


def swap_halves(values_in):
    lane = lax.broadcasted_iota(jnp.int32, values_in.shape, 1)
    ahead = pltpu.roll(values_in, LANES - HEAD // 2, 1)
    behind = pltpu.roll(values_in, HEAD // 2, 1)
    return jnp.where(lane % HEAD < HEAD // 2, ahead, behind)


def turn(values_in, cosines, sines):
    return values_in * cosines + swap_halves(values_in) * sines


def turn_back(grads_in, cosines, sines):
    return grads_in * cosines - swap_halves(grads_in) * sines


def project_kernel(x_ref, gain_ref, w_ref, bias_ref, cos_ref, sin_ref, normed_ref, q_ref, kv_ref):
    x = x_ref[...].astype(f32)
    scale = lax.rsqrt(jnp.mean(x * x, axis=1, keepdims=True) + EPSILON)
    normed = (x * scale * gain_ref[...]).astype(bf16)
    normed_ref[...] = normed
    project = dot_nn(normed, w_ref[...]) + bias_ref[...]
    cosines, sines = cos_ref[...], sin_ref[...]
    width = q_ref.shape[1]
    for start in range(0, width, LANES):
        part = slice(start, start + LANES)
        q_ref[:, part] = turn(project[:, part], cosines, sines).astype(bf16) * (HEAD**-0.5)
    kv_ref[:, :LANES] = turn(project[:, width : width + LANES], cosines, sines).astype(bf16)
    kv_ref[:, LANES:] = project[:, width + LANES :].astype(bf16)


def project_call(x, gain, weight, bias, cosines, sines):
    tokens, width = x.shape
    outs = weight.shape[1]
    rows = tokens // 3
    row = lambda cols: pl.BlockSpec((rows, cols), lambda i: (i, 0))
    whole = lambda *shape: pl.BlockSpec(shape, lambda i: (0, 0))
    return pl.pallas_call(
        project_kernel,
        grid=(3,),
        in_specs=[
            row(width),
            whole(1, width),
            whole(width, outs),
            whole(1, outs),
            row(LANES),
            row(LANES),
        ],
        out_specs=[row(width), row(width), row(2 * LANES)],
        out_shape=[
            jax.ShapeDtypeStruct((tokens, width), bf16),
            jax.ShapeDtypeStruct((tokens, width), bf16),
            jax.ShapeDtypeStruct((tokens, 2 * LANES), bf16),
        ],
        compiler_params=pltpu.CompilerParams(vmem_limit_bytes=62 * MIB),
        cost_estimate=LIGHT,
        name="project",
    )(x, gain, weight, bias, cosines, sines)


def dropping(kernel, start, count):
    def inner(*refs, **settings):
        kernel(*refs[:start], *refs[start + count :], **settings)

    return inner


def spread(ref, columns, out_ref, turned_ref=None):
    both = ref[:, columns].astype(f32)
    shifted = pltpu.roll(both, HEAD, 1)
    low = lax.broadcasted_iota(jnp.int32, both.shape, 1) < HEAD
    for head in range(2):
        for parity in range(2):
            source = both if head == parity else shifted
            alone = jnp.where(low if parity == 0 else ~low, source, 0.0)
            out_ref[head, parity] = alone.astype(bf16)
            if turned_ref is not None:
                turned_ref[head, parity] = alone.T.astype(bf16)


def causal(scores, flipped):
    row_at = lax.broadcasted_iota(jnp.int32, scores.shape, 0)
    col_at = lax.broadcasted_iota(jnp.int32, scores.shape, 1)
    return jnp.where(row_at <= col_at if flipped else col_at <= row_at, scores, FAR)


def near_forward_kernel(q_ref, qx_ref, kv_ref, kx_ref, o_ref, lse_ref, k_s, v_s, *, group):
    step = pl.program_id(0)
    block = q_ref.shape[0] // 2
    lane = lax.broadcasted_iota(jnp.int32, (block, LANES), 1)

    @pl.when(step == 0)
    def _():
        spread(kv_ref, slice(0, LANES), k_s)
        spread(kv_ref, slice(LANES, 2 * LANES), v_s)
        lse_ref[...] = jnp.zeros_like(lse_ref)

    for b in range(2):
        rows = slice(b * block, (b + 1) * block)
        q = jnp.concatenate([q_ref[rows], qx_ref[rows]], axis=1)
        total = None
        stats = lse_ref[rows]
        for parity in range(2):
            kv = (2 * step + parity) // group
            k_at = lambda rows: jnp.concatenate([k_s[kv, parity, rows], kx_ref[rows]], axis=1)
            pieces = [(causal(dot_nt(q, k_at(rows)), False), v_s[kv, parity, rows])]
            if b:
                first = slice(0, block)
                pieces.append((dot_nt(q, k_at(first)), v_s[kv, parity, first]))
            top = functools.reduce(jnp.maximum, [jnp.max(s, axis=1, keepdims=True) for s, _ in pieces])
            weights = [(jnp.exp(s - top), v) for s, v in pieces]
            norm = sum(jnp.sum(p, axis=1, keepdims=True) for p, _ in weights)
            out = sum(dot_nn(p.astype(bf16), v) for p, v in weights) * (1.0 / norm)
            total = out if total is None else total + out
            stats = jnp.where(lane == 2 * step + parity, top + jnp.log(norm), stats)
        o_ref[rows] = total
        lse_ref[rows] = stats


def far_forward_kernel(half_ref, q_ref, qx_ref, kv_ref, kx_ref, near_ref, stats_ref, o_ref, lse_ref, k_s, v_s, lse_s, *, group):
    step = pl.program_id(0)
    tokens = q_ref.shape[0]
    block = tokens // 2

    @pl.when(step == 0)
    def _():
        spread(kv_ref, slice(0, LANES), k_s)
        spread(kv_ref, slice(LANES, 2 * LANES), v_s)
        lse_s[...] = stats_ref[...]

    def run(blocks, keys):
        for b in blocks:
            rows = slice(b * block, (b + 1) * block)
            q = jnp.concatenate([q_ref[rows], qx_ref[rows]], axis=1)
            lane = lax.broadcasted_iota(jnp.int32, (block, LANES), 1)
            stats = lse_s[rows]
            total = None
            scale = None
            for parity in range(2):
                head = 2 * step + parity
                kv = head // group
                k = jnp.concatenate([k_s[kv, parity, keys], kx_ref[keys]], axis=1)
                s = dot_nt(q, k)
                top = jnp.max(s, axis=1, keepdims=True)
                p = jnp.exp(s - top)
                norm = jnp.sum(p, axis=1, keepdims=True)
                far = top + jnp.log(norm)
                near = jnp.sum(jnp.where(lane == head, stats, 0.0), axis=1, keepdims=True)
                both = jnp.maximum(near, far)
                both = both + jnp.log(jnp.exp(near - both) + jnp.exp(far - both))
                out = dot_nn(p.astype(bf16), v_s[kv, parity, keys]) * jnp.exp(top - both)
                total = out if total is None else total + out
                weight = jnp.exp(near - both)
                scale = weight if scale is None else jnp.where(lane < HEAD, scale, weight)
                stats = jnp.where(lane == head, both, stats)
            o_ref[rows] = (near_ref[rows] * scale + total).astype(bf16)
            lse_s[rows] = stats

    @pl.when(half_ref[0] == 0)
    def _():
        first = slice(0, block)
        o_ref[first] = near_ref[first].astype(bf16)
        run((1,), slice(0, tokens))

    @pl.when(half_ref[0] != 0)
    def _():
        run((0, 1), slice(0, block))

    @pl.when(step == pl.num_programs(0) - 1)
    def _():
        lse_ref[...] = lse_s[...].T


def near_forward(q, qx, kv, kx, group):
    tokens, width = q.shape
    column = pl.BlockSpec((tokens, LANES), lambda p: (0, p))
    whole = lambda *shape: pl.BlockSpec(shape, lambda p: (0, 0))
    spare = lambda: pltpu.VMEM((2, 2, tokens, LANES), bf16)
    return pl.pallas_call(
        functools.partial(near_forward_kernel, group=group),
        grid=(width // LANES,),
        in_specs=[column, whole(tokens, LANES), whole(tokens, 2 * LANES), whole(tokens, LANES)],
        out_specs=[column, whole(tokens, LANES)],
        scratch_shapes=[spare(), spare()],
        out_shape=[
            jax.ShapeDtypeStruct((tokens, width), f32),
            jax.ShapeDtypeStruct((tokens, LANES), f32),
        ],
        compiler_params=pltpu.CompilerParams(vmem_limit_bytes=62 * MIB),
        cost_estimate=HEAVY,
        name="attention_near",
    )(q, qx, kv, kx)


def far_forward(half, q, qx, kv, kx, near, stats, group):
    tokens, width = q.shape
    column = pl.BlockSpec((tokens, LANES), lambda p, *_: (0, p))
    whole = lambda *shape: pl.BlockSpec(shape, lambda p, *_: (0, 0))
    spare = lambda: pltpu.VMEM((2, 2, tokens, LANES), bf16)
    return pl.pallas_call(
        functools.partial(far_forward_kernel, group=group),
        grid_spec=pltpu.PrefetchScalarGridSpec(
            num_scalar_prefetch=1,
            grid=(width // LANES,),
            in_specs=[
                column,
                whole(tokens, LANES),
                whole(tokens, 2 * LANES),
                whole(tokens, LANES),
                column,
                whole(tokens, LANES),
            ],
            out_specs=[column, whole(LANES, tokens)],
            scratch_shapes=[spare(), spare(), pltpu.VMEM((tokens, LANES), f32)],
        ),
        out_shape=[
            jax.ShapeDtypeStruct((tokens, width), bf16),
            jax.ShapeDtypeStruct((LANES, tokens), f32),
        ],
        compiler_params=pltpu.CompilerParams(vmem_limit_bytes=62 * MIB),
        cost_estimate=LIGHT,
        name="attention_far",
    )(half, q, qx, kv, kx, near, stats)


def back_block(q, q_wide, g, lse, delta, k, kx, turned, v, masked):
    s = dot_nt(jnp.concatenate([k, kx], axis=1), q_wide)
    if masked:
        s = causal(s, True)
    p = jnp.exp(s - lse)
    ds = (p * (dot_nt(v, g) - delta)).astype(bf16)
    return dot_nn(p.astype(bf16), g), dot_nn(ds, q), dot_nn(turned, ds)


def gather_heads(acc, out_ref, columns):
    low = lax.broadcasted_iota(jnp.int32, acc.shape[2:], 1) < HEAD
    first = acc[0, 0] + pltpu.roll(acc[0, 1], HEAD, 1)
    second = acc[1, 1] + pltpu.roll(acc[1, 0], HEAD, 1)
    out_ref[:, columns] = jnp.where(low, first, second).astype(out_ref.dtype)


def far_backward_kernel(half_ref, q_ref, qx_ref, g_ref, o_ref, lse_ref, kv_ref, kx_ref, dq_ref, dkv_ref, k_s, t_s, v_s, ka, va, *, group):
    step = pl.program_id(0)
    tokens = q_ref.shape[0]
    block = tokens // 2
    keys, values = slice(0, LANES), slice(LANES, 2 * LANES)

    @pl.when(step == 0)
    def _():
        spread(kv_ref, keys, k_s, t_s)
        spread(kv_ref, values, v_s)
        ka[...] = jnp.zeros_like(ka)
        va[...] = jnp.zeros_like(va)

    def run(blocks, key_blocks):
        for b in blocks:
            rows = slice(b * block, (b + 1) * block)
            q = q_ref[rows]
            q_wide = jnp.concatenate([q, qx_ref[rows]], axis=1)
            g = g_ref[rows]
            product = (g.astype(f32) * o_ref[rows].astype(f32)).T
            total = None
            for parity in range(2):
                head = 2 * step + parity
                kv = head // group
                lse = lse_ref[pl.ds(head, 1), rows]
                delta = jnp.sum(product[parity * HEAD : (parity + 1) * HEAD], axis=0, keepdims=True)
                for c in key_blocks:
                    part = slice(c * block, (c + 1) * block)
                    dv, dk, dq = back_block(
                        q, q_wide, g, lse, delta, k_s[kv, parity, part], kx_ref[part],
                        t_s[kv, parity, :, part], v_s[kv, parity, part], False,
                    )
                    va[kv, parity, part] += dv
                    ka[kv, parity, part] += dk
                    total = dq if total is None else total + dq
            dq_ref[:, rows] = total

    @pl.when(half_ref[0] == 0)
    def _():
        dq_ref[:, :block] = jnp.zeros((LANES, block), f32)
        run((1,), (0, 1))

    @pl.when(half_ref[0] != 0)
    def _():
        run((0, 1), (0,))

    @pl.when(step == pl.num_programs(0) - 1)
    def _():
        gather_heads(ka, dkv_ref, keys)
        gather_heads(va, dkv_ref, values)


def near_backward_kernel(q_ref, qx_ref, g_ref, o_ref, lse_ref, cos_ref, sin_ref, kv_ref, kx_ref, far_ref, dq_ref, dkv_ref, k_s, t_s, v_s, ka, va, *, group):
    step = pl.program_id(0)
    tokens = q_ref.shape[0]
    block = tokens // 2
    keys, values = slice(0, LANES), slice(LANES, 2 * LANES)

    @pl.when(step == 0)
    def _():
        spread(kv_ref, keys, k_s, t_s)
        spread(kv_ref, values, v_s)
        ka[...] = jnp.zeros_like(ka)
        va[...] = jnp.zeros_like(va)

    for b in range(2):
        rows = slice(b * block, (b + 1) * block)
        q = q_ref[rows]
        q_wide = jnp.concatenate([q, qx_ref[rows]], axis=1)
        g = g_ref[rows]
        product = (g.astype(f32) * o_ref[rows].astype(f32)).T
        total = far_ref[:, rows]
        for parity in range(2):
            head = 2 * step + parity
            kv = head // group
            lse = lse_ref[pl.ds(head, 1), rows]
            delta = jnp.sum(product[parity * HEAD : (parity + 1) * HEAD], axis=0, keepdims=True)
            for c in range(b + 1):
                part = slice(c * block, (c + 1) * block)
                dv, dk, dq = back_block(
                    q, q_wide, g, lse, delta, k_s[kv, parity, part], kx_ref[part],
                    t_s[kv, parity, :, part], v_s[kv, parity, part], c == b,
                )
                va[kv, parity, part] += dv
                ka[kv, parity, part] += dk
                total = total + dq
        dq_ref[rows] = turn_back(total.T * (HEAD**-0.5), cos_ref[rows], sin_ref[rows]).astype(bf16)

    @pl.when(step == pl.num_programs(0) - 1)
    def _():
        gather_heads(ka, dkv_ref, keys)
        gather_heads(va, dkv_ref, values)


ANYWHERE = pl.BlockSpec(memory_space=pl.ANY)


def alike(arrays):
    return [jax.ShapeDtypeStruct(array.shape, array.dtype) for array in arrays]


def backward_scratch(tokens):
    return [
        pltpu.VMEM((2, 2, tokens, LANES), bf16),
        pltpu.VMEM((2, 2, LANES, tokens), bf16),
        pltpu.VMEM((2, 2, tokens, LANES), bf16),
        pltpu.VMEM((2, 2, tokens, LANES), f32),
        pltpu.VMEM((2, 2, tokens, LANES), f32),
    ]


def far_backward(half, q, qx, g, o, lse, kv, kx, group, through):
    tokens, width = q.shape
    column = pl.BlockSpec((tokens, LANES), lambda p, *_: (0, p))
    across = pl.BlockSpec((LANES, tokens), lambda p, *_: (p, 0))
    whole = lambda *shape: pl.BlockSpec(shape, lambda p, *_: (0, 0))
    return pl.pallas_call(
        functools.partial(dropping(dropping(far_backward_kernel, 10, len(through)), 8, len(through)), group=group),
        grid_spec=pltpu.PrefetchScalarGridSpec(
            num_scalar_prefetch=1,
            grid=(width // LANES,),
            in_specs=[
                column,
                whole(tokens, LANES),
                column,
                column,
                whole(LANES, tokens),
                whole(tokens, 2 * LANES),
                whole(tokens, LANES),
            ]
            + [ANYWHERE] * len(through),
            out_specs=[across, whole(tokens, 2 * LANES)] + [ANYWHERE] * len(through),
            scratch_shapes=backward_scratch(tokens),
        ),
        out_shape=[
            jax.ShapeDtypeStruct((width, tokens), f32),
            jax.ShapeDtypeStruct((tokens, 2 * LANES), bf16),
            *alike(through),
        ],
        input_output_aliases={8 + i: 2 + i for i in range(len(through))},
        compiler_params=pltpu.CompilerParams(vmem_limit_bytes=64 * MIB - 65536),
        cost_estimate=LIGHT,
        name="attention_far_back",
    )(half, q, qx, g, o, lse, kv, kx, *through)


def near_backward(q, qx, g, o, lse, cosines, sines, kv, kx, far, group, others):
    tokens, width = q.shape
    column = pl.BlockSpec((tokens, LANES), lambda p: (0, p))
    across = pl.BlockSpec((LANES, tokens), lambda p: (p, 0))
    whole = lambda *shape: pl.BlockSpec(shape, lambda p: (0, 0))
    return pl.pallas_call(
        functools.partial(dropping(near_backward_kernel, 10, len(others)), group=group),
        grid=(width // LANES,),
        in_specs=[
            column,
            whole(tokens, LANES),
            column,
            column,
            whole(LANES, tokens),
            whole(tokens, LANES),
            whole(tokens, LANES),
            whole(tokens, 2 * LANES),
            whole(tokens, LANES),
            across,
        ]
        + [ANYWHERE] * len(others),
        out_specs=[column, whole(tokens, 2 * LANES)],
        scratch_shapes=backward_scratch(tokens),
        out_shape=[
            jax.ShapeDtypeStruct((tokens, width), bf16),
            jax.ShapeDtypeStruct((tokens, 2 * LANES), f32),
        ],
        compiler_params=pltpu.CompilerParams(vmem_limit_bytes=64 * MIB - 65536),
        cost_estimate=LIGHT,
        name="attention_near_back",
    )(q, qx, g, o, lse, cosines, sines, kv, kx, far, *others)


def weight_grads_kernel(at_ref, normed_ref, dq_ref, dkv_ref, got_ref, cos_ref, sin_ref, branch_ref, att_ref, project_ref, mine_ref, theirs_ref, bias_ref):
    kv = dkv_ref[...] + got_ref[...].astype(f32)
    keys = turn_back(kv[:, :LANES], cos_ref[...], sin_ref[...])
    project = jnp.concatenate([dq_ref[...], keys.astype(bf16), kv[:, LANES:].astype(bf16)], axis=1)
    project_ref[...] = project
    bias = jnp.sum(project.astype(f32), axis=0, keepdims=True)
    bias_ref[...] = bias
    core, inner, line, seq = (at_ref[i] for i in range(4))
    width = normed_ref.shape[1]
    chips = 8
    piece = width // chips // 2
    normed_t, att_t = normed_ref[...].T, att_ref[...].T
    columns = [(normed_t, project[:, s : s + LANES]) for s in range(0, project.shape[1], LANES)]
    columns += [(att_t, branch_ref[:, s : s + LANES]) for s in range(0, width, LANES)]
    for pair in range(len(columns) // 2):
        (left, one), (other, two) = columns[2 * pair : 2 * pair + 2]
        if left is other:
            value = dot_nn(left, jnp.concatenate([one, two], axis=1))
            one, two = value[:, :LANES], value[:, LANES:]
        else:
            one, two = dot_nn(left, one), dot_nn(other, two)
        quarter = pair // 2
        half = (quarter % 2) ^ seq
        start = quarter // 2 * (4 * piece + 16) + pair % 2 * 2 * piece
        for chip in range(chips):
            rows = slice(chip * 2 * piece, (chip + 1) * 2 * piece)
            here, there = one[rows], two[rows]
            low = jnp.concatenate([here[:piece], there[:piece]], axis=0)
            high = jnp.concatenate([here[piece:], there[piece:]], axis=0)
            away = (chip // 2) ^ line
            place = 2 * (away % 2) + away // 2
            for ref, first in ((mine_ref, core == 0), (theirs_ref, core != 0)):
                value = jnp.where(first, low, high).astype(bf16)
                ref[(chip % 2) ^ inner, half, place, start : start + 2 * piece, :] = value
    row = lax.broadcasted_iota(jnp.int32, (16, LANES), 0)
    last = bias[:, project.shape[1] - LANES :]
    for chip in range(chips):
        away = (chip // 2) ^ line
        place = 2 * (away % 2) + away // 2
        first = bias[:, chip * LANES : (chip + 1) * LANES]
        value = jnp.where(row == 0, first, jnp.where(row == 1, last, 0.0)).astype(bf16)
        for ref in (mine_ref, theirs_ref):
            for half in range(2):
                ref[(chip % 2) ^ inner, half, place, 4 * piece : 4 * piece + 16, :] = value
                ref[(chip % 2) ^ inner, half, place, 8 * piece + 16 :, :] = value


def weight_grads(at, normed, dq, dkv, got, cosines, sines, branch, attended, outs, others):
    tokens, width = normed.shape
    rows = (outs + width) // LANES * (width // 16) // 2 + 32
    packed = jax.ShapeDtypeStruct((2, 2, 4, rows, LANES), bf16)
    out_shape = [
        jax.ShapeDtypeStruct((tokens, outs), bf16),
        packed,
        packed,
        jax.ShapeDtypeStruct((1, outs), f32),
    ]
    args = (normed, dq, dkv, got, cosines, sines, branch, attended)
    whole = lambda array: pl.BlockSpec(array.shape, lambda i, *_: (0,) * len(array.shape))
    return pl.pallas_call(
        dropping(weight_grads_kernel, 9, len(others)),
        grid_spec=pltpu.PrefetchScalarGridSpec(
            num_scalar_prefetch=1,
            grid=(1,),
            in_specs=[whole(array) for array in args] + [ANYWHERE] * len(others),
            out_specs=[whole(array) for array in out_shape],
        ),
        out_shape=out_shape,
        compiler_params=pltpu.CompilerParams(vmem_limit_bytes=64 * MIB - 65536),
        cost_estimate=LIGHT,
        name="weight_grads",
    )(at, *args, *others)


def store_half(value, kept_ref, sent_ref):
    for step, ref in enumerate((kept_ref, sent_ref)):

        @pl.when(pl.program_id(0) == step)
        def _(ref=ref):
            ref[...] = value


def input_grad_kernel(at_ref, x_ref, gain_ref, project_ref, w_ref, gm_ref, kept_ref, sent_ref):
    grad = dot_nt(project_ref[...], w_ref[...]) * gain_ref[...]
    x = x_ref[...].astype(f32)
    scale = lax.rsqrt(jnp.mean(x * x, axis=1, keepdims=True) + EPSILON)
    normal = x * scale
    mean = jnp.mean(grad * normal, axis=1, keepdims=True)
    store_half((gm_ref[...] + scale * (grad - normal * mean)).astype(bf16), kept_ref, sent_ref)


def input_grad(half, x, gain, project, weight, grad_middle, others):
    tokens, width = x.shape
    outs = weight.shape[1]
    rows = tokens // 2
    row = lambda cols: pl.BlockSpec((rows, cols), lambda i, half: (i ^ half[0], 0))
    whole = lambda *shape: pl.BlockSpec(shape, lambda i, half: (0, 0))
    return pl.pallas_call(
        dropping(input_grad_kernel, 6, len(others)),
        grid_spec=pltpu.PrefetchScalarGridSpec(
            num_scalar_prefetch=1,
            grid=(2,),
            in_specs=[row(width), whole(1, width), row(outs), whole(width, outs), row(width)]
            + [ANYWHERE] * len(others),
            out_specs=[whole(rows, width)] * 2,
        ),
        out_shape=[jax.ShapeDtypeStruct((rows, width), bf16)] * 2,
        compiler_params=pltpu.CompilerParams(vmem_limit_bytes=64 * MIB - 65536),
        cost_estimate=LIGHT,
        name="input_grad",
    )(half, x, gain, project, weight, grad_middle, *others)


def out_project_kernel(x_ref, att_ref, gain_ref, w_ref, middle_ref, normed_ref, out_ref, raw_s, w_s, sem, *, start):
    step = pl.program_id(0)

    @pl.when(step == 0)
    def _():
        if start is None:
            w_s[...] = w_ref[...]
        else:
            copy = pltpu.make_async_copy(w_ref.at[:, pl.ds(start, raw_s.shape[1]), :], raw_s, sem)
            copy.start()
            copy.wait()
            width = w_s.shape[0]
            depth = width // raw_s.shape[0]
            for c in range(width // LANES):
                rows = raw_s[:, c * depth : (c + 1) * depth, :].astype(f32)
                w_s[:, c * LANES : (c + 1) * LANES] = rows.reshape(width, LANES).astype(bf16)
        out_ref[...] = w_s[...]

    middle = x_ref[...].astype(f32) + dot_nn(att_ref[...], w_s[...])
    middle_ref[...] = middle
    scale = lax.rsqrt(jnp.mean(middle * middle, axis=1, keepdims=True) + EPSILON)
    normed_ref[...] = (middle * scale * gain_ref[...]).astype(bf16)


def out_project(x, attended, gain, weight, start, rows):
    tokens, width = x.shape
    part = tokens // 3
    row = pl.BlockSpec((part, width), lambda i: (i, 0))
    whole = lambda *shape: pl.BlockSpec(shape, lambda i: (0, 0))
    raw = start is not None
    return pl.pallas_call(
        functools.partial(out_project_kernel, start=start),
        grid=(3,),
        in_specs=[
            row,
            row,
            whole(1, width),
            pl.BlockSpec(memory_space=pl.ANY) if raw else whole(width, width),
        ],
        out_specs=[row, row, whole(width, width)],
        out_shape=[
            jax.ShapeDtypeStruct((tokens, width), f32),
            jax.ShapeDtypeStruct((tokens, width), bf16),
            jax.ShapeDtypeStruct((width, width), bf16),
        ],
        scratch_shapes=[
            pltpu.VMEM((weight.shape[0], rows, LANES) if raw else (8, LANES), bf16),
            pltpu.VMEM((width, width), bf16),
            pltpu.SemaphoreType.DMA,
        ],
        compiler_params=pltpu.CompilerParams(vmem_limit_bytes=62 * MIB),
        cost_estimate=LIGHT,
        name="out_project",
    )(x, attended, gain, weight)


def middle_back_kernel(at_ref, o1_ref, o2_ref, o3_ref, o4_ref, g1_ref, g2_ref, g3_ref, g4_ref, middle_ref, gout_ref, gain_ref, w_ref, kept_ref, sent_ref, gm_ref, branch_ref, gatt_ref):
    middle = middle_ref[...]
    added = sum(ref[...].astype(f32) for ref in (o1_ref, o2_ref, o3_ref, o4_ref))
    store_half((middle + added).astype(bf16), kept_ref, sent_ref)
    grad = sum(ref[...].astype(f32) for ref in (g1_ref, g2_ref, g3_ref, g4_ref))
    grad = grad * gain_ref[...]
    scale = lax.rsqrt(jnp.mean(middle * middle, axis=1, keepdims=True) + EPSILON)
    normal = middle * scale
    mean = jnp.mean(grad * normal, axis=1, keepdims=True)
    grad = gout_ref[...].astype(f32) + scale * (grad - normal * mean)
    gm_ref[...] = grad
    branch = grad.astype(bf16)
    branch_ref[...] = branch
    gatt_ref[...] = dot_nt(branch, w_ref[...]).astype(bf16)


def middle_back(half, terms, middle, grad_out, gain, weight, others, through):
    tokens, width = middle.shape
    rows = tokens // 2
    row = pl.BlockSpec((rows, width), lambda i, half: (i ^ half[0], 0))
    below = pl.BlockSpec((rows, width), lambda i, half: (2 + (i ^ half[0]), 0))
    whole = lambda *shape: pl.BlockSpec(shape, lambda i, half: (0, 0))
    shape = lambda kind: jax.ShapeDtypeStruct((tokens, width), kind)
    return pl.pallas_call(
        dropping(dropping(middle_back_kernel, 18, len(through)), 13, len(others) + len(through)),
        grid_spec=pltpu.PrefetchScalarGridSpec(
            num_scalar_prefetch=1,
            grid=(2,),
            in_specs=[row] * 4
            + [below] * 4
            + [row, row, whole(1, width), whole(width, width)]
            + [ANYWHERE] * (len(others) + len(through)),
            out_specs=[whole(rows, width)] * 2 + [row] * 3 + [ANYWHERE] * len(through),
        ),
        out_shape=[jax.ShapeDtypeStruct((rows, width), bf16)] * 2 + [shape(f32), shape(bf16), shape(bf16)] + alike(through),
        input_output_aliases={13 + len(others) + i: 5 + i for i in range(len(through))},
        compiler_params=pltpu.CompilerParams(vmem_limit_bytes=64 * MIB - 65536),
        cost_estimate=LIGHT,
        name="middle_back",
    )(half, *terms, *terms, middle, grad_out, gain, weight, *others, *through)


LINE = (0, 2, 1, 3)


def mlp_kernel(at_ref, near_ref, far_ref, gnear_ref, gfar_ref, *rest, counts, tiles, first, split):
    w_refs, rest = rest[: len(counts)], rest[len(counts) :]
    own_ref, other_ref, keep_x, send_x, keep_y, send_y = rest[:6]
    n_s, t_s, g_s, p_s, out_s, grad_s, gate_s, up_s, down_s = rest[6:]
    step = pl.program_id(0)
    tile = 2 * (first + step) + at_ref[0]
    tokens, width = near_ref.shape
    shards = w_refs[0].shape[0]
    depth = width // shards
    own = TILE // shards
    chips = shards // 2

    @pl.when(step == 0)
    def _():
        n_s[:tokens] = near_ref[...]
        n_s[tokens:] = far_ref[...]
        g_s[:tokens] = gnear_ref[...]
        g_s[tokens:] = gfar_ref[...]
        t_s[:, :tokens] = near_ref[...].T
        t_s[:, tokens:] = far_ref[...].T
        out_s[...] = jnp.zeros_like(out_s)
        grad_s[...] = jnp.zeros_like(grad_s)

    def load(w_ref):
        for at, square in ((0, gate_s), (2 * depth, up_s)):
            for c in range(TILE // LANES):
                rows = w_ref[:, at + c * depth : at + (c + 1) * depth, :]
                rows = rows.astype(f32).reshape(width, LANES).astype(bf16)
                square[:, c * LANES : (c + 1) * LANES] = rows
        for c in range(width // LANES):
            rows = w_ref[:, 4 * depth + c * own : 4 * depth + (c + 1) * own, :]
            down_s[:, c * LANES : (c + 1) * LANES] = rows.reshape(TILE, LANES)

    begin = 0
    for w_ref, many in zip(w_refs, counts):
        pl.when((step >= begin) & (step < begin + many))(functools.partial(load, w_ref))
        begin += many

    @pl.when(tile >= tiles)
    def _():
        p_s[...] = jnp.zeros_like(p_s)

    @pl.when(tile < tiles)
    def _():
        gate_w, up_w, down_w = gate_s[...], up_s[...], down_s[...]
        n = n_s[...]
        g = g_s[...]
        gate = dot_nn(n, gate_w)
        up = dot_nn(n, up_w)
        grad_hidden = dot_nt(g, down_w)
        sig = 1.0 / (1.0 + jnp.exp(-gate))
        silu = gate * sig
        hidden = (silu * up).astype(bf16)
        grad_gate = (grad_hidden * up * (sig + silu * (1.0 - sig))).astype(bf16)
        grad_up = (grad_hidden * silu).astype(bf16)
        out_s[...] += dot_nn(hidden, down_w)
        grad_s[...] += dot_nt(grad_gate, gate_w) + dot_nt(grad_up, up_w)
        for at, value in ((0, dot_nn(t_s[...], grad_gate)), (1, dot_nn(t_s[...], grad_up))):
            for c in range(TILE // LANES):
                part = value[:, c * LANES : (c + 1) * LANES].astype(bf16)
                start = (2 * at + c) * 2 * depth
                p_s[:, start : start + 2 * depth, :] = part.reshape(chips, 2 * depth, LANES)
        down = dot_tn(hidden, g)
        for c in range(width // LANES):
            part = down[:, c * LANES : (c + 1) * LANES].astype(bf16)
            start = 8 * depth + c * 2 * own
            p_s[:, start : start + 2 * own, :] = part.reshape(chips, 2 * own, LANES)

    half_rows = 6 * depth
    inner, line, seq = at_ref[1], at_ref[2], at_ref[3]

    def piece(line_off, inner_off, half_off):
        chip = 2 * (line ^ line_off) + (inner ^ inner_off)
        start = pl.multiple_of((seq ^ half_off) * half_rows, half_rows)
        return p_s[chip, pl.ds(start, half_rows), :]

    @pl.when(step < split)
    def _():
        for a, off in enumerate(LINE):
            for h in range(2):
                keep_x[h, a] = piece(off, 0, h)
                send_x[h, a] = piece(off, 1, h)

    @pl.when(step >= split)
    def _():
        for a, off in enumerate(LINE):
            for b in range(2):
                keep_y[b, a] = piece(off, b, 0)
                send_y[b, a] = piece(off, b, 1)

    @pl.when(step == pl.num_programs(0) - 1)
    def _():
        for ref, rows in ((own_ref, slice(0, tokens)), (other_ref, slice(tokens, 2 * tokens))):
            ref[:tokens] = out_s[rows].astype(bf16)
            ref[tokens:] = grad_s[rows].astype(bf16)


def mlp_call(at, near, far, gnear, gfar, weights, counts, tiles, first, split):
    tokens, width = near.shape
    shards = weights[0][0].shape[0]
    rows = 6 * width // shards
    count = sum(counts)
    whole = lambda *shape: pl.BlockSpec(shape, lambda j, *_: (0,) * len(shape))
    early = pl.BlockSpec((2, 4, rows, LANES), lambda j, *_: (0, 0, jnp.minimum(j, split - 1), 0))
    late = pl.BlockSpec((2, 4, rows, LANES), lambda j, *_: (0, 0, jnp.maximum(j - split, 0), 0))
    shape_x = jax.ShapeDtypeStruct((2, 4, rows * split, LANES), bf16)
    shape_y = jax.ShapeDtypeStruct((2, 4, rows * (count - split), LANES), bf16)
    wide = jax.ShapeDtypeStruct((2 * tokens, width), bf16)

    def block_of(index):
        return pl.BlockSpec((shards, rows, LANES), lambda j, at: (0, index(j, at), 0))

    return pl.pallas_call(
        functools.partial(mlp_kernel, counts=counts, tiles=tiles, first=first, split=split),
        grid_spec=pltpu.PrefetchScalarGridSpec(
            num_scalar_prefetch=1,
            grid=(count,),
            in_specs=[whole(tokens, width)] * 4 + [block_of(index) for _, index in weights],
            out_specs=[whole(2 * tokens, width)] * 2 + [early, early, late, late],
            scratch_shapes=[
                pltpu.VMEM((2 * tokens, width), bf16),
                pltpu.VMEM((width, 2 * tokens), bf16),
                pltpu.VMEM((2 * tokens, width), bf16),
                pltpu.VMEM((shards // 2, 2 * rows, LANES), bf16),
                pltpu.VMEM((2 * tokens, width), f32),
                pltpu.VMEM((2 * tokens, width), f32),
                pltpu.VMEM((width, TILE), bf16),
                pltpu.VMEM((width, TILE), bf16),
                pltpu.VMEM((TILE, width), bf16),
            ],
        ),
        out_shape=[
            wide,
            wide,
            shape_x,
            shape_x,
            shape_y,
            shape_y,
        ],
        compiler_params=pltpu.CompilerParams(vmem_limit_bytes=64 * MIB - 65536),
        cost_estimate=HEAVY,
        name="feed_forward",
    )(at, near, far, gnear, gfar, *(w for w, _ in weights))


def pack_kernel(half_ref, gate_ref, up_ref, down_ref, out_ref, one_ref, two_ref, *, shards, early, shared):
    depth, hidden = gate_ref.shape
    width = down_ref.shape[1]
    tiles = hidden // TILE
    own = TILE // shards
    rows = 6 * depth
    per = LANES // own
    lane = lax.broadcasted_iota(jnp.int32, (depth, LANES), 1) // own

    def write(target, at, blocks, tile):
        target[at : at + 4 * depth, :] = blocks
        for c in range(width // LANES):
            start = at + 4 * depth + c * own
            target[start : start + own, :] = down_ref[tile * own : (tile + 1) * own, c * LANES : (c + 1) * LANES]

    for tile in range(tiles):
        blocks = []
        for ref in (gate_ref, up_ref):
            for c in range(TILE // LANES):
                total = None
                by_shift = {}
                for i in range(per):
                    at = ((c * per + i) * tiles + tile) * own
                    by_shift.setdefault((i - at // own) % per, []).append((i, at // LANES))
                for shift, sources in by_shift.items():
                    value = None
                    for i, block in sources:
                        part = ref[:, block * LANES : (block + 1) * LANES].astype(f32)
                        here = lane == (i - shift) % per
                        value = part if value is None else jnp.where(here, part, value)
                    if shift:
                        value = pltpu.roll(value, shift * own, 1)
                    if total is None:
                        total = value
                    else:
                        for i, _ in sources:
                            total = jnp.where(lane == i, value, total)
                blocks.append(total)
        blocks = jnp.concatenate(blocks, axis=0).astype(bf16)
        if tile < early:
            write(one_ref, tile * rows, blocks, tile)
        elif tile < early + 2 * shared:
            which, at = divmod(tile - early, shared)
            pl.when(half_ref[0] == which)(
                functools.partial(write, one_ref, (early + at) * rows, blocks, tile)
            )
        else:
            write(two_ref, (tile - early - 2 * shared) * rows, blocks, tile)
    pieces = [out_ref[:, c * LANES : (c + 1) * LANES].astype(f32) for c in range(width // LANES)]
    at = (early + shared) * rows
    rest = one_ref.shape[0] - at - len(pieces) * depth
    if rest:
        pieces.append(jnp.zeros((rest, LANES), f32))
    one_ref[at:, :] = jnp.concatenate(pieces, axis=0).astype(bf16)


def out_rows(width, depth):
    return -(-(width // LANES * depth) // 16) * 16


def pack_call(half, w_gate, w_up, w_down, w_out, shards, early, shared):
    depth, hidden = w_gate.shape
    width = w_down.shape[1]
    rows = 6 * depth
    tiles = hidden // TILE
    sizes = (early + shared) * rows + out_rows(width, depth), (tiles - early - 2 * shared) * rows
    whole = lambda shape: pl.BlockSpec(shape, lambda i, *_: (0, 0))
    return pl.pallas_call(
        functools.partial(pack_kernel, shards=shards, early=early, shared=shared),
        grid_spec=pltpu.PrefetchScalarGridSpec(
            num_scalar_prefetch=1,
            grid=(1,),
            in_specs=[whole(w.shape) for w in (w_gate, w_up, w_down, w_out)],
            out_specs=[whole((n, LANES)) for n in sizes],
        ),
        out_shape=[jax.ShapeDtypeStruct((n, LANES), bf16) for n in sizes],
        compiler_params=pltpu.CompilerParams(vmem_limit_bytes=62 * MIB),
        cost_estimate=LIGHT,
        name="pack",
    )(half, w_gate, w_up, w_down, w_out)


def unpack_kernel(at_ref, *refs, shards, cuts):
    chunks = [refs[:4], refs[4:8]]
    wg_ref, wu_ref, gate_ref, up_ref, down_ref, gain_ref, *scratch = refs[8:]
    depth, hidden = gate_ref.shape
    width = down_ref.shape[1]
    tiles = hidden // TILE
    own = TILE // shards
    per = LANES // own
    half_rows = 6 * depth
    core, seq = at_ref[0], at_ref[3]
    for (a, b, c, d), ref in zip(chunks, scratch):
        ref[core, seq] = a[...]
        ref[core, 1 - seq] = b[...]
        ref[1 - core, seq] = c[...]
        ref[1 - core, 1 - seq] = d[...]
    counts = [3 * sum(cut) // half_rows for cut in cuts]

    def rows_of(tile, half, start, size):
        at = tile // 2
        chunk = at >= counts[0]
        at -= counts[0] * chunk
        first, second = cuts[chunk]
        place = at * half_rows + start
        begin, cut = 0, first
        if place >= 3 * first:
            place, begin, cut = place - 3 * first, first, second

        def line_of(place):
            block, place = divmod(place, cut)
            return block * (first + second) + begin + place

        if size == depth:
            row = line_of(place)
            both = scratch[chunk][tile % 2, half, row : row + 2 * size, :].astype(f32)
            low, high = both[:size], both[size:]
        else:
            low, high = (
                scratch[chunk][tile % 2, half, row : row + size, :].astype(f32)
                for row in (line_of(place), line_of(place + size))
            )
        return jnp.where(core == 0, low, high)

    lane = lax.broadcasted_iota(jnp.int32, (depth, LANES), 1) // own
    wide = [[rows_of(tile, at // 3, at % 3 * 2 * depth, depth) for at in range(4)] for tile in range(tiles)]
    gain = jnp.zeros((depth, LANES), f32)
    for number, (ref, weight_ref) in enumerate(((gate_ref, wg_ref), (up_ref, wu_ref))):
        for block in range(hidden // LANES):
            total = None
            for i in range(per):
                shard, tile = divmod(block * per + i, tiles)
                c, at = divmod(shard, per)
                value = wide[tile][2 * number + c]
                if (i - at) % per:
                    value = pltpu.roll(value, (i - at) % per * own, 1)
                total = value if total is None else jnp.where(lane == i, value, total)
            columns = slice(block * LANES, (block + 1) * LANES)
            ref[:, columns] = total
            gain = gain + total * weight_ref[:, columns].astype(f32)
    gain_ref[...] = gain
    for tile in range(tiles):
        for c in range(width // LANES):
            value = rows_of(tile, 1, 2 * depth + c * 2 * own, own)
            down_ref[tile * own : (tile + 1) * own, c * LANES : (c + 1) * LANES] = value


def unpack_call(at, chunks, cuts, w_gate, w_up, shards):
    depth, hidden = w_gate.shape
    tiles = hidden // TILE
    own = TILE // shards
    width = depth * shards
    args = [piece for chunk in chunks for piece in chunk] + [w_gate, w_up]
    out_shape = [
        jax.ShapeDtypeStruct((depth, hidden), f32),
        jax.ShapeDtypeStruct((depth, hidden), f32),
        jax.ShapeDtypeStruct((tiles * own, width), f32),
        jax.ShapeDtypeStruct((depth, LANES), f32),
    ]
    whole = lambda array: pl.BlockSpec(array.shape, lambda i, *_: (0, 0))
    return pl.pallas_call(
        functools.partial(unpack_kernel, shards=shards, cuts=cuts),
        grid_spec=pltpu.PrefetchScalarGridSpec(
            num_scalar_prefetch=1,
            grid=(1,),
            in_specs=[whole(array) for array in args],
            out_specs=[whole(array) for array in out_shape],
            scratch_shapes=[pltpu.VMEM((2, 2, *chunk[0].shape), bf16) for chunk in chunks],
        ),
        out_shape=out_shape,
        compiler_params=pltpu.CompilerParams(vmem_limit_bytes=64 * MIB - 65536),
        cost_estimate=LIGHT,
        name="unpack",
    )(at, *args)


def pack_weights(w_gate, w_up, w_down, shards):
    depth, hidden = w_gate.shape
    tiles = hidden // TILE
    own = TILE // shards

    def columns(weight):
        parts = weight.reshape(depth, shards, tiles, own).transpose(0, 2, 1, 3)
        parts = parts.reshape(depth, tiles, TILE // LANES, LANES).transpose(1, 2, 0, 3)
        return parts.reshape(tiles, -1, LANES)

    width = w_down.shape[1]
    down = w_down.reshape(tiles, own, width // LANES, LANES).transpose(0, 2, 1, 3)
    return jnp.concatenate([columns(w_gate), columns(w_up), down.reshape(tiles, -1, LANES)], axis=1)


def unpack_grads(packed, shards, depth):
    tiles = packed.shape[0]
    own = TILE // shards

    def columns(part):
        part = part.reshape(tiles, TILE // LANES, depth, LANES).transpose(2, 0, 1, 3)
        part = part.reshape(depth, tiles, shards, own).transpose(0, 2, 1, 3)
        return part.reshape(depth, tiles * TILE)

    gate, up = columns(packed[:, : 2 * depth]), columns(packed[:, 2 * depth : 4 * depth])
    down = packed[:, 4 * depth :].reshape(tiles, -1, own, LANES).transpose(0, 2, 1, 3)
    return gate, up, down.reshape(tiles * own, -1)


def regroup_weights(gathered, groups, tiles, depth, own):
    shards = gathered.shape[0]
    if shards == groups:
        return gathered
    many = shards // groups
    gathered = gathered.reshape(groups, many, tiles, -1, LANES)
    outs = []
    for start, size in ((0, depth), (2 * depth, depth), (4 * depth, own)):
        stop = start + 2 * depth
        part = gathered[:, :, :, start:stop].reshape(groups, many, tiles, -1, size, LANES)
        outs.append(part.transpose(0, 2, 3, 1, 4, 5).reshape(groups, tiles, -1, LANES))
    return jnp.concatenate(outs, axis=2).reshape(groups, -1, LANES)


class Wires:
    def __init__(self, shards):
        self.shards = shards
        place = lax.axis_index("fsdp")
        self.core = place % 2
        self.inner = (place // 2) % 2
        self.line = place // 4
        self.seq = lax.axis_index("seq")

    def flip(self, values_in, bit):
        return lax.ppermute(values_in, "fsdp", [(i, i ^ bit) for i in range(self.shards)])

    def other_half(self, values_in):
        return lax.ppermute(values_in, "seq", [(0, 1), (1, 0)])


def ordered(bit, own, other):
    return jnp.where(bit == 0, own, other), jnp.where(bit == 0, other, own)


def gather_small(wires, shard, beside):
    if wires.shards != 16:
        return lax.all_gather(shard, "fsdp", axis=0, tiled=False)
    rows = shard.shape[0] // 2
    have = lax.dynamic_slice_in_dim(shard, wires.seq * rows, rows)[None]
    have = jnp.stack(ordered(wires.line // 2, have, wires.flip(have, 8)), axis=0)
    have = jnp.concatenate(ordered(wires.line % 2, have, wires.flip(have, 4)), axis=1)
    have = have.reshape(4, rows, -1)
    beside = beside(have)
    have = jnp.stack(ordered(wires.inner, have, after(wires.flip(have, 2), beside)), axis=1)
    have = jnp.concatenate(ordered(wires.seq, have, wires.other_half(have)), axis=2)
    have = jnp.stack(ordered(wires.core, have, wires.flip(have, 1)), axis=2)
    return have.reshape((16,) + shard.shape)


def pick(values_in, place, axis):
    return lax.dynamic_index_in_dim(values_in, place, axis, keepdims=False)


def plus(*terms):
    return sum(term.astype(f32) for term in terms).astype(bf16)


def after(values_in, others):
    return lax.optimization_barrier((values_in, others))[0]


def sums_kernel(*refs, plan):
    ins = iter(refs)
    for out_ref, parts in zip(refs[sum(map(sum, plan)) :], plan):
        start = 0
        for count in parts:
            total = sum(next(ins)[...].astype(f32) for _ in range(count)).astype(bf16)
            stop = start + total.shape[-2]
            out_ref[..., start:stop, :] = total
            start = stop


def sums(groups, grid=1, others=(), cost=LIGHT, through=()):
    args, in_specs, out_specs, out_shape, plan = [], [], [], [], []
    for parts in groups:
        below = 0
        for terms in parts:
            for array, block, place in terms:
                args.append(array)
                index = lambda i, place=place: (*place[:-2], place[-2] * grid + i, 0)
                in_specs.append(pl.BlockSpec(block, index))
            below += block[-2]
        lead = tuple(n for n in block[:-2] if n is not None)
        out_specs.append(pl.BlockSpec((*lead, below, LANES), lambda i, n=len(lead): (0,) * n + (i, 0)))
        out_shape.append(jax.ShapeDtypeStruct((*lead, below * grid, LANES), bf16))
        plan.append([len(terms) for terms in parts])
    return pl.pallas_call(
        dropping(functools.partial(sums_kernel, plan=plan), len(args), len(others) + len(through)),
        grid=(grid,),
        in_specs=in_specs + [ANYWHERE] * (len(others) + len(through)),
        out_specs=out_specs + [ANYWHERE] * len(through),
        out_shape=out_shape + alike(through),
        input_output_aliases={len(args) + len(others) + i: len(plan) + i for i in range(len(through))},
        compiler_params=pltpu.CompilerParams(vmem_limit_bytes=64 * MIB - 65536),
        cost_estimate=cost,
        name="sums",
    )(*args, *others, *through)


class ChipSum:
    def __init__(self, wires, keep_x, send_x, keep_y, send_y, grid):
        self.wires, self.grid = wires, grid
        self.kept = keep_x, keep_y
        self.got = wires.flip(send_x, 2), wires.other_half(send_y)

    def rows(self, array):
        return array.shape[-2] // self.grid

    def second(self, grid=1):
        whole = lambda array: (array, (None, 4, array.shape[-2] // grid, LANES), (1, 0, 0, 0))
        return [[[whole(k), whole(g)]] for k, g in zip(self.kept, self.got)]

    def second_sent(self, *sent):
        self.sent = sent
        self.next = self.wires.other_half(sent[0]), self.wires.flip(sent[1], 2)

    def third(self):
        groups = []
        for at in (1, 0):
            parts = []
            for k, g, n in zip(self.kept, self.got, self.next):
                old = (None, 2, self.rows(k), LANES), (0, at, 0, 0)
                parts.append([(k, *old), (g, *old), (n, old[0][1:], old[1][1:])])
            groups.append(parts)
        return groups

    def third_sent(self, sent, kept):
        self.sent, self.kept = (sent,), kept
        self.got = self.wires.flip(sent, 4)

    def fourth(self, grid=1):
        block = (None, self.kept.shape[-2] // grid, LANES)
        return [[[(self.kept, block, (1, 0, 0)), (self.got, block, (1, 0, 0))]]]

    def fourth_sent(self, sent):
        self.sent = (sent,)
        self.next = self.wires.flip(sent, 8)

    def fifth(self, grid=1):
        block = (None, self.kept.shape[-2] // grid, LANES)
        terms = [(self.kept, block, (0, 0, 0)), (self.got, block, (0, 0, 0)), (self.next, block[1:], (0, 0))]
        return [[terms]]

    def fifth_sent(self, sent):
        self.sent = (sent,)
        self.got = self.wires.other_half(sent)

    def total(self):
        return ordered(self.wires.seq, self.sent[0], self.got)


def quarters_in(wires, values_in):
    half = values_in.shape[0] // 2
    got = wires.other_half(values_in[half:])
    return jnp.concatenate(ordered(wires.seq, values_in[:half], got), axis=0)


def per_device(
    shards, tokens, seg_ids, first_gain, w_qkv, b_qkv, w_out, second_gain, w_gate, w_up, w_down, cotangent
):
    wires = Wires(shards)
    tokens = tokens[0]
    count, width = tokens.shape
    depth, qkv_width = w_qkv.shape
    kv_width = (qkv_width - width) // 2
    group = (width // HEAD) // (kv_width // HEAD)
    tiles = w_gate.shape[1] // TILE
    own = TILE // shards
    own_bias = b_qkv.shape[0]
    groups = 16
    chips = groups // 2
    full_depth = width // groups
    full_own = TILE // groups
    small_mesh = shards == groups
    half = wires.seq.astype(jnp.int32).reshape(1)
    if small_mesh:
        at = jnp.stack([wires.core, wires.inner, wires.line, wires.seq]).astype(jnp.int32)
    else:
        at = jnp.stack([wires.core] + [jnp.zeros_like(wires.core)] * 3).astype(jnp.int32)
    steps = -(-tiles // 2)
    early, shared = (EARLY, SHARED) if small_mesh else (2 * (steps // 2), 0)

    pad_rows = -(-(depth + 1) // 8) * 8 - depth
    vector = jnp.concatenate([first_gain, b_qkv, second_gain])
    vector = jnp.pad(vector, (0, qkv_width - vector.shape[0]))
    small = jnp.concatenate([w_qkv, jnp.pad(vector[None], ((0, pad_rows - 1), (0, 0)))], axis=0)
    other_segs = wires.other_half(seg_ids)
    tokens = quarters_in(wires, tokens)
    small, (w_gate, w_up, w_down, w_out) = lax.optimization_barrier((small, (w_gate, w_up, w_down, w_out)))
    out_packed = w_out.reshape(depth, width // LANES, LANES).transpose(1, 0, 2).reshape(-1, LANES)
    out_packed = jnp.pad(out_packed, ((0, out_rows(width, depth) - out_packed.shape[0]), (0, 0)))
    if small_mesh:
        packed_one, packed_two = pack_call(
            half, w_gate, w_up, w_down, w_out, shards, early, shared
        )
    else:
        packed = pack_weights(w_gate, w_up, w_down, shards)
        packed_one = jnp.concatenate([packed[:early].reshape(-1, LANES), out_packed], axis=0)
        packed_two = packed[early:].reshape(-1, LANES)
    all_one = lax.all_gather(packed_one, "fsdp", axis=0, tiled=False)
    packed_two = after(packed_two, packed_one)
    all_two = lax.all_gather(packed_two, "fsdp", axis=0, tiled=False)
    block = count // 2

    def tables(seg_ids, other_segs):
        less = lambda k: jnp.sum((seg_ids < k).astype(jnp.int32)) + jnp.sum((other_segs < k).astype(jnp.int32))
        ones, twos = less(1), less(2)
        own_segs = jnp.concatenate(ordered(wires.seq, seg_ids[0, :block], other_segs[0, block:]))
        far_segs = jnp.concatenate(ordered(wires.seq, seg_ids[0, block:], other_segs[0, :block]))
        index = jnp.arange(count, dtype=jnp.int32)
        index = index + jnp.where(wires.seq == 0, jnp.where(index < block, 0, 2 * block), block)
        local_pos = index - jnp.where(own_segs == 0, 0, jnp.where(own_segs == 1, ones, twos))
        inverse = THETA ** (-(jnp.arange(HEAD // 2, dtype=f32) * 2.0 / HEAD))
        angles = local_pos.astype(f32)[:, None] * inverse[None, :]
        cosines, sines = jnp.cos(angles), jnp.sin(angles)
        cosines = jnp.concatenate([cosines] * 4, axis=1)
        sines = jnp.concatenate([-sines, sines] * 2, axis=1)
        doc = jnp.arange(LANES, dtype=jnp.int32)[None, :]
        kx = (own_segs[:, None] == doc).astype(bf16)
        rkx = (far_segs[:, None] == doc).astype(bf16)
        qx = jnp.where((own_segs[:, None] == doc) | (doc >= 3), 0.0, FAR).astype(bf16)
        return cosines, sines, kx, rkx, qx

    made = []

    def beside(started):
        made.extend(tables(*after((seg_ids, other_segs), started)))
        made.append(after(tokens, started))
        return tuple(made)

    small_all = gather_small(wires, small, beside)
    if not made:
        beside(())
    cosines, sines, kx, rkx, qx, tokens = made
    qkv_full = small_all[:, :depth].reshape(width, qkv_width)
    vectors = small_all[:, depth]
    gain_one = vectors[:, :depth].reshape(1, width).astype(f32)
    bias = vectors[:, depth : depth + own_bias].reshape(1, qkv_width).astype(f32)
    gain_two = vectors[:, depth + own_bias : 2 * depth + own_bias].reshape(1, width).astype(f32)

    normed, queries, kv = project_call(tokens, gain_one, qkv_full, bias, cosines, sines)
    far_kv = wires.other_half(kv)
    cotangent = after(cotangent[0], small_all)
    got = wires.other_half(cotangent[block:])
    near, stats = near_forward(queries, qx, kv, kx, group)
    far_kv, got = after((far_kv, got), stats)
    grad_mlp = jnp.concatenate(ordered(wires.seq, cotangent[:block], got), axis=0)
    far_grad = wires.flip(grad_mlp, 1)
    attended, lse = far_forward(half, queries, qx, far_kv, rkx, near, after(stats, grad_mlp), group)
    far_grad = after(far_grad, lse)
    first_rows = all_one.shape[1] - out_packed.shape[0]
    if small_mesh:
        start, out_weight = first_rows, all_one
    else:
        out_weight = all_one[:, first_rows : first_rows + width // LANES * depth]
        out_weight = out_weight.reshape(shards, width // LANES, depth, LANES).transpose(0, 2, 1, 3)
        start, out_weight = None, out_weight.reshape(width, width)
    middle, normed_two, out_full = out_project(
        tokens, attended, gain_two, out_weight, start, out_packed.shape[0]
    )
    far_normed = wires.flip(normed_two, 1)

    if not small_mesh:
        all_one = regroup_weights(all_one[:, :first_rows], groups, early, depth, own)
        all_two = regroup_weights(all_two, groups, tiles - early, depth, own)
    rows = 6 * full_depth
    tokens_in = at, normed_two, far_normed, grad_mlp, far_grad
    own_tile = lambda start, last: lambda j, at: jnp.clip(2 * (j - start) + at[0], 0, last)
    one_steps = early // 2
    two_weights, two_counts = [(all_two, own_tile(shared, tiles - early - 2 * shared - 1))], [steps - one_steps - shared]
    if shared:
        mine = lax.dynamic_slice_in_dim(all_one, (early + wires.core) * rows, rows, axis=1)
        theirs = wires.other_half(mine)
    own_one, other_one, *grads_one = mlp_call(
        *tokens_in, [(all_one, own_tile(0, early - 1))], [one_steps], tiles, 0, one_steps // 2
    )
    if shared:
        both = jnp.concatenate(ordered(wires.seq, mine, after(theirs, own_one)), axis=1)
        two_weights.insert(0, (both, lambda j, at: jnp.minimum(j, shared - 1)))
        two_counts.insert(0, shared)
    if small_mesh:
        sum_one = ChipSum(wires, *grads_one, 3)
    back_one = wires.flip(other_one, 1)
    own_two, other_two, *grads_two = mlp_call(
        *tokens_in, two_weights, two_counts, tiles, one_steps, (steps - one_steps) // 2
    )
    back_two = wires.flip(other_two, 1)
    if small_mesh:
        sum_one.second_sent(*sums(sum_one.second(1), 1, (own_two,), HEAVY))

    others = sum_one.sent if small_mesh else ()
    kept_result, sent_result, grad_middle, branch, grad_attended, *grads_two = middle_back(
        half, (own_one, own_two, back_one, back_two), middle, grad_mlp, gain_two, out_full, others, grads_two
    )
    if small_mesh:
        sum_two = ChipSum(wires, *grads_two, 3)
    far_query, far_kv_grad = far_backward(
        half, queries, qx, grad_attended, attended, lse, far_kv, rkx, group, ()
    )
    got_kv = wires.other_half(far_kv_grad)
    others = ()
    if small_mesh:
        sum_one.third_sent(*sums(sum_one.third(), 3, (far_query,), MIDDLE))
        others = sum_one.sent
    query_grad, kv_grad = near_backward(
        queries, qx, grad_attended, attended, lse, cosines, sines, kv, kx, far_query, group, others
    )
    others = ()
    if small_mesh:
        *sent_two, sent_one, sent_result = sums(
            sum_two.second(1) + sum_one.fourth(1), 1, (query_grad, got_kv), through=(sent_result,)
        )
        sum_two.second_sent(*sent_two)
        sum_one.fourth_sent(sent_one)
        others = (*sum_two.sent, *sum_one.sent)
    got_result = wires.other_half(sent_result)
    project, mine, theirs, bias_grad = weight_grads(
        at, normed, query_grad, kv_grad, got_kv, cosines, sines, branch, attended, qkv_width, others
    )

    qk_own = (width + kv_width) // shards
    blocks = (qkv_width + width) // LANES
    cut = blocks // 4 * full_depth
    if small_mesh:
        theirs = wires.flip(theirs, 1)
        kept_grad, sent_grad = input_grad(half, tokens, gain_one, project, qkv_full, grad_middle, ())
        sent_two, kept_two, sent_one = sums(sum_two.third() + sum_one.fifth(3), 3, (kept_grad,), HEAVY)
        sum_two.third_sent(sent_two, kept_two)
        sum_one.fifth_sent(sent_one)
        groups_of = []
        for axis in range(2):
            block = [2, 2, 4, cut + 16, LANES]
            block[axis] = None
            for part in (0, 1):
                place = [0, 0, 0, axis, 0]
                place[axis] = part
                groups_of.append([[(array, tuple(block), tuple(place)) for array in (mine, theirs)]])
        small = ChipSum(wires, *sums(groups_of, 1, (*sum_two.sent, got_result)), 1)
        *sent, sent_two, sent_grad = sums(small.second() + sum_two.fourth(), 1, (), LIGHT, (sent_grad,))
        small.second_sent(*sent)
        sum_two.fourth_sent(sent_two)
        got_grad = wires.other_half(sent_grad)
        small.third_sent(*sums(small.third(), 1, sum_two.sent, MIDDLE))
        sent, sent_two = sums(small.fourth() + sum_two.fifth())
        small.fourth_sent(sent)
        sum_two.fifth_sent(sent_two)
        sent, sum_one.got, got_grad, got_result = sums(
            small.fifth(), 1, sum_two.sent, LIGHT, (sum_one.got, got_grad, got_result)
        )
        small.fifth_sent(sent)
        one, two = small.total()
        bias = one[2 * cut + 16 : 2 * cut + 18].astype(f32)
        bias_qk = lax.dynamic_slice_in_dim(bias[0], wires.core * qk_own, qk_own)
        bias_v = lax.dynamic_slice_in_dim(bias[1], lax.axis_index("fsdp") * (kv_width // shards), kv_width // shards)
        total = jnp.stack([one, two], axis=0).reshape(2, 2, cut + 16, LANES)[:, :, :cut]
        total = total.transpose(1, 0, 2, 3).reshape(blocks, depth, LANES)
    else:
        kept_grad, sent_grad = input_grad(half, tokens, gain_one, project, qkv_full, grad_middle, ())
        got_grad = wires.other_half(sent_grad)
        total = jnp.stack(ordered(wires.core, mine, theirs), axis=0)[:, :, :, jnp.array(LINE)]
        total = total.reshape(*total.shape[:4], 2, cut + 16, LANES)[:, :, :, :, :, :cut]
        total = total.reshape(2, 2, 2, 4, 2, blocks // 4, shards // groups, depth, LANES)
        total = total.transpose(3, 1, 0, 6, 4, 2, 5, 7, 8).reshape(shards, -1, LANES)
        total = lax.psum_scatter(total.astype(f32), "fsdp", scatter_dimension=0, tiled=True)[0]
        total = lax.psum(total.astype(bf16), "seq").reshape(blocks, depth, LANES)
        bias = lax.psum(bias_grad[0], ("seq", "fsdp"))
        place = lax.axis_index("fsdp")
        bias_qk = lax.dynamic_slice_in_dim(bias, place * qk_own, qk_own)
        bias_v = lax.dynamic_slice_in_dim(
            bias, width + kv_width + place * (kv_width // shards), kv_width // shards
        )
    result = jnp.concatenate([kept_result, got_result], axis=0)
    grad_input = jnp.concatenate([kept_grad, got_grad], axis=0)
    total = total.transpose(1, 0, 2).reshape(depth, -1).astype(f32)
    gain_one_grad = jnp.sum(total[:, :qkv_width] * w_qkv.astype(f32), axis=1) / first_gain.astype(f32)

    half_rows = 6 * full_depth
    if small_mesh:
        chunks, cuts = [], []
        for chip_sum, (first, _, second, _) in ((sum_one, grads_one), (sum_two, grads_two)):
            pair = chip_sum.sent[0], chip_sum.got
            chunks.append((*pair, *(wires.flip(piece, 1) for piece in pair)))
            cuts.append((first.shape[2] // 3, second.shape[2] // 3))
        gate_grad, up_grad, down_grad, gain_two_grad = unpack_call(at, chunks, cuts, w_gate, w_up, shards)
        gain_two_grad = jnp.sum(gain_two_grad, axis=1) / second_gain.astype(f32)
    else:
        many = shards // groups
        terms = []
        for keep_x, send_x, keep_y, send_y in (grads_one, grads_two):
            first = jnp.stack([keep_x, send_x], axis=0).reshape(2, 2, 4, -1, half_rows, LANES)
            second = jnp.stack([keep_y, send_y], axis=0).reshape(2, 2, 4, -1, half_rows, LANES)
            places = jnp.array(LINE)
            first = first.transpose(2, 0, 3, 1, 4, 5)[places].reshape(chips, -1, 2, half_rows, LANES)
            second = second.transpose(2, 1, 3, 0, 4, 5)[places].reshape(chips, -1, 2, half_rows, LANES)
            terms += [first, second]
        terms = jnp.concatenate(terms, axis=1).reshape(chips, steps, 2 * half_rows, LANES)
        parts = []
        for start, size in ((0, depth), (4 * full_depth, depth), (8 * full_depth, own)):
            part = terms[:, :, start : start + 4 * full_depth]
            part = part.reshape(chips, steps, -1, 2 * many, size, LANES)
            parts.append(part.transpose(0, 3, 1, 2, 4, 5).reshape(shards, steps, -1, LANES))
        terms = jnp.concatenate(parts, axis=2).astype(f32)
        terms = lax.dynamic_update_index_in_dim(jnp.zeros((2,) + terms.shape, f32), terms, wires.core, 0)
        terms = lax.psum_scatter(terms, "fsdp", scatter_dimension=1, tiled=True)[:, 0]
        terms = lax.psum(terms.astype(bf16), "seq")
        mlp_grads = terms.transpose(1, 0, 2, 3).reshape(2 * steps, -1, LANES)[:tiles]
        gate_grad, up_grad, down_grad = unpack_grads(mlp_grads, shards, depth)
        both = gate_grad.astype(f32) * w_gate.astype(f32) + up_grad.astype(f32) * w_up.astype(f32)
        gain_two_grad = jnp.sum(both, axis=1) / second_gain.astype(f32)
    return (
        result[None],
        grad_input[None],
        gain_one_grad,
        total[:, :qkv_width],
        bias_qk,
        bias_v,
        total[:, qkv_width:],
        gain_two_grad,
        gate_grad.astype(f32),
        up_grad.astype(f32),
        down_grad.astype(f32),
    )


def solution(mesh):
    rows, split, lone = P("fsdp", "seq", None), P("fsdp", None), P("fsdp")
    in_specs = (rows, P("fsdp", "seq"), lone, split, lone, split, lone, split, split, split, rows)
    out_specs = (rows, rows, lone, split, lone, lone, split, lone, split, split, split)
    return jax.shard_map(
        functools.partial(per_device, mesh.shape["fsdp"]),
        mesh=mesh,
        in_specs=in_specs,
        out_specs=out_specs,
        check_vma=False,
    )
```

```python
import functools

import jax
import jax.numpy as jnp
from jax import lax
from jax.experimental import pallas as pl
from jax.experimental.pallas import tpu as pltpu
from jax.sharding import PartitionSpec as P

HEAD = 64
LANES = 128
TILE = 256
EPSILON = 1e-06
THETA = 1000000.0
FAR = -1e30
MIB = 2**20
EARLY = 10
SHARED = 2

LIGHT = pl.CostEstimate(flops=1, bytes_accessed=1, transcendentals=0)
MIDDLE = pl.CostEstimate(flops=8 * 10**9, bytes_accessed=MIB, transcendentals=0)
SHORT = pl.CostEstimate(flops=69 * 10**8, bytes_accessed=MIB, transcendentals=0)
HEAVY = pl.CostEstimate(flops=6 * 10**10, bytes_accessed=16 * MIB, transcendentals=0)

bf16 = jnp.bfloat16
f32 = jnp.float32


def dot_nn(left, right):
    return lax.dot_general(left, right, (((1,), (0,)), ((), ())), preferred_element_type=f32)


def dot_nt(left, right):
    return lax.dot_general(left, right, (((1,), (1,)), ((), ())), preferred_element_type=f32)


def dot_tn(left, right):
    return lax.dot_general(left, right, (((0,), (0,)), ((), ())), preferred_element_type=f32)


def swap_halves(values_in):
    lane = lax.broadcasted_iota(jnp.int32, values_in.shape, 1)
    ahead = pltpu.roll(values_in, LANES - HEAD // 2, 1)
    behind = pltpu.roll(values_in, HEAD // 2, 1)
    return jnp.where(lane % HEAD < HEAD // 2, ahead, behind)


def turn(values_in, cosines, sines):
    return values_in * cosines + swap_halves(values_in) * sines


def turn_back(grads_in, cosines, sines):
    return grads_in * cosines - swap_halves(grads_in) * sines


def project_kernel(x_ref, gain_ref, w_ref, bias_ref, cos_ref, sin_ref, normed_ref, q_ref, kv_ref):
    x = x_ref[...].astype(f32)
    scale = lax.rsqrt(jnp.mean(x * x, axis=1, keepdims=True) + EPSILON)
    normed = (x * scale * gain_ref[...]).astype(bf16)
    normed_ref[...] = normed
    project = dot_nn(normed, w_ref[...]) + bias_ref[...]
    cosines, sines = cos_ref[...], sin_ref[...]
    width = q_ref.shape[1]
    for start in range(0, width, LANES):
        part = slice(start, start + LANES)
        q_ref[:, part] = turn(project[:, part], cosines, sines).astype(bf16) * (HEAD**-0.5)
    kv_ref[:, :LANES] = turn(project[:, width : width + LANES], cosines, sines).astype(bf16)
    kv_ref[:, LANES:] = project[:, width + LANES :].astype(bf16)


def project_call(x, gain, weight, bias, cosines, sines):
    tokens, width = x.shape
    outs = weight.shape[1]
    rows = tokens // 3
    row = lambda cols: pl.BlockSpec((rows, cols), lambda i: (i, 0))
    whole = lambda *shape: pl.BlockSpec(shape, lambda i: (0, 0))
    return pl.pallas_call(
        project_kernel,
        grid=(3,),
        in_specs=[
            row(width),
            whole(1, width),
            whole(width, outs),
            whole(1, outs),
            row(LANES),
            row(LANES),
        ],
        out_specs=[row(width), row(width), row(2 * LANES)],
        out_shape=[
            jax.ShapeDtypeStruct((tokens, width), bf16),
            jax.ShapeDtypeStruct((tokens, width), bf16),
            jax.ShapeDtypeStruct((tokens, 2 * LANES), bf16),
        ],
        compiler_params=pltpu.CompilerParams(vmem_limit_bytes=62 * MIB),
        cost_estimate=LIGHT,
        name="project",
    )(x, gain, weight, bias, cosines, sines)


def dropping(kernel, start, count):
    def inner(*refs, **settings):
        kernel(*refs[:start], *refs[start + count :], **settings)

    return inner


def spread(ref, columns, out_ref, turned_ref=None):
    both = ref[:, columns].astype(f32)
    shifted = pltpu.roll(both, HEAD, 1)
    low = lax.broadcasted_iota(jnp.int32, both.shape, 1) < HEAD
    for head in range(2):
        for parity in range(2):
            source = both if head == parity else shifted
            alone = jnp.where(low if parity == 0 else ~low, source, 0.0)
            out_ref[head, parity] = alone.astype(bf16)
            if turned_ref is not None:
                turned_ref[head, parity] = alone.T.astype(bf16)


def causal(scores, flipped):
    row_at = lax.broadcasted_iota(jnp.int32, scores.shape, 0)
    col_at = lax.broadcasted_iota(jnp.int32, scores.shape, 1)
    return jnp.where(row_at <= col_at if flipped else col_at <= row_at, scores, FAR)


def near_forward_kernel(q_ref, qx_ref, kv_ref, kx_ref, o_ref, lse_ref, k_s, v_s, *, group):
    step = pl.program_id(0)
    block = q_ref.shape[0] // 2
    lane = lax.broadcasted_iota(jnp.int32, (block, LANES), 1)

    @pl.when(step == 0)
    def _():
        spread(kv_ref, slice(0, LANES), k_s)
        spread(kv_ref, slice(LANES, 2 * LANES), v_s)
        lse_ref[...] = jnp.zeros_like(lse_ref)

    for b in range(2):
        rows = slice(b * block, (b + 1) * block)
        q = jnp.concatenate([q_ref[rows], qx_ref[rows]], axis=1)
        total = None
        stats = lse_ref[rows]
        for parity in range(2):
            kv = (2 * step + parity) // group
            k_at = lambda rows: jnp.concatenate([k_s[kv, parity, rows], kx_ref[rows]], axis=1)
            pieces = [(causal(dot_nt(q, k_at(rows)), False), v_s[kv, parity, rows])]
            if b:
                first = slice(0, block)
                pieces.append((dot_nt(q, k_at(first)), v_s[kv, parity, first]))
            top = functools.reduce(jnp.maximum, [jnp.max(s, axis=1, keepdims=True) for s, _ in pieces])
            weights = [(jnp.exp(s - top), v) for s, v in pieces]
            norm = sum(jnp.sum(p, axis=1, keepdims=True) for p, _ in weights)
            out = sum(dot_nn(p.astype(bf16), v) for p, v in weights) * (1.0 / norm)
            total = out if total is None else total + out
            stats = jnp.where(lane == 2 * step + parity, top + jnp.log(norm), stats)
        o_ref[rows] = total
        lse_ref[rows] = stats


def far_forward_kernel(half_ref, q_ref, qx_ref, kv_ref, kx_ref, near_ref, stats_ref, o_ref, lse_ref, k_s, v_s, lse_s, *, group):
    step = pl.program_id(0)
    tokens = q_ref.shape[0]
    block = tokens // 2

    @pl.when(step == 0)
    def _():
        spread(kv_ref, slice(0, LANES), k_s)
        spread(kv_ref, slice(LANES, 2 * LANES), v_s)
        lse_s[...] = stats_ref[...]

    def run(blocks, keys):
        for b in blocks:
            rows = slice(b * block, (b + 1) * block)
            q = jnp.concatenate([q_ref[rows], qx_ref[rows]], axis=1)
            lane = lax.broadcasted_iota(jnp.int32, (block, LANES), 1)
            stats = lse_s[rows]
            total = None
            scale = None
            for parity in range(2):
                head = 2 * step + parity
                kv = head // group
                k = jnp.concatenate([k_s[kv, parity, keys], kx_ref[keys]], axis=1)
                s = dot_nt(q, k)
                top = jnp.max(s, axis=1, keepdims=True)
                p = jnp.exp(s - top)
                norm = jnp.sum(p, axis=1, keepdims=True)
                far = top + jnp.log(norm)
                near = jnp.sum(jnp.where(lane == head, stats, 0.0), axis=1, keepdims=True)
                both = jnp.maximum(near, far)
                both = both + jnp.log(jnp.exp(near - both) + jnp.exp(far - both))
                out = dot_nn(p.astype(bf16), v_s[kv, parity, keys]) * jnp.exp(top - both)
                total = out if total is None else total + out
                weight = jnp.exp(near - both)
                scale = weight if scale is None else jnp.where(lane < HEAD, scale, weight)
                stats = jnp.where(lane == head, both, stats)
            o_ref[rows] = (near_ref[rows] * scale + total).astype(bf16)
            lse_s[rows] = stats

    @pl.when(half_ref[0] == 0)
    def _():
        first = slice(0, block)
        o_ref[first] = near_ref[first].astype(bf16)
        run((1,), slice(0, tokens))

    @pl.when(half_ref[0] != 0)
    def _():
        run((0, 1), slice(0, block))

    @pl.when(step == pl.num_programs(0) - 1)
    def _():
        lse_ref[...] = lse_s[...].T


def near_forward(q, qx, kv, kx, group):
    tokens, width = q.shape
    column = pl.BlockSpec((tokens, LANES), lambda p: (0, p))
    whole = lambda *shape: pl.BlockSpec(shape, lambda p: (0, 0))
    spare = lambda: pltpu.VMEM((2, 2, tokens, LANES), bf16)
    return pl.pallas_call(
        functools.partial(near_forward_kernel, group=group),
        grid=(width // LANES,),
        in_specs=[column, whole(tokens, LANES), whole(tokens, 2 * LANES), whole(tokens, LANES)],
        out_specs=[column, whole(tokens, LANES)],
        scratch_shapes=[spare(), spare()],
        out_shape=[
            jax.ShapeDtypeStruct((tokens, width), f32),
            jax.ShapeDtypeStruct((tokens, LANES), f32),
        ],
        compiler_params=pltpu.CompilerParams(vmem_limit_bytes=62 * MIB),
        cost_estimate=HEAVY,
        name="attention_near",
    )(q, qx, kv, kx)


def far_forward(half, q, qx, kv, kx, near, stats, group):
    tokens, width = q.shape
    column = pl.BlockSpec((tokens, LANES), lambda p, *_: (0, p))
    whole = lambda *shape: pl.BlockSpec(shape, lambda p, *_: (0, 0))
    spare = lambda: pltpu.VMEM((2, 2, tokens, LANES), bf16)
    return pl.pallas_call(
        functools.partial(far_forward_kernel, group=group),
        grid_spec=pltpu.PrefetchScalarGridSpec(
            num_scalar_prefetch=1,
            grid=(width // LANES,),
            in_specs=[
                column,
                whole(tokens, LANES),
                whole(tokens, 2 * LANES),
                whole(tokens, LANES),
                column,
                whole(tokens, LANES),
            ],
            out_specs=[column, whole(LANES, tokens)],
            scratch_shapes=[spare(), spare(), pltpu.VMEM((tokens, LANES), f32)],
        ),
        out_shape=[
            jax.ShapeDtypeStruct((tokens, width), bf16),
            jax.ShapeDtypeStruct((LANES, tokens), f32),
        ],
        compiler_params=pltpu.CompilerParams(vmem_limit_bytes=62 * MIB),
        cost_estimate=LIGHT,
        name="attention_far",
    )(half, q, qx, kv, kx, near, stats)


def back_block(q, q_wide, g, lse, delta, k, kx, turned, v, masked):
    s = dot_nt(jnp.concatenate([k, kx], axis=1), q_wide)
    if masked:
        s = causal(s, True)
    p = jnp.exp(s - lse)
    ds = (p * (dot_nt(v, g) - delta)).astype(bf16)
    return dot_nn(p.astype(bf16), g), dot_nn(ds, q), dot_nn(turned, ds)


def gather_heads(acc, out_ref, columns):
    low = lax.broadcasted_iota(jnp.int32, acc.shape[2:], 1) < HEAD
    first = acc[0, 0] + pltpu.roll(acc[0, 1], HEAD, 1)
    second = acc[1, 1] + pltpu.roll(acc[1, 0], HEAD, 1)
    out_ref[:, columns] = jnp.where(low, first, second).astype(out_ref.dtype)


def far_backward_kernel(half_ref, q_ref, qx_ref, g_ref, o_ref, lse_ref, kv_ref, kx_ref, dq_ref, dkv_ref, k_s, t_s, v_s, ka, va, *, group):
    step = pl.program_id(0)
    tokens = q_ref.shape[0]
    block = tokens // 2
    keys, values = slice(0, LANES), slice(LANES, 2 * LANES)

    @pl.when(step == 0)
    def _():
        spread(kv_ref, keys, k_s, t_s)
        spread(kv_ref, values, v_s)
        ka[...] = jnp.zeros_like(ka)
        va[...] = jnp.zeros_like(va)

    def run(blocks, key_blocks):
        for b in blocks:
            rows = slice(b * block, (b + 1) * block)
            q = q_ref[rows]
            q_wide = jnp.concatenate([q, qx_ref[rows]], axis=1)
            g = g_ref[rows]
            product = (g.astype(f32) * o_ref[rows].astype(f32)).T
            total = None
            for parity in range(2):
                head = 2 * step + parity
                kv = head // group
                lse = lse_ref[pl.ds(head, 1), rows]
                delta = jnp.sum(product[parity * HEAD : (parity + 1) * HEAD], axis=0, keepdims=True)
                for c in key_blocks:
                    part = slice(c * block, (c + 1) * block)
                    dv, dk, dq = back_block(
                        q, q_wide, g, lse, delta, k_s[kv, parity, part], kx_ref[part],
                        t_s[kv, parity, :, part], v_s[kv, parity, part], False,
                    )
                    va[kv, parity, part] += dv
                    ka[kv, parity, part] += dk
                    total = dq if total is None else total + dq
            dq_ref[:, rows] = total

    @pl.when(half_ref[0] == 0)
    def _():
        dq_ref[:, :block] = jnp.zeros((LANES, block), f32)
        run((1,), (0, 1))

    @pl.when(half_ref[0] != 0)
    def _():
        run((0, 1), (0,))

    @pl.when(step == pl.num_programs(0) - 1)
    def _():
        gather_heads(ka, dkv_ref, keys)
        gather_heads(va, dkv_ref, values)


def near_backward_kernel(q_ref, qx_ref, g_ref, o_ref, lse_ref, cos_ref, sin_ref, kv_ref, kx_ref, far_ref, dq_ref, dkv_ref, k_s, t_s, v_s, ka, va, *, group):
    step = pl.program_id(0)
    tokens = q_ref.shape[0]
    block = tokens // 2
    keys, values = slice(0, LANES), slice(LANES, 2 * LANES)

    @pl.when(step == 0)
    def _():
        spread(kv_ref, keys, k_s, t_s)
        spread(kv_ref, values, v_s)
        ka[...] = jnp.zeros_like(ka)
        va[...] = jnp.zeros_like(va)

    for b in range(2):
        rows = slice(b * block, (b + 1) * block)
        q = q_ref[rows]
        q_wide = jnp.concatenate([q, qx_ref[rows]], axis=1)
        g = g_ref[rows]
        product = (g.astype(f32) * o_ref[rows].astype(f32)).T
        total = far_ref[:, rows]
        for parity in range(2):
            head = 2 * step + parity
            kv = head // group
            lse = lse_ref[pl.ds(head, 1), rows]
            delta = jnp.sum(product[parity * HEAD : (parity + 1) * HEAD], axis=0, keepdims=True)
            for c in range(b + 1):
                part = slice(c * block, (c + 1) * block)
                dv, dk, dq = back_block(
                    q, q_wide, g, lse, delta, k_s[kv, parity, part], kx_ref[part],
                    t_s[kv, parity, :, part], v_s[kv, parity, part], c == b,
                )
                va[kv, parity, part] += dv
                ka[kv, parity, part] += dk
                total = total + dq
        dq_ref[rows] = turn_back(total.T * (HEAD**-0.5), cos_ref[rows], sin_ref[rows]).astype(bf16)

    @pl.when(step == pl.num_programs(0) - 1)
    def _():
        gather_heads(ka, dkv_ref, keys)
        gather_heads(va, dkv_ref, values)


ANYWHERE = pl.BlockSpec(memory_space=pl.ANY)


def alike(arrays):
    return [jax.ShapeDtypeStruct(array.shape, array.dtype) for array in arrays]


def backward_scratch(tokens):
    return [
        pltpu.VMEM((2, 2, tokens, LANES), bf16),
        pltpu.VMEM((2, 2, LANES, tokens), bf16),
        pltpu.VMEM((2, 2, tokens, LANES), bf16),
        pltpu.VMEM((2, 2, tokens, LANES), f32),
        pltpu.VMEM((2, 2, tokens, LANES), f32),
    ]


def far_backward(half, q, qx, g, o, lse, kv, kx, group, through):
    tokens, width = q.shape
    column = pl.BlockSpec((tokens, LANES), lambda p, *_: (0, p))
    across = pl.BlockSpec((LANES, tokens), lambda p, *_: (p, 0))
    whole = lambda *shape: pl.BlockSpec(shape, lambda p, *_: (0, 0))
    return pl.pallas_call(
        functools.partial(dropping(dropping(far_backward_kernel, 10, len(through)), 8, len(through)), group=group),
        grid_spec=pltpu.PrefetchScalarGridSpec(
            num_scalar_prefetch=1,
            grid=(width // LANES,),
            in_specs=[
                column,
                whole(tokens, LANES),
                column,
                column,
                whole(LANES, tokens),
                whole(tokens, 2 * LANES),
                whole(tokens, LANES),
            ]
            + [ANYWHERE] * len(through),
            out_specs=[across, whole(tokens, 2 * LANES)] + [ANYWHERE] * len(through),
            scratch_shapes=backward_scratch(tokens),
        ),
        out_shape=[
            jax.ShapeDtypeStruct((width, tokens), f32),
            jax.ShapeDtypeStruct((tokens, 2 * LANES), bf16),
            *alike(through),
        ],
        input_output_aliases={8 + i: 2 + i for i in range(len(through))},
        compiler_params=pltpu.CompilerParams(vmem_limit_bytes=64 * MIB - 65536),
        cost_estimate=LIGHT,
        name="attention_far_back",
    )(half, q, qx, g, o, lse, kv, kx, *through)


def near_backward(q, qx, g, o, lse, cosines, sines, kv, kx, far, group, others):
    tokens, width = q.shape
    column = pl.BlockSpec((tokens, LANES), lambda p: (0, p))
    across = pl.BlockSpec((LANES, tokens), lambda p: (p, 0))
    whole = lambda *shape: pl.BlockSpec(shape, lambda p: (0, 0))
    return pl.pallas_call(
        functools.partial(dropping(near_backward_kernel, 10, len(others)), group=group),
        grid=(width // LANES,),
        in_specs=[
            column,
            whole(tokens, LANES),
            column,
            column,
            whole(LANES, tokens),
            whole(tokens, LANES),
            whole(tokens, LANES),
            whole(tokens, 2 * LANES),
            whole(tokens, LANES),
            across,
        ]
        + [ANYWHERE] * len(others),
        out_specs=[column, whole(tokens, 2 * LANES)],
        scratch_shapes=backward_scratch(tokens),
        out_shape=[
            jax.ShapeDtypeStruct((tokens, width), bf16),
            jax.ShapeDtypeStruct((tokens, 2 * LANES), f32),
        ],
        compiler_params=pltpu.CompilerParams(vmem_limit_bytes=64 * MIB - 65536),
        cost_estimate=LIGHT,
        name="attention_near_back",
    )(q, qx, g, o, lse, cosines, sines, kv, kx, far, *others)


def weight_grads_kernel(at_ref, normed_ref, dq_ref, dkv_ref, got_ref, cos_ref, sin_ref, branch_ref, att_ref, project_ref, mine_ref, theirs_ref, bias_ref):
    kv = dkv_ref[...] + got_ref[...].astype(f32)
    keys = turn_back(kv[:, :LANES], cos_ref[...], sin_ref[...])
    project = jnp.concatenate([dq_ref[...], keys.astype(bf16), kv[:, LANES:].astype(bf16)], axis=1)
    project_ref[...] = project
    bias = jnp.sum(project.astype(f32), axis=0, keepdims=True)
    bias_ref[...] = bias
    core, inner, line, seq = (at_ref[i] for i in range(4))
    width = normed_ref.shape[1]
    chips = 8
    piece = width // chips // 2
    normed_t, att_t = normed_ref[...].T, att_ref[...].T
    columns = [(normed_t, project[:, s : s + LANES]) for s in range(0, project.shape[1], LANES)]
    columns += [(att_t, branch_ref[:, s : s + LANES]) for s in range(0, width, LANES)]
    for pair in range(len(columns) // 2):
        (left, one), (other, two) = columns[2 * pair : 2 * pair + 2]
        if left is other:
            value = dot_nn(left, jnp.concatenate([one, two], axis=1))
            one, two = value[:, :LANES], value[:, LANES:]
        else:
            one, two = dot_nn(left, one), dot_nn(other, two)
        quarter = pair // 2
        half = (quarter % 2) ^ seq
        start = quarter // 2 * (4 * piece + 16) + pair % 2 * 2 * piece
        for chip in range(chips):
            rows = slice(chip * 2 * piece, (chip + 1) * 2 * piece)
            here, there = one[rows], two[rows]
            low = jnp.concatenate([here[:piece], there[:piece]], axis=0)
            high = jnp.concatenate([here[piece:], there[piece:]], axis=0)
            away = (chip // 2) ^ line
            place = 2 * (away % 2) + away // 2
            for ref, first in ((mine_ref, core == 0), (theirs_ref, core != 0)):
                value = jnp.where(first, low, high).astype(bf16)
                ref[(chip % 2) ^ inner, half, place, start : start + 2 * piece, :] = value
    row = lax.broadcasted_iota(jnp.int32, (16, LANES), 0)
    last = bias[:, project.shape[1] - LANES :]
    for chip in range(chips):
        away = (chip // 2) ^ line
        place = 2 * (away % 2) + away // 2
        first = bias[:, chip * LANES : (chip + 1) * LANES]
        value = jnp.where(row == 0, first, jnp.where(row == 1, last, 0.0)).astype(bf16)
        for ref in (mine_ref, theirs_ref):
            for half in range(2):
                ref[(chip % 2) ^ inner, half, place, 4 * piece : 4 * piece + 16, :] = value
                ref[(chip % 2) ^ inner, half, place, 8 * piece + 16 :, :] = value


def weight_grads(at, normed, dq, dkv, got, cosines, sines, branch, attended, outs, others):
    tokens, width = normed.shape
    rows = (outs + width) // LANES * (width // 16) // 2 + 32
    packed = jax.ShapeDtypeStruct((2, 2, 4, rows, LANES), bf16)
    out_shape = [
        jax.ShapeDtypeStruct((tokens, outs), bf16),
        packed,
        packed,
        jax.ShapeDtypeStruct((1, outs), f32),
    ]
    args = (normed, dq, dkv, got, cosines, sines, branch, attended)
    whole = lambda array: pl.BlockSpec(array.shape, lambda i, *_: (0,) * len(array.shape))
    return pl.pallas_call(
        dropping(weight_grads_kernel, 9, len(others)),
        grid_spec=pltpu.PrefetchScalarGridSpec(
            num_scalar_prefetch=1,
            grid=(1,),
            in_specs=[whole(array) for array in args] + [ANYWHERE] * len(others),
            out_specs=[whole(array) for array in out_shape],
        ),
        out_shape=out_shape,
        compiler_params=pltpu.CompilerParams(vmem_limit_bytes=64 * MIB - 65536),
        cost_estimate=LIGHT,
        name="weight_grads",
    )(at, *args, *others)


def store_half(value, kept_ref, sent_ref):
    for step, ref in enumerate((kept_ref, sent_ref)):

        @pl.when(pl.program_id(0) == step)
        def _(ref=ref):
            ref[...] = value


def input_grad_kernel(at_ref, x_ref, gain_ref, project_ref, w_ref, gm_ref, kept_ref, sent_ref):
    grad = dot_nt(project_ref[...], w_ref[...]) * gain_ref[...]
    x = x_ref[...].astype(f32)
    scale = lax.rsqrt(jnp.mean(x * x, axis=1, keepdims=True) + EPSILON)
    normal = x * scale
    mean = jnp.mean(grad * normal, axis=1, keepdims=True)
    store_half((gm_ref[...] + scale * (grad - normal * mean)).astype(bf16), kept_ref, sent_ref)


def input_grad(half, x, gain, project, weight, grad_middle, others):
    tokens, width = x.shape
    outs = weight.shape[1]
    rows = tokens // 2
    row = lambda cols: pl.BlockSpec((rows, cols), lambda i, half: (i ^ half[0], 0))
    whole = lambda *shape: pl.BlockSpec(shape, lambda i, half: (0, 0))
    return pl.pallas_call(
        dropping(input_grad_kernel, 6, len(others)),
        grid_spec=pltpu.PrefetchScalarGridSpec(
            num_scalar_prefetch=1,
            grid=(2,),
            in_specs=[row(width), whole(1, width), row(outs), whole(width, outs), row(width)]
            + [ANYWHERE] * len(others),
            out_specs=[whole(rows, width)] * 2,
        ),
        out_shape=[jax.ShapeDtypeStruct((rows, width), bf16)] * 2,
        compiler_params=pltpu.CompilerParams(vmem_limit_bytes=64 * MIB - 65536),
        cost_estimate=SHORT,
        name="input_grad",
    )(half, x, gain, project, weight, grad_middle, *others)


def out_project_kernel(x_ref, att_ref, gain_ref, w_ref, middle_ref, normed_ref, out_ref, raw_s, w_s, sem, *, start):
    step = pl.program_id(0)

    @pl.when(step == 0)
    def _():
        if start is None:
            w_s[...] = w_ref[...]
        else:
            copy = pltpu.make_async_copy(w_ref.at[:, pl.ds(start, raw_s.shape[1]), :], raw_s, sem)
            copy.start()
            copy.wait()
            width = w_s.shape[0]
            depth = width // raw_s.shape[0]
            for c in range(width // LANES):
                rows = raw_s[:, c * depth : (c + 1) * depth, :].astype(f32)
                w_s[:, c * LANES : (c + 1) * LANES] = rows.reshape(width, LANES).astype(bf16)
        out_ref[...] = w_s[...]

    middle = x_ref[...].astype(f32) + dot_nn(att_ref[...], w_s[...])
    middle_ref[...] = middle
    scale = lax.rsqrt(jnp.mean(middle * middle, axis=1, keepdims=True) + EPSILON)
    normed_ref[...] = (middle * scale * gain_ref[...]).astype(bf16)


def out_project(x, attended, gain, weight, start, rows):
    tokens, width = x.shape
    part = tokens // 3
    row = pl.BlockSpec((part, width), lambda i: (i, 0))
    whole = lambda *shape: pl.BlockSpec(shape, lambda i: (0, 0))
    raw = start is not None
    return pl.pallas_call(
        functools.partial(out_project_kernel, start=start),
        grid=(3,),
        in_specs=[
            row,
            row,
            whole(1, width),
            pl.BlockSpec(memory_space=pl.ANY) if raw else whole(width, width),
        ],
        out_specs=[row, row, whole(width, width)],
        out_shape=[
            jax.ShapeDtypeStruct((tokens, width), f32),
            jax.ShapeDtypeStruct((tokens, width), bf16),
            jax.ShapeDtypeStruct((width, width), bf16),
        ],
        scratch_shapes=[
            pltpu.VMEM((weight.shape[0], rows, LANES) if raw else (8, LANES), bf16),
            pltpu.VMEM((width, width), bf16),
            pltpu.SemaphoreType.DMA,
        ],
        compiler_params=pltpu.CompilerParams(vmem_limit_bytes=62 * MIB),
        cost_estimate=LIGHT,
        name="out_project",
    )(x, attended, gain, weight)


def middle_back_kernel(at_ref, o1_ref, o2_ref, o3_ref, o4_ref, g1_ref, g2_ref, g3_ref, g4_ref, middle_ref, gout_ref, gain_ref, w_ref, kept_ref, sent_ref, gm_ref, branch_ref, gatt_ref):
    middle = middle_ref[...]
    added = sum(ref[...].astype(f32) for ref in (o1_ref, o2_ref, o3_ref, o4_ref))
    store_half((middle + added).astype(bf16), kept_ref, sent_ref)
    grad = sum(ref[...].astype(f32) for ref in (g1_ref, g2_ref, g3_ref, g4_ref))
    grad = grad * gain_ref[...]
    scale = lax.rsqrt(jnp.mean(middle * middle, axis=1, keepdims=True) + EPSILON)
    normal = middle * scale
    mean = jnp.mean(grad * normal, axis=1, keepdims=True)
    grad = gout_ref[...].astype(f32) + scale * (grad - normal * mean)
    gm_ref[...] = grad
    branch = grad.astype(bf16)
    branch_ref[...] = branch
    gatt_ref[...] = dot_nt(branch, w_ref[...]).astype(bf16)


def middle_back(half, terms, middle, grad_out, gain, weight, others, through):
    tokens, width = middle.shape
    rows = tokens // 2
    row = pl.BlockSpec((rows, width), lambda i, half: (i ^ half[0], 0))
    below = pl.BlockSpec((rows, width), lambda i, half: (2 + (i ^ half[0]), 0))
    whole = lambda *shape: pl.BlockSpec(shape, lambda i, half: (0, 0))
    shape = lambda kind: jax.ShapeDtypeStruct((tokens, width), kind)
    return pl.pallas_call(
        dropping(dropping(middle_back_kernel, 18, len(through)), 13, len(others) + len(through)),
        grid_spec=pltpu.PrefetchScalarGridSpec(
            num_scalar_prefetch=1,
            grid=(2,),
            in_specs=[row] * 4
            + [below] * 4
            + [row, row, whole(1, width), whole(width, width)]
            + [ANYWHERE] * (len(others) + len(through)),
            out_specs=[whole(rows, width)] * 2 + [row] * 3 + [ANYWHERE] * len(through),
        ),
        out_shape=[jax.ShapeDtypeStruct((rows, width), bf16)] * 2 + [shape(f32), shape(bf16), shape(bf16)] + alike(through),
        input_output_aliases={13 + len(others) + i: 5 + i for i in range(len(through))},
        compiler_params=pltpu.CompilerParams(vmem_limit_bytes=64 * MIB - 65536),
        cost_estimate=LIGHT,
        name="middle_back",
    )(half, *terms, *terms, middle, grad_out, gain, weight, *others, *through)


LINE = (0, 2, 1, 3)


def mlp_kernel(at_ref, near_ref, far_ref, gnear_ref, gfar_ref, *rest, counts, tiles, first, split):
    w_refs, rest = rest[: len(counts)], rest[len(counts) :]
    own_ref, other_ref, keep_x, send_x, keep_y, send_y = rest[:6]
    n_s, t_s, g_s, p_s, out_s, grad_s, gate_s, up_s, down_s = rest[6:]
    step = pl.program_id(0)
    tile = 2 * (first + step) + at_ref[0]
    tokens, width = near_ref.shape
    shards = w_refs[0].shape[0]
    depth = width // shards
    own = TILE // shards
    chips = shards // 2

    @pl.when(step == 0)
    def _():
        n_s[:tokens] = near_ref[...]
        n_s[tokens:] = far_ref[...]
        g_s[:tokens] = gnear_ref[...]
        g_s[tokens:] = gfar_ref[...]
        t_s[:, :tokens] = near_ref[...].T
        t_s[:, tokens:] = far_ref[...].T
        out_s[...] = jnp.zeros_like(out_s)
        grad_s[...] = jnp.zeros_like(grad_s)

    def load(w_ref):
        for at, square in ((0, gate_s), (2 * depth, up_s)):
            for c in range(TILE // LANES):
                rows = w_ref[:, at + c * depth : at + (c + 1) * depth, :]
                rows = rows.astype(f32).reshape(width, LANES).astype(bf16)
                square[:, c * LANES : (c + 1) * LANES] = rows
        for c in range(width // LANES):
            rows = w_ref[:, 4 * depth + c * own : 4 * depth + (c + 1) * own, :]
            down_s[:, c * LANES : (c + 1) * LANES] = rows.reshape(TILE, LANES)

    begin = 0
    for w_ref, many in zip(w_refs, counts):
        pl.when((step >= begin) & (step < begin + many))(functools.partial(load, w_ref))
        begin += many

    @pl.when(tile >= tiles)
    def _():
        p_s[...] = jnp.zeros_like(p_s)

    @pl.when(tile < tiles)
    def _():
        gate_w, up_w, down_w = gate_s[...], up_s[...], down_s[...]
        n = n_s[...]
        g = g_s[...]
        gate = dot_nn(n, gate_w)
        up = dot_nn(n, up_w)
        grad_hidden = dot_nt(g, down_w)
        sig = 1.0 / (1.0 + jnp.exp(-gate))
        silu = gate * sig
        hidden = (silu * up).astype(bf16)
        grad_gate = (grad_hidden * up * (sig + silu * (1.0 - sig))).astype(bf16)
        grad_up = (grad_hidden * silu).astype(bf16)
        out_s[...] += dot_nn(hidden, down_w)
        grad_s[...] += dot_nt(grad_gate, gate_w) + dot_nt(grad_up, up_w)
        for at, value in ((0, dot_nn(t_s[...], grad_gate)), (1, dot_nn(t_s[...], grad_up))):
            for c in range(TILE // LANES):
                part = value[:, c * LANES : (c + 1) * LANES].astype(bf16)
                start = (2 * at + c) * 2 * depth
                p_s[:, start : start + 2 * depth, :] = part.reshape(chips, 2 * depth, LANES)
        down = dot_tn(hidden, g)
        for c in range(width // LANES):
            part = down[:, c * LANES : (c + 1) * LANES].astype(bf16)
            start = 8 * depth + c * 2 * own
            p_s[:, start : start + 2 * own, :] = part.reshape(chips, 2 * own, LANES)

    half_rows = 6 * depth
    inner, line, seq = at_ref[1], at_ref[2], at_ref[3]

    def piece(line_off, inner_off, half_off):
        chip = 2 * (line ^ line_off) + (inner ^ inner_off)
        start = pl.multiple_of((seq ^ half_off) * half_rows, half_rows)
        return p_s[chip, pl.ds(start, half_rows), :]

    @pl.when(step < split)
    def _():
        for a, off in enumerate(LINE):
            for h in range(2):
                keep_x[h, a] = piece(off, 0, h)
                send_x[h, a] = piece(off, 1, h)

    @pl.when(step >= split)
    def _():
        for a, off in enumerate(LINE):
            for b in range(2):
                keep_y[b, a] = piece(off, b, 0)
                send_y[b, a] = piece(off, b, 1)

    @pl.when(step == pl.num_programs(0) - 1)
    def _():
        for ref, rows in ((own_ref, slice(0, tokens)), (other_ref, slice(tokens, 2 * tokens))):
            ref[:tokens] = out_s[rows].astype(bf16)
            ref[tokens:] = grad_s[rows].astype(bf16)


def mlp_call(at, near, far, gnear, gfar, weights, counts, tiles, first, split):
    tokens, width = near.shape
    shards = weights[0][0].shape[0]
    rows = 6 * width // shards
    count = sum(counts)
    whole = lambda *shape: pl.BlockSpec(shape, lambda j, *_: (0,) * len(shape))
    early = pl.BlockSpec((2, 4, rows, LANES), lambda j, *_: (0, 0, jnp.minimum(j, split - 1), 0))
    late = pl.BlockSpec((2, 4, rows, LANES), lambda j, *_: (0, 0, jnp.maximum(j - split, 0), 0))
    shape_x = jax.ShapeDtypeStruct((2, 4, rows * split, LANES), bf16)
    shape_y = jax.ShapeDtypeStruct((2, 4, rows * (count - split), LANES), bf16)
    wide = jax.ShapeDtypeStruct((2 * tokens, width), bf16)

    def block_of(index):
        return pl.BlockSpec((shards, rows, LANES), lambda j, at: (0, index(j, at), 0))

    return pl.pallas_call(
        functools.partial(mlp_kernel, counts=counts, tiles=tiles, first=first, split=split),
        grid_spec=pltpu.PrefetchScalarGridSpec(
            num_scalar_prefetch=1,
            grid=(count,),
            in_specs=[whole(tokens, width)] * 4 + [block_of(index) for _, index in weights],
            out_specs=[whole(2 * tokens, width)] * 2 + [early, early, late, late],
            scratch_shapes=[
                pltpu.VMEM((2 * tokens, width), bf16),
                pltpu.VMEM((width, 2 * tokens), bf16),
                pltpu.VMEM((2 * tokens, width), bf16),
                pltpu.VMEM((shards // 2, 2 * rows, LANES), bf16),
                pltpu.VMEM((2 * tokens, width), f32),
                pltpu.VMEM((2 * tokens, width), f32),
                pltpu.VMEM((width, TILE), bf16),
                pltpu.VMEM((width, TILE), bf16),
                pltpu.VMEM((TILE, width), bf16),
            ],
        ),
        out_shape=[
            wide,
            wide,
            shape_x,
            shape_x,
            shape_y,
            shape_y,
        ],
        compiler_params=pltpu.CompilerParams(vmem_limit_bytes=64 * MIB - 65536),
        cost_estimate=HEAVY,
        name="feed_forward",
    )(at, near, far, gnear, gfar, *(w for w, _ in weights))


def pack_kernel(half_ref, gate_ref, up_ref, down_ref, out_ref, one_ref, two_ref, *, shards, early, shared):
    depth, hidden = gate_ref.shape
    width = down_ref.shape[1]
    tiles = hidden // TILE
    own = TILE // shards
    rows = 6 * depth
    per = LANES // own
    lane = lax.broadcasted_iota(jnp.int32, (depth, LANES), 1) // own

    def write(target, at, blocks, tile):
        target[at : at + 4 * depth, :] = blocks
        for c in range(width // LANES):
            start = at + 4 * depth + c * own
            target[start : start + own, :] = down_ref[tile * own : (tile + 1) * own, c * LANES : (c + 1) * LANES]

    for tile in range(tiles):
        blocks = []
        for ref in (gate_ref, up_ref):
            for c in range(TILE // LANES):
                total = None
                by_shift = {}
                for i in range(per):
                    at = ((c * per + i) * tiles + tile) * own
                    by_shift.setdefault((i - at // own) % per, []).append((i, at // LANES))
                for shift, sources in by_shift.items():
                    value = None
                    for i, block in sources:
                        part = ref[:, block * LANES : (block + 1) * LANES].astype(f32)
                        here = lane == (i - shift) % per
                        value = part if value is None else jnp.where(here, part, value)
                    if shift:
                        value = pltpu.roll(value, shift * own, 1)
                    if total is None:
                        total = value
                    else:
                        for i, _ in sources:
                            total = jnp.where(lane == i, value, total)
                blocks.append(total)
        blocks = jnp.concatenate(blocks, axis=0).astype(bf16)
        if tile < early:
            write(one_ref, tile * rows, blocks, tile)
        elif tile < early + 2 * shared:
            which, at = divmod(tile - early, shared)
            pl.when(half_ref[0] == which)(
                functools.partial(write, one_ref, (early + at) * rows, blocks, tile)
            )
        else:
            write(two_ref, (tile - early - 2 * shared) * rows, blocks, tile)
    pieces = [out_ref[:, c * LANES : (c + 1) * LANES].astype(f32) for c in range(width // LANES)]
    at = (early + shared) * rows
    rest = one_ref.shape[0] - at - len(pieces) * depth
    if rest:
        pieces.append(jnp.zeros((rest, LANES), f32))
    one_ref[at:, :] = jnp.concatenate(pieces, axis=0).astype(bf16)


def out_rows(width, depth):
    return -(-(width // LANES * depth) // 16) * 16


def pack_call(half, w_gate, w_up, w_down, w_out, shards, early, shared):
    depth, hidden = w_gate.shape
    width = w_down.shape[1]
    rows = 6 * depth
    tiles = hidden // TILE
    sizes = (early + shared) * rows + out_rows(width, depth), (tiles - early - 2 * shared) * rows
    whole = lambda shape: pl.BlockSpec(shape, lambda i, *_: (0, 0))
    return pl.pallas_call(
        functools.partial(pack_kernel, shards=shards, early=early, shared=shared),
        grid_spec=pltpu.PrefetchScalarGridSpec(
            num_scalar_prefetch=1,
            grid=(1,),
            in_specs=[whole(w.shape) for w in (w_gate, w_up, w_down, w_out)],
            out_specs=[whole((n, LANES)) for n in sizes],
        ),
        out_shape=[jax.ShapeDtypeStruct((n, LANES), bf16) for n in sizes],
        compiler_params=pltpu.CompilerParams(vmem_limit_bytes=62 * MIB),
        cost_estimate=LIGHT,
        name="pack",
    )(half, w_gate, w_up, w_down, w_out)


def unpack_kernel(at_ref, *refs, shards, cuts):
    chunks = [refs[:4], refs[4:8]]
    wg_ref, wu_ref, gate_ref, up_ref, down_ref, gain_ref, *scratch = refs[8:]
    depth, hidden = gate_ref.shape
    width = down_ref.shape[1]
    tiles = hidden // TILE
    own = TILE // shards
    per = LANES // own
    half_rows = 6 * depth
    core, seq = at_ref[0], at_ref[3]
    for (a, b, c, d), ref in zip(chunks, scratch):
        ref[core, seq] = a[...]
        ref[core, 1 - seq] = b[...]
        ref[1 - core, seq] = c[...]
        ref[1 - core, 1 - seq] = d[...]
    counts = [3 * sum(cut) // half_rows for cut in cuts]

    def rows_of(tile, half, start, size):
        at = tile // 2
        chunk = at >= counts[0]
        at -= counts[0] * chunk
        first, second = cuts[chunk]
        place = at * half_rows + start
        begin, cut = 0, first
        if place >= 3 * first:
            place, begin, cut = place - 3 * first, first, second

        def line_of(place):
            block, place = divmod(place, cut)
            return block * (first + second) + begin + place

        if size == depth:
            row = line_of(place)
            both = scratch[chunk][tile % 2, half, row : row + 2 * size, :].astype(f32)
            low, high = both[:size], both[size:]
        else:
            low, high = (
                scratch[chunk][tile % 2, half, row : row + size, :].astype(f32)
                for row in (line_of(place), line_of(place + size))
            )
        return jnp.where(core == 0, low, high)

    lane = lax.broadcasted_iota(jnp.int32, (depth, LANES), 1) // own
    wide = [[rows_of(tile, at // 3, at % 3 * 2 * depth, depth) for at in range(4)] for tile in range(tiles)]
    gain = jnp.zeros((depth, LANES), f32)
    for number, (ref, weight_ref) in enumerate(((gate_ref, wg_ref), (up_ref, wu_ref))):
        for block in range(hidden // LANES):
            total = None
            for i in range(per):
                shard, tile = divmod(block * per + i, tiles)
                c, at = divmod(shard, per)
                value = wide[tile][2 * number + c]
                if (i - at) % per:
                    value = pltpu.roll(value, (i - at) % per * own, 1)
                total = value if total is None else jnp.where(lane == i, value, total)
            columns = slice(block * LANES, (block + 1) * LANES)
            ref[:, columns] = total
            gain = gain + total * weight_ref[:, columns].astype(f32)
    gain_ref[...] = gain
    for tile in range(tiles):
        for c in range(width // LANES):
            value = rows_of(tile, 1, 2 * depth + c * 2 * own, own)
            down_ref[tile * own : (tile + 1) * own, c * LANES : (c + 1) * LANES] = value


def unpack_call(at, chunks, cuts, w_gate, w_up, shards):
    depth, hidden = w_gate.shape
    tiles = hidden // TILE
    own = TILE // shards
    width = depth * shards
    args = [piece for chunk in chunks for piece in chunk] + [w_gate, w_up]
    out_shape = [
        jax.ShapeDtypeStruct((depth, hidden), f32),
        jax.ShapeDtypeStruct((depth, hidden), f32),
        jax.ShapeDtypeStruct((tiles * own, width), f32),
        jax.ShapeDtypeStruct((depth, LANES), f32),
    ]
    whole = lambda array: pl.BlockSpec(array.shape, lambda i, *_: (0, 0))
    return pl.pallas_call(
        functools.partial(unpack_kernel, shards=shards, cuts=cuts),
        grid_spec=pltpu.PrefetchScalarGridSpec(
            num_scalar_prefetch=1,
            grid=(1,),
            in_specs=[whole(array) for array in args],
            out_specs=[whole(array) for array in out_shape],
            scratch_shapes=[pltpu.VMEM((2, 2, *chunk[0].shape), bf16) for chunk in chunks],
        ),
        out_shape=out_shape,
        compiler_params=pltpu.CompilerParams(vmem_limit_bytes=64 * MIB - 65536),
        cost_estimate=LIGHT,
        name="unpack",
    )(at, *args)


def pack_weights(w_gate, w_up, w_down, shards):
    depth, hidden = w_gate.shape
    tiles = hidden // TILE
    own = TILE // shards

    def columns(weight):
        parts = weight.reshape(depth, shards, tiles, own).transpose(0, 2, 1, 3)
        parts = parts.reshape(depth, tiles, TILE // LANES, LANES).transpose(1, 2, 0, 3)
        return parts.reshape(tiles, -1, LANES)

    width = w_down.shape[1]
    down = w_down.reshape(tiles, own, width // LANES, LANES).transpose(0, 2, 1, 3)
    return jnp.concatenate([columns(w_gate), columns(w_up), down.reshape(tiles, -1, LANES)], axis=1)


def unpack_grads(packed, shards, depth):
    tiles = packed.shape[0]
    own = TILE // shards

    def columns(part):
        part = part.reshape(tiles, TILE // LANES, depth, LANES).transpose(2, 0, 1, 3)
        part = part.reshape(depth, tiles, shards, own).transpose(0, 2, 1, 3)
        return part.reshape(depth, tiles * TILE)

    gate, up = columns(packed[:, : 2 * depth]), columns(packed[:, 2 * depth : 4 * depth])
    down = packed[:, 4 * depth :].reshape(tiles, -1, own, LANES).transpose(0, 2, 1, 3)
    return gate, up, down.reshape(tiles * own, -1)


def regroup_weights(gathered, groups, tiles, depth, own):
    shards = gathered.shape[0]
    if shards == groups:
        return gathered
    many = shards // groups
    gathered = gathered.reshape(groups, many, tiles, -1, LANES)
    outs = []
    for start, size in ((0, depth), (2 * depth, depth), (4 * depth, own)):
        stop = start + 2 * depth
        part = gathered[:, :, :, start:stop].reshape(groups, many, tiles, -1, size, LANES)
        outs.append(part.transpose(0, 2, 3, 1, 4, 5).reshape(groups, tiles, -1, LANES))
    return jnp.concatenate(outs, axis=2).reshape(groups, -1, LANES)


class Wires:
    def __init__(self, shards):
        self.shards = shards
        place = lax.axis_index("fsdp")
        self.core = place % 2
        self.inner = (place // 2) % 2
        self.line = place // 4
        self.seq = lax.axis_index("seq")

    def flip(self, values_in, bit):
        return lax.ppermute(values_in, "fsdp", [(i, i ^ bit) for i in range(self.shards)])

    def other_half(self, values_in):
        return lax.ppermute(values_in, "seq", [(0, 1), (1, 0)])


def ordered(bit, own, other):
    return jnp.where(bit == 0, own, other), jnp.where(bit == 0, other, own)


def gather_small(wires, shard, beside):
    if wires.shards != 16:
        return lax.all_gather(shard, "fsdp", axis=0, tiled=False)
    rows = shard.shape[0] // 2
    have = lax.dynamic_slice_in_dim(shard, wires.seq * rows, rows)[None]
    have = jnp.stack(ordered(wires.line // 2, have, wires.flip(have, 8)), axis=0)
    have = jnp.concatenate(ordered(wires.line % 2, have, wires.flip(have, 4)), axis=1)
    have = have.reshape(4, rows, -1)
    beside = beside(have)
    have = jnp.stack(ordered(wires.inner, have, after(wires.flip(have, 2), beside)), axis=1)
    have = jnp.concatenate(ordered(wires.seq, have, wires.other_half(have)), axis=2)
    have = jnp.stack(ordered(wires.core, have, wires.flip(have, 1)), axis=2)
    return have.reshape((16,) + shard.shape)


def pick(values_in, place, axis):
    return lax.dynamic_index_in_dim(values_in, place, axis, keepdims=False)


def plus(*terms):
    return sum(term.astype(f32) for term in terms).astype(bf16)


def after(values_in, others):
    return lax.optimization_barrier((values_in, others))[0]


def sums_kernel(*refs, plan):
    ins = iter(refs)
    for out_ref, parts in zip(refs[sum(map(sum, plan)) :], plan):
        start = 0
        for count in parts:
            total = sum(next(ins)[...].astype(f32) for _ in range(count)).astype(bf16)
            stop = start + total.shape[-2]
            out_ref[..., start:stop, :] = total
            start = stop


def sums(groups, grid=1, others=(), cost=LIGHT, through=()):
    args, in_specs, out_specs, out_shape, plan = [], [], [], [], []
    for parts in groups:
        below = 0
        for terms in parts:
            for array, block, place in terms:
                args.append(array)
                index = lambda i, place=place: (*place[:-2], place[-2] * grid + i, 0)
                in_specs.append(pl.BlockSpec(block, index))
            below += block[-2]
        lead = tuple(n for n in block[:-2] if n is not None)
        out_specs.append(pl.BlockSpec((*lead, below, LANES), lambda i, n=len(lead): (0,) * n + (i, 0)))
        out_shape.append(jax.ShapeDtypeStruct((*lead, below * grid, LANES), bf16))
        plan.append([len(terms) for terms in parts])
    return pl.pallas_call(
        dropping(functools.partial(sums_kernel, plan=plan), len(args), len(others) + len(through)),
        grid=(grid,),
        in_specs=in_specs + [ANYWHERE] * (len(others) + len(through)),
        out_specs=out_specs + [ANYWHERE] * len(through),
        out_shape=out_shape + alike(through),
        input_output_aliases={len(args) + len(others) + i: len(plan) + i for i in range(len(through))},
        compiler_params=pltpu.CompilerParams(vmem_limit_bytes=64 * MIB - 65536),
        cost_estimate=cost,
        name="sums",
    )(*args, *others, *through)


class ChipSum:
    def __init__(self, wires, keep_x, send_x, keep_y, send_y, grid):
        self.wires, self.grid = wires, grid
        self.kept = keep_x, keep_y
        self.got = wires.flip(send_x, 2), wires.other_half(send_y)

    def rows(self, array):
        return array.shape[-2] // self.grid

    def second(self, grid=1):
        whole = lambda array: (array, (None, 4, array.shape[-2] // grid, LANES), (1, 0, 0, 0))
        return [[[whole(k), whole(g)]] for k, g in zip(self.kept, self.got)]

    def second_sent(self, *sent):
        self.sent = sent
        self.next = self.wires.other_half(sent[0]), self.wires.flip(sent[1], 2)

    def third(self):
        groups = []
        for at in (1, 0):
            parts = []
            for k, g, n in zip(self.kept, self.got, self.next):
                old = (None, 2, self.rows(k), LANES), (0, at, 0, 0)
                parts.append([(k, *old), (g, *old), (n, old[0][1:], old[1][1:])])
            groups.append(parts)
        return groups

    def third_sent(self, sent, kept):
        self.sent, self.kept = (sent,), kept
        self.got = self.wires.flip(sent, 4)

    def fourth(self, grid=1):
        block = (None, self.kept.shape[-2] // grid, LANES)
        return [[[(self.kept, block, (1, 0, 0)), (self.got, block, (1, 0, 0))]]]

    def fourth_sent(self, sent):
        self.sent = (sent,)
        self.next = self.wires.flip(sent, 8)

    def fifth(self, grid=1):
        block = (None, self.kept.shape[-2] // grid, LANES)
        terms = [(self.kept, block, (0, 0, 0)), (self.got, block, (0, 0, 0)), (self.next, block[1:], (0, 0))]
        return [[terms]]

    def fifth_sent(self, sent):
        self.sent = (sent,)
        self.got = self.wires.other_half(sent)

    def total(self):
        return ordered(self.wires.seq, self.sent[0], self.got)


def quarters_in(wires, values_in):
    half = values_in.shape[0] // 2
    got = wires.other_half(values_in[half:])
    return jnp.concatenate(ordered(wires.seq, values_in[:half], got), axis=0)


def per_device(
    shards, tokens, seg_ids, first_gain, w_qkv, b_qkv, w_out, second_gain, w_gate, w_up, w_down, cotangent
):
    wires = Wires(shards)
    tokens = tokens[0]
    count, width = tokens.shape
    depth, qkv_width = w_qkv.shape
    kv_width = (qkv_width - width) // 2
    group = (width // HEAD) // (kv_width // HEAD)
    tiles = w_gate.shape[1] // TILE
    own = TILE // shards
    own_bias = b_qkv.shape[0]
    groups = 16
    chips = groups // 2
    full_depth = width // groups
    full_own = TILE // groups
    small_mesh = shards == groups
    half = wires.seq.astype(jnp.int32).reshape(1)
    if small_mesh:
        at = jnp.stack([wires.core, wires.inner, wires.line, wires.seq]).astype(jnp.int32)
    else:
        at = jnp.stack([wires.core] + [jnp.zeros_like(wires.core)] * 3).astype(jnp.int32)
    steps = -(-tiles // 2)
    early, shared = (EARLY, SHARED) if small_mesh else (2 * (steps // 2), 0)

    pad_rows = -(-(depth + 1) // 8) * 8 - depth
    vector = jnp.concatenate([first_gain, b_qkv, second_gain])
    vector = jnp.pad(vector, (0, qkv_width - vector.shape[0]))
    small = jnp.concatenate([w_qkv, jnp.pad(vector[None], ((0, pad_rows - 1), (0, 0)))], axis=0)
    other_segs = wires.other_half(seg_ids)
    tokens = quarters_in(wires, tokens)
    small, (w_gate, w_up, w_down, w_out) = lax.optimization_barrier((small, (w_gate, w_up, w_down, w_out)))
    out_packed = w_out.reshape(depth, width // LANES, LANES).transpose(1, 0, 2).reshape(-1, LANES)
    out_packed = jnp.pad(out_packed, ((0, out_rows(width, depth) - out_packed.shape[0]), (0, 0)))
    if small_mesh:
        packed_one, packed_two = pack_call(
            half, w_gate, w_up, w_down, w_out, shards, early, shared
        )
    else:
        packed = pack_weights(w_gate, w_up, w_down, shards)
        packed_one = jnp.concatenate([packed[:early].reshape(-1, LANES), out_packed], axis=0)
        packed_two = packed[early:].reshape(-1, LANES)
    all_one = lax.all_gather(packed_one, "fsdp", axis=0, tiled=False)
    packed_two = after(packed_two, packed_one)
    all_two = lax.all_gather(packed_two, "fsdp", axis=0, tiled=False)
    block = count // 2

    def tables(seg_ids, other_segs):
        less = lambda k: jnp.sum((seg_ids < k).astype(jnp.int32)) + jnp.sum((other_segs < k).astype(jnp.int32))
        ones, twos = less(1), less(2)
        own_segs = jnp.concatenate(ordered(wires.seq, seg_ids[0, :block], other_segs[0, block:]))
        far_segs = jnp.concatenate(ordered(wires.seq, seg_ids[0, block:], other_segs[0, :block]))
        index = jnp.arange(count, dtype=jnp.int32)
        index = index + jnp.where(wires.seq == 0, jnp.where(index < block, 0, 2 * block), block)
        local_pos = index - jnp.where(own_segs == 0, 0, jnp.where(own_segs == 1, ones, twos))
        inverse = THETA ** (-(jnp.arange(HEAD // 2, dtype=f32) * 2.0 / HEAD))
        angles = local_pos.astype(f32)[:, None] * inverse[None, :]
        cosines, sines = jnp.cos(angles), jnp.sin(angles)
        cosines = jnp.concatenate([cosines] * 4, axis=1)
        sines = jnp.concatenate([-sines, sines] * 2, axis=1)
        doc = jnp.arange(LANES, dtype=jnp.int32)[None, :]
        kx = (own_segs[:, None] == doc).astype(bf16)
        rkx = (far_segs[:, None] == doc).astype(bf16)
        qx = jnp.where((own_segs[:, None] == doc) | (doc >= 3), 0.0, FAR).astype(bf16)
        return cosines, sines, kx, rkx, qx

    made = []

    def beside(started):
        made.extend(tables(*after((seg_ids, other_segs), started)))
        made.append(after(tokens, started))
        return tuple(made)

    small_all = gather_small(wires, small, beside)
    if not made:
        beside(())
    cosines, sines, kx, rkx, qx, tokens = made
    qkv_full = small_all[:, :depth].reshape(width, qkv_width)
    vectors = small_all[:, depth]
    gain_one = vectors[:, :depth].reshape(1, width).astype(f32)
    bias = vectors[:, depth : depth + own_bias].reshape(1, qkv_width).astype(f32)
    gain_two = vectors[:, depth + own_bias : 2 * depth + own_bias].reshape(1, width).astype(f32)

    normed, queries, kv = project_call(tokens, gain_one, qkv_full, bias, cosines, sines)
    far_kv = wires.other_half(kv)
    cotangent = after(cotangent[0], small_all)
    got = wires.other_half(cotangent[block:])
    near, stats = near_forward(queries, qx, kv, kx, group)
    far_kv, got = after((far_kv, got), stats)
    grad_mlp = jnp.concatenate(ordered(wires.seq, cotangent[:block], got), axis=0)
    far_grad = wires.flip(grad_mlp, 1)
    attended, lse = far_forward(half, queries, qx, far_kv, rkx, near, after(stats, grad_mlp), group)
    far_grad = after(far_grad, lse)
    first_rows = all_one.shape[1] - out_packed.shape[0]
    if small_mesh:
        start, out_weight = first_rows, all_one
    else:
        out_weight = all_one[:, first_rows : first_rows + width // LANES * depth]
        out_weight = out_weight.reshape(shards, width // LANES, depth, LANES).transpose(0, 2, 1, 3)
        start, out_weight = None, out_weight.reshape(width, width)
    middle, normed_two, out_full = out_project(
        tokens, attended, gain_two, out_weight, start, out_packed.shape[0]
    )
    far_normed = wires.flip(normed_two, 1)

    if not small_mesh:
        all_one = regroup_weights(all_one[:, :first_rows], groups, early, depth, own)
        all_two = regroup_weights(all_two, groups, tiles - early, depth, own)
    rows = 6 * full_depth
    tokens_in = at, normed_two, far_normed, grad_mlp, far_grad
    own_tile = lambda start, last: lambda j, at: jnp.clip(2 * (j - start) + at[0], 0, last)
    one_steps = early // 2
    two_weights, two_counts = [(all_two, own_tile(shared, tiles - early - 2 * shared - 1))], [steps - one_steps - shared]
    if shared:
        mine = lax.dynamic_slice_in_dim(all_one, (early + wires.core) * rows, rows, axis=1)
        theirs = wires.other_half(mine)
    own_one, other_one, *grads_one = mlp_call(
        *tokens_in, [(all_one, own_tile(0, early - 1))], [one_steps], tiles, 0, one_steps // 2
    )
    if shared:
        both = jnp.concatenate(ordered(wires.seq, mine, after(theirs, own_one)), axis=1)
        two_weights.insert(0, (both, lambda j, at: jnp.minimum(j, shared - 1)))
        two_counts.insert(0, shared)
    if small_mesh:
        sum_one = ChipSum(wires, *grads_one, 3)
    back_one = wires.flip(other_one, 1)
    own_two, other_two, *grads_two = mlp_call(
        *tokens_in, two_weights, two_counts, tiles, one_steps, (steps - one_steps) // 2
    )
    back_two = wires.flip(other_two, 1)
    if small_mesh:
        sum_one.second_sent(*sums(sum_one.second(1), 1, (own_two,), HEAVY))

    others = sum_one.sent if small_mesh else ()
    kept_result, sent_result, grad_middle, branch, grad_attended, *grads_two = middle_back(
        half, (own_one, own_two, back_one, back_two), middle, grad_mlp, gain_two, out_full, others, grads_two
    )
    if small_mesh:
        sum_two = ChipSum(wires, *grads_two, 3)
    far_query, far_kv_grad = far_backward(
        half, queries, qx, grad_attended, attended, lse, far_kv, rkx, group, ()
    )
    got_kv = wires.other_half(far_kv_grad)
    others = ()
    if small_mesh:
        sum_one.third_sent(*sums(sum_one.third(), 3, (far_query,), MIDDLE))
        others = sum_one.sent
    query_grad, kv_grad = near_backward(
        queries, qx, grad_attended, attended, lse, cosines, sines, kv, kx, far_query, group, others
    )
    others = ()
    if small_mesh:
        (sent_one,) = sums(sum_one.fourth(), 1, (query_grad,))
        sum_one.fourth_sent(sent_one)
        *sent_two, sent_result = sums(sum_two.second(), 1, (sent_one, got_kv), through=(sent_result,))
        sum_two.second_sent(*sent_two)
        others = (*sum_two.sent, *sum_one.sent)
    got_result = wires.other_half(sent_result)
    project, mine, theirs, bias_grad = weight_grads(
        at, normed, query_grad, kv_grad, got_kv, cosines, sines, branch, attended, qkv_width, others
    )

    qk_own = (width + kv_width) // shards
    blocks = (qkv_width + width) // LANES
    cut = blocks // 4 * full_depth
    if small_mesh:
        theirs = wires.flip(theirs, 1)
        (sent_one,) = sums(sum_one.fifth(), 1, (project,))
        sum_one.fifth_sent(sent_one)
        kept_grad, sent_grad = input_grad(half, tokens, gain_one, project, qkv_full, grad_middle, (sent_one,))
        first, later = sum_two.third()
        (sent_two,) = sums([first], 3, (kept_grad,), HEAVY)

        def small_groups(part, grid):
            for axis in range(2):
                block, place = [2, 2, 4, (cut + 16) // grid, LANES], [0, 0, 0, axis, 0]
                block[axis], place[axis] = None, part
                yield [[(array, tuple(block), tuple(place)) for array in (mine, theirs)]]

        send_x, send_y = sums(list(small_groups(1, 1)), 1, (sent_two, got_result))
        keep_x, keep_y, kept_two = sums([*small_groups(0, 3), later], 3, (send_x, send_y))
        small = ChipSum(wires, keep_x, send_x, keep_y, send_y, 1)
        sum_two.third_sent(sent_two, kept_two)
        *sent, sent_two, sent_grad = sums(small.second() + sum_two.fourth(), 1, (), LIGHT, (sent_grad,))
        small.second_sent(*sent)
        sum_two.fourth_sent(sent_two)
        got_grad = wires.other_half(sent_grad)
        small.third_sent(*sums(small.third(), 1, sum_two.sent, MIDDLE))
        sent, sent_two = sums(small.fourth() + sum_two.fifth())
        small.fourth_sent(sent)
        sum_two.fifth_sent(sent_two)
        sent, sum_one.got, got_grad, got_result = sums(
            small.fifth(), 1, sum_two.sent, LIGHT, (sum_one.got, got_grad, got_result)
        )
        small.fifth_sent(sent)
        one, two = small.total()
        bias = one[2 * cut + 16 : 2 * cut + 18].astype(f32)
        bias_qk = lax.dynamic_slice_in_dim(bias[0], wires.core * qk_own, qk_own)
        bias_v = lax.dynamic_slice_in_dim(bias[1], lax.axis_index("fsdp") * (kv_width // shards), kv_width // shards)
        total = jnp.stack([one, two], axis=0).reshape(2, 2, cut + 16, LANES)[:, :, :cut]
        total = total.transpose(1, 0, 2, 3).reshape(blocks, depth, LANES)
    else:
        kept_grad, sent_grad = input_grad(half, tokens, gain_one, project, qkv_full, grad_middle, ())
        got_grad = wires.other_half(sent_grad)
        total = jnp.stack(ordered(wires.core, mine, theirs), axis=0)[:, :, :, jnp.array(LINE)]
        total = total.reshape(*total.shape[:4], 2, cut + 16, LANES)[:, :, :, :, :, :cut]
        total = total.reshape(2, 2, 2, 4, 2, blocks // 4, shards // groups, depth, LANES)
        total = total.transpose(3, 1, 0, 6, 4, 2, 5, 7, 8).reshape(shards, -1, LANES)
        total = lax.psum_scatter(total.astype(f32), "fsdp", scatter_dimension=0, tiled=True)[0]
        total = lax.psum(total.astype(bf16), "seq").reshape(blocks, depth, LANES)
        bias = lax.psum(bias_grad[0], ("seq", "fsdp"))
        place = lax.axis_index("fsdp")
        bias_qk = lax.dynamic_slice_in_dim(bias, place * qk_own, qk_own)
        bias_v = lax.dynamic_slice_in_dim(
            bias, width + kv_width + place * (kv_width // shards), kv_width // shards
        )
    result = jnp.concatenate([kept_result, got_result], axis=0)
    grad_input = jnp.concatenate([kept_grad, got_grad], axis=0)
    total = total.transpose(1, 0, 2).reshape(depth, -1).astype(f32)
    gain_one_grad = jnp.sum(total[:, :qkv_width] * w_qkv.astype(f32), axis=1) / first_gain.astype(f32)

    half_rows = 6 * full_depth
    if small_mesh:
        chunks, cuts = [], []
        for chip_sum, (first, _, second, _) in ((sum_one, grads_one), (sum_two, grads_two)):
            pair = chip_sum.sent[0], chip_sum.got
            chunks.append((*pair, *(wires.flip(piece, 1) for piece in pair)))
            cuts.append((first.shape[2] // 3, second.shape[2] // 3))
        gate_grad, up_grad, down_grad, gain_two_grad = unpack_call(at, chunks, cuts, w_gate, w_up, shards)
        gain_two_grad = jnp.sum(gain_two_grad, axis=1) / second_gain.astype(f32)
    else:
        many = shards // groups
        terms = []
        for keep_x, send_x, keep_y, send_y in (grads_one, grads_two):
            first = jnp.stack([keep_x, send_x], axis=0).reshape(2, 2, 4, -1, half_rows, LANES)
            second = jnp.stack([keep_y, send_y], axis=0).reshape(2, 2, 4, -1, half_rows, LANES)
            places = jnp.array(LINE)
            first = first.transpose(2, 0, 3, 1, 4, 5)[places].reshape(chips, -1, 2, half_rows, LANES)
            second = second.transpose(2, 1, 3, 0, 4, 5)[places].reshape(chips, -1, 2, half_rows, LANES)
            terms += [first, second]
        terms = jnp.concatenate(terms, axis=1).reshape(chips, steps, 2 * half_rows, LANES)
        parts = []
        for start, size in ((0, depth), (4 * full_depth, depth), (8 * full_depth, own)):
            part = terms[:, :, start : start + 4 * full_depth]
            part = part.reshape(chips, steps, -1, 2 * many, size, LANES)
            parts.append(part.transpose(0, 3, 1, 2, 4, 5).reshape(shards, steps, -1, LANES))
        terms = jnp.concatenate(parts, axis=2).astype(f32)
        terms = lax.dynamic_update_index_in_dim(jnp.zeros((2,) + terms.shape, f32), terms, wires.core, 0)
        terms = lax.psum_scatter(terms, "fsdp", scatter_dimension=1, tiled=True)[:, 0]
        terms = lax.psum(terms.astype(bf16), "seq")
        mlp_grads = terms.transpose(1, 0, 2, 3).reshape(2 * steps, -1, LANES)[:tiles]
        gate_grad, up_grad, down_grad = unpack_grads(mlp_grads, shards, depth)
        both = gate_grad.astype(f32) * w_gate.astype(f32) + up_grad.astype(f32) * w_up.astype(f32)
        gain_two_grad = jnp.sum(both, axis=1) / second_gain.astype(f32)
    return (
        result[None],
        grad_input[None],
        gain_one_grad,
        total[:, :qkv_width],
        bias_qk,
        bias_v,
        total[:, qkv_width:],
        gain_two_grad,
        gate_grad.astype(f32),
        up_grad.astype(f32),
        down_grad.astype(f32),
    )


def solution(mesh):
    rows, split, lone = P("fsdp", "seq", None), P("fsdp", None), P("fsdp")
    in_specs = (rows, P("fsdp", "seq"), lone, split, lone, split, lone, split, split, split, rows)
    out_specs = (rows, rows, lone, split, lone, lone, split, lone, split, split, split)
    return jax.shard_map(
        functools.partial(per_device, mesh.shape["fsdp"]),
        mesh=mesh,
        in_specs=in_specs,
        out_specs=out_specs,
        check_vma=False,
    )
```
